32 devices in a mesh: alpha: 16 (over z, y, x), beta: 2 (over core).
Axes of the slice: x: 2, y: 2, z: 4, core: 2. Of those that a mesh axis runs over, the one named last changes fastest.
Arguments:
- coeffs: bfloat16 [1024, 512], P('alpha', 'beta'), may hold values from -6 to 6
- integrals: bfloat16 [484, 484], replicated, may hold values from -0.0234375 to 0.0234375
- send_block: int32 [16, 128], P('alpha'), may hold values from 0 to 16, as said below
- alpha_slot: int32 [256, 132], P('alpha'), may hold values from 0 to 63, as said below
- alpha_pair: int32 [256, 132], P('alpha'), may hold values from 0 to 483, as said below
- alpha_parity: int32 [256, 132], P('alpha'), may hold values from 0 to 1
- beta_pair: int32 [32, 132], P('beta'), may hold values from 0 to 483, as said below
- beta_target: int32 [32, 132], P('beta'), may hold values from 0 to 31
- beta_parity: int32 [32, 132], P('beta'), may hold values from 0 to 1
Outputs:
- sigma: float32 [1024, 512], P('alpha', 'beta')
The draws below stay inside these ranges and needn't reach their ends.
Inputs may be any that keep to these rules, and one draw needn't show every extreme that they name: `send_block`: in each batch the filled slots from one sender to one receiver come first; at most 4 are filled, 4 is reached from every sender to some receiver in every batch, and some slots stay empty in every batch. `alpha_slot`: every entry names a slot that holds a block. `alpha_pair`: the pairs of one row are distinct. `beta_pair`: the pairs of one row are distinct.
All inputs are finite; a program needn't handle non-finite values.
Results may differ from the reference program's by a relative error of at most 0.0003.
Values may be sent and summed in bfloat16 or wider, within the bound.
No kernel may reach another device: no remote copies, remote signals or barrier semaphores. Data moves between devices by JAX's collectives and lax.ppermute only.
A program may use at most 64 MiB of HBM per device.

```python
import jax
import jax.numpy as jnp
from jax import lax

P_SIZE = 484
EXC_BLK = 132
EXCB = 132
SB = 4
BBLK = 16
BATCHES = 2
CAP = 4
BLK_DEV = 16
BLK_BATCH = 8
SLOTS = 64
ABLOCKS = 256
NA = 1024
NB = 512
NBLKB = 32
N_ALPHA = 16


def alpha_plan(key):
    base = jax.random.fold_in(key, 7)
    key_count, key_busy, key_block, key_sender, key_cell, key_quiet = jax.random.split(base, 6)
    counts = jax.random.randint(key_count, (BATCHES, N_ALPHA, N_ALPHA), 1, CAP + 1)
    busy = jax.random.randint(key_busy, (BATCHES,), 0, N_ALPHA)
    quiet = jax.random.randint(key_quiet, (BATCHES, N_ALPHA), 0, N_ALPHA)
    receivers = jnp.arange(N_ALPHA, dtype=jnp.int32)
    senders_all = jnp.arange(N_ALPHA, dtype=jnp.int32)
    silent = (senders_all[None, :, None] == quiet[:, None, :]) & (receivers[None, None, :] != busy[:, None, None])
    counts = jnp.where(silent, 0, counts)
    counts = jnp.where(receivers[None, None, :] == busy[:, None, None], CAP, counts)
    chosen = jax.random.randint(key_block, (BATCHES, N_ALPHA, N_ALPHA, CAP), 0, BLK_DEV)
    cells = jnp.arange(CAP, dtype=jnp.int32)
    filled = cells[None, None, None, :] < counts[..., None]
    sending = jnp.where(filled, chosen, BLK_DEV)
    send_table = sending.transpose(1, 0, 2, 3).reshape(N_ALPHA, BATCHES * N_ALPHA * CAP)
    batch_of = jnp.arange(BLK_DEV, dtype=jnp.int32) // (BLK_DEV // BATCHES)
    owners = jnp.arange(N_ALPHA, dtype=jnp.int32)
    quiet_here = quiet[batch_of[None, :, None], owners[:, None, None]]
    raw_sender = jax.random.randint(key_sender, (N_ALPHA, BLK_DEV, EXC_BLK), 0, N_ALPHA - 1)
    sender = raw_sender + (raw_sender >= quiet_here).astype(jnp.int32)
    raw_cell = jax.random.randint(key_cell, (N_ALPHA, BLK_DEV, EXC_BLK), 0, 1 << 20)
    count_here = counts[batch_of[None, :, None], sender, owners[:, None, None]]
    cell_pick = raw_cell % jnp.maximum(count_here, 1)
    slot_table = (sender * CAP + cell_pick).reshape(N_ALPHA * BLK_DEV, EXC_BLK)
    return (send_table.astype(jnp.int32), slot_table.astype(jnp.int32))


def distinct_pairs(key, row_count, pick_count):
    scores = jax.random.randint(key, (row_count, P_SIZE), 0, 1 << 20) * P_SIZE + jnp.arange(P_SIZE, dtype=jnp.int32)[None, :]
    return jnp.argsort(scores, axis=1)[:, :pick_count].astype(jnp.int32)


def draw_send_block(key, part):
    return alpha_plan(key)[0]


def draw_alpha_slot(key, part):
    return alpha_plan(key)[1]


def draw_alpha_pair(key, part):
    return distinct_pairs(jax.random.fold_in(key, 11), ABLOCKS, EXC_BLK)


def draw_beta_pair(key, part):
    return distinct_pairs(jax.random.fold_in(key, 13), NBLKB, EXCB)


def touch_ends(values, rng, least, top_value):
    longest = values.shape.index(max(values.shape))
    spots = []
    for shift in (0, 1):
        where = [jax.random.randint(jax.random.fold_in(rng, axis), (), 0, length) for axis, length in enumerate(values.shape)]
        where[longest] = (where[longest] + shift) % values.shape[longest]
        spots.append(tuple(where))
    return values.at[spots[0]].set(least).at[spots[1]].set(top_value)


def steps_of(own_key, extent, cuts, smallest, largest):
    def one(axis_at, blocks):
        draws = jax.random.uniform(jax.random.fold_in(jax.random.fold_in(own_key, 6), axis_at), (blocks,), jnp.float32, smallest / len(cuts), largest / len(cuts))
        return jnp.repeat(jnp.exp(draws), extent[axis_at] // blocks).reshape((-1,) + (1,) * (len(extent) - axis_at - 1))

    level = one(*cuts[0])
    for cut in cuts[1:]:
        level = level * one(*cut)
    return level


def noise(rng, shape, spread, limit, cuts=(), kind=jnp.bfloat16):
    array = jax.random.normal(rng, shape, jnp.float32) * spread
    if len(cuts) > 0:
        array = steps_of(rng, shape, cuts, -0.22, 0.18) * array
    return jnp.clip(array, min=-limit, max=limit).astype(kind)


def setup_inputs(seed: int = 0) -> dict:
    keys = jax.random.split(jax.random.key(seed), 10)
    return {
        "coeffs": noise(keys[0], (NA, NB), 1.0, 6.0, ((0, 16), (1, 2))),
        "integrals": noise(keys[1], (P_SIZE, P_SIZE), (P_SIZE * EXCB) ** -0.5, 0.0234375),
        "send_block": draw_send_block(jax.random.fold_in(keys[9], 71), 0),
        "alpha_slot": draw_alpha_slot(jax.random.fold_in(keys[9], 71), 0),
        "alpha_pair": draw_alpha_pair(jax.random.fold_in(keys[9], 71), 0),
        "alpha_parity": touch_ends(jax.random.randint(keys[5], (ABLOCKS, EXC_BLK), 0, 2), jax.random.fold_in(keys[5], 1), 0, 1).astype(jnp.int32),
        "beta_pair": draw_beta_pair(jax.random.fold_in(keys[9], 71), 0),
        "beta_target": touch_ends(jax.random.randint(keys[7], (NBLKB, EXCB), 0, NBLKB), jax.random.fold_in(keys[7], 1), 0, NBLKB - 1).astype(jnp.int32),
        "beta_parity": touch_ends(jax.random.randint(keys[8], (NBLKB, EXCB), 0, 2), jax.random.fold_in(keys[8], 1), 0, 1).astype(jnp.int32),
    }


def reference(coeffs, integrals, send_block, alpha_slot, alpha_pair, alpha_parity, beta_pair, beta_target, beta_parity):
    shaped = coeffs.reshape(N_ALPHA, BLK_DEV, SB, NB)
    empty_row = jnp.zeros((N_ALPHA, 1, SB, NB), coeffs.dtype)
    padded = jnp.concatenate([shaped, empty_row], axis=1)
    beta_factor = (1 - 2 * beta_parity).astype(jnp.float32)
    flat_target = beta_target.reshape(-1)

    def one_block(global_block):
        device = global_block // BLK_DEV
        local_block = global_block % BLK_DEV
        batch_index = local_block // BLK_BATCH
        slots = alpha_slot[global_block]
        sender = slots // CAP
        cell_index = slots % CAP
        column = batch_index * SLOTS + device * CAP + cell_index
        chosen = send_block[sender, column]
        rows_taken = padded[sender, chosen]
        factor = (1 - 2 * alpha_parity[global_block]).astype(coeffs.dtype)
        signed = rows_taken * factor[:, None, None]
        selected = integrals[:, alpha_pair[global_block]]
        contracted = jnp.dot(selected.astype(jnp.float32), signed.reshape(EXC_BLK, SB * NB).astype(jnp.float32), precision=lax.Precision.HIGHEST)
        arranged = contracted.reshape(P_SIZE, SB, NBLKB, BBLK).transpose(2, 0, 1, 3)
        picked = jnp.take_along_axis(arranged, beta_pair[:, :, None, None], axis=1)
        picked = picked * beta_factor[:, :, None, None]
        summed = jax.ops.segment_sum(picked.reshape(NBLKB * EXCB, SB, BBLK), flat_target, num_segments=NBLKB)
        return summed.transpose(1, 0, 2).reshape(SB, NB)

    result = lax.map(one_block, jnp.arange(ABLOCKS, dtype=jnp.int32))
    return result.reshape(NA, NB)
```

```python
import jax
import jax.numpy as jnp
from jax import lax
from jax.experimental import pallas as pl
from jax.experimental.pallas import tpu as pltpu
from jax.sharding import PartitionSpec as P

BATCHES = 2
CAP = 4
BF = jnp.bfloat16
F32 = jnp.float32
LANES = 128
SUB = 8


def iota(shape, axis):
    return lax.broadcasted_iota(jnp.int32, shape, axis)


def one(condition):
    return jnp.where(condition, 1.0, 0.0).astype(F32)


def dot(a, b):
    return jnp.dot(a, b, preferred_element_type=F32)


def dot_nt(a, b):
    return lax.dot_general(a, b, (((1,), (1,)), ((), ())), preferred_element_type=F32)


def split(x):
    high = x.astype(BF)
    return high, (x - high.astype(F32)).astype(BF)


def outgoing_kernel(strings, width, coeffs_ref, send_ref, out_ref):
    rows, columns = coeffs_ref.shape
    slots = send_ref.shape[1]
    wide = strings * columns
    group = strings * width
    k, n = iota((columns, wide), 0), iota((columns, wide), 1)
    spread = one((k // width == n // group) & (k % width == n % width)).astype(BF)
    spaced = dot(coeffs_ref[...], spread)
    keep = iota((rows, wide), 0) % strings == (iota((rows, wide), 1) // width) % strings
    spaced = jnp.where(keep, spaced, 0.0).astype(BF)
    r, lane = iota((slots, slots), 0), iota((slots, slots), 1)
    per = BATCHES * CAP
    column = (r % per) // CAP * (slots // BATCHES) + r // per * CAP + r % CAP
    chosen = jnp.sum(
        jnp.where(column == lane, send_ref[...].astype(F32), 0.0), axis=1, keepdims=True
    ).astype(jnp.int32)
    pick = one(iota((slots, rows), 1) // strings == chosen).astype(BF)
    out_ref[...] = dot(pick, spaced).astype(BF)


def tables_kernel(
    beta_blocks,
    integrals_ref,
    slot_ref,
    pair_ref,
    parity_ref,
    bpair_ref,
    btarget_ref,
    bparity_ref,
    pair_t_ref,
    bpair_t_ref,
    out_ref,
    t_ref,
    w_ref,
    hot_ref,
):
    orbitals = integrals_ref.shape[0]
    blocks, excitations = slot_ref.shape
    beta_local, beta_excitations = bpair_ref.shape
    pairs = blocks // BATCHES
    slots = hot_ref.shape[0] // pairs
    for v in range(beta_local):
        factor = (1 - 2 * bparity_ref[v : v + 1, :]).astype(F32)
        target = btarget_ref[v : v + 1, :]
        left = jnp.where(iota((beta_blocks, beta_excitations), 0) == target, factor, 0.0).astype(BF)
        right = one(
            iota((beta_excitations, orbitals), 1) == bpair_t_ref[:, v : v + 1]
        ).astype(BF)
        t_ref[v * beta_blocks : (v + 1) * beta_blocks, :] = dot(left, right).astype(BF)
    high, low = split(dot(t_ref[...], integrals_ref[...]))
    w_ref[0] = high
    w_ref[1] = low
    for t in range(pairs):
        total = None
        for h in range(BATCHES):
            g = h * pairs + t
            factor = (1 - 2 * parity_ref[g : g + 1, :]).astype(F32)
            slot = slot_ref[g : g + 1, :]
            row = slot // CAP * (BATCHES * CAP) + h * CAP + slot % CAP
            left = jnp.where(iota((slots, excitations), 0) == row, factor, 0.0).astype(BF)
            right = one(
                iota((excitations, orbitals), 1) == pair_t_ref[:, g : g + 1]
            ).astype(BF)
            part = dot(left, right)
            total = part if total is None else total + part
        hot_ref[t * slots : (t + 1) * slots, :] = total.astype(BF)
    for t in range(pairs):
        hot = hot_ref[t * slots : (t + 1) * slots, :]
        high, low = split(dot_nt(w_ref[0], hot) + dot_nt(w_ref[1], hot))
        for v in range(beta_local):
            rows = slice(t * beta_blocks, (t + 1) * beta_blocks)
            source = slice(v * beta_blocks, (v + 1) * beta_blocks)
            first = v * 2 * slots
            out_ref[rows, first : first + slots] = high[source]
            out_ref[rows, first + slots : first + 2 * slots] = low[source]


def sigma_kernel(strings, width, table_ref, received_ref, *refs):
    outs, (right_ref, sum_ref, place_ref) = refs[:-3], refs[-3:]
    slots, wide = received_ref.shape
    group = strings * width
    both = BATCHES * group
    beta_local = wide // group
    pairs = outs[0].shape[0] // strings // BATCHES
    blocks = table_ref.shape[0] // pairs
    r, lane = iota((slots, both), 0), iota((slots, both), 1)
    batch = r // CAP % BATCHES
    low = one((batch == 0) & (lane < group)).astype(BF)
    high = one((batch == 1) & (lane >= group)).astype(BF)
    for tile in range(wide // both):
        x = received_ref[:, tile * both : (tile + 1) * both]
        turned = jnp.concatenate([x[:, group:], x[:, :group]], axis=1)
        for v, (a, b) in ((2 * tile, (x, turned)), (2 * tile + 1, (turned, x))):
            value = a * low + b * high
            right_ref[2 * v * slots : (2 * v + 1) * slots, :] = value
            right_ref[(2 * v + 1) * slots : (2 * v + 2) * slots, :] = value
    product = dot(table_ref[...], right_ref[...])
    both_parts = jnp.concatenate(split(product), axis=1)
    per_tile = LANES // width
    columns = BATCHES * strings * LANES
    k, n = iota((2 * both, columns), 0), iota((2 * both, columns), 1)
    expand = one(((k % both) // width == n // LANES) & (k % width == n % width)).astype(BF)
    spread = dot(both_parts, expand)
    shape = (pairs * blocks, columns)
    keep = iota(shape, 0) % per_tile == (iota(shape, 1) // width) % per_tile
    spread = jnp.where(keep, spread, 0.0)
    tiles = blocks // per_tile
    summed = jnp.sum(spread.reshape(pairs * tiles, per_tile, columns), axis=1)
    for hs in range(BATCHES * strings):
        sum_ref[hs] = summed[:, hs * LANES : (hs + 1) * LANES]
    per_out = tiles // len(outs)
    for q in range(tiles):
        for h in range(BATCHES):
            for s in range(strings):
                place_ref[q, pl.ds(h * pairs * strings + s, pairs, stride=strings), :] = sum_ref[
                    h * strings + s, pl.ds(q, pairs, stride=tiles), :
                ]
        at = q % per_out * LANES
        outs[q // per_out][:, at : at + LANES] = place_ref[q]


def on_device(
    coeffs,
    integrals,
    send_block,
    alpha_slot,
    alpha_pair,
    alpha_parity,
    beta_pair,
    beta_target,
    beta_parity,
):
    local_rows, local_columns = coeffs.shape
    local_blocks = alpha_slot.shape[0]
    strings = local_rows // local_blocks
    pairs = local_blocks // BATCHES
    beta_local = beta_pair.shape[0]
    width = local_columns // beta_local
    cores = lax.axis_size("beta")
    senders = lax.axis_size("alpha")
    beta_blocks = cores * beta_local
    orbitals = integrals.shape[0]
    slots = send_block.shape[1]
    wide = strings * local_columns

    outgoing = pl.pallas_call(
        lambda *refs: outgoing_kernel(strings, width, *refs),
        out_shape=jax.ShapeDtypeStruct((slots, wide), BF),
        name="outgoing",
    )(coeffs, send_block)
    received = lax.all_to_all(
        outgoing.reshape(senders, slots // senders, wide), "alpha", split_axis=0, concat_axis=0, tiled=True
    ).reshape(slots, wide)

    target = jnp.remainder(beta_target - lax.axis_index("beta") * beta_local, beta_blocks)
    flops = 2 * beta_local * beta_blocks * orbitals * (orbitals + 2 * pairs * slots)
    table = pl.pallas_call(
        lambda *refs: tables_kernel(beta_blocks, *refs),
        out_shape=jax.ShapeDtypeStruct((pairs * beta_blocks, 2 * beta_local * slots), BF),
        scratch_shapes=[
            pltpu.VMEM((beta_local * beta_blocks, orbitals), BF),
            pltpu.VMEM((2, beta_local * beta_blocks, orbitals), BF),
            pltpu.VMEM((pairs * slots, orbitals), BF),
        ],
        compiler_params=pltpu.CompilerParams(vmem_limit_bytes=40 * 2**20),
        cost_estimate=pl.CostEstimate(flops=flops, bytes_accessed=8 * 2**20, transcendentals=0),
        name="tables",
    )(
        integrals,
        alpha_slot,
        alpha_pair,
        alpha_parity,
        beta_pair,
        target,
        beta_parity,
        alpha_pair.T,
        beta_pair.T,
    )
    part = jax.ShapeDtypeStruct((local_rows, local_columns), F32)
    both = BATCHES * strings * width
    tiles = beta_blocks * width // LANES
    parts = pl.pallas_call(
        lambda *refs: sigma_kernel(strings, width, *refs),
        out_shape=[part] * cores,
        scratch_shapes=[
            pltpu.VMEM((2 * beta_local * slots, both), BF),
            pltpu.VMEM((BATCHES * strings, pairs * tiles, LANES), F32),
            pltpu.VMEM((tiles, local_rows, LANES), F32),
        ],
        compiler_params=pltpu.CompilerParams(vmem_limit_bytes=40 * 2**20),
        name="sigma",
    )(table, received)
    result = parts[0]
    for step in range(1, cores):
        route = [(core, (core + step) % cores) for core in range(cores)]
        result = result + lax.ppermute(parts[step], "beta", route)
    return result


def solution(mesh):
    in_specs = (
        P("alpha", "beta"),
        P(),
        P("alpha", None),
        P("alpha", None),
        P("alpha", None),
        P("alpha", None),
        P("beta", None),
        P("beta", None),
        P("beta", None),
    )
    out_specs = P("alpha", "beta")
    return jax.shard_map(
        on_device, mesh=mesh, in_specs=in_specs, out_specs=out_specs, check_vma=False
    )
```

```python
import jax
import jax.numpy as jnp
from jax import lax
from jax.experimental import pallas as pl
from jax.experimental.pallas import tpu as pltpu
from jax.sharding import PartitionSpec as P

BATCHES = 2
CAP = 4
BF = jnp.bfloat16
F32 = jnp.float32
LANES = 128
WIDE = 256


def row_of(length):
    return lax.broadcasted_iota(jnp.int32, (1, length), 1)


def column_of(length):
    return lax.broadcasted_iota(jnp.int32, (length, 1), 0)


def over(x, n):
    if n & (n - 1) == 0:
        return lax.shift_right_logical(x, jnp.int32(n.bit_length() - 1))
    return lax.div(x, jnp.int32(n))


def modulo(x, n):
    if n & (n - 1) == 0:
        return x & (n - 1)
    return lax.rem(x, jnp.int32(n))


def one(condition):
    return jnp.where(condition, 1.0, 0.0).astype(BF)


def dot(a, b):
    return jnp.dot(a, b, preferred_element_type=F32)


def dot_nt(a, b):
    return lax.dot_general(a, b, (((1,), (1,)), ((), ())), preferred_element_type=F32)


def split(x):
    high = x.astype(BF)
    return high, (x - high.astype(F32)).astype(BF)


def outgoing_kernel(strings, width, coeffs_ref, send_ref, out_ref):
    rows, columns = coeffs_ref.shape
    slots = send_ref.shape[1]
    wide = strings * columns
    group = strings * width
    per = BATCHES * CAP
    n = row_of(wide)
    spread = one(column_of(columns) == over(n, group) * width + modulo(n, width))
    spaced = dot(coeffs_ref[...], spread)
    keep = modulo(column_of(rows), strings) == modulo(over(n, width), strings)
    spaced = jnp.where(keep, spaced, 0.0).astype(BF)
    r = column_of(slots)
    wanted = over(modulo(r, per), CAP) * (slots // BATCHES) + over(r, per) * CAP + modulo(r, CAP)
    chosen = jnp.sum(
        jnp.where(wanted == row_of(slots), send_ref[...].astype(F32), 0.0), axis=1, keepdims=True
    ).astype(jnp.int32)
    pick = one(over(row_of(rows), strings) == chosen)
    out_ref[...] = dot(pick, spaced).astype(BF)


def tables_kernel(beta_blocks, *refs):
    sources, target_ref, copies = refs[:7], refs[7], refs[8:15]
    out_ref, t_ref, w_ref, hot_ref, in_sems, out_sems = refs[15:]
    moves = [
        pltpu.make_async_copy(source, copy, in_sems.at[i])
        for i, (source, copy) in enumerate(zip(sources, copies))
    ]
    for move in moves:
        move.start()
    bpair_ref, btarget_ref, bparity_ref, slot_ref, pair_ref, parity_ref, integrals_ref = copies
    orbitals = integrals_ref.shape[0]
    blocks, excitations = slot_ref.shape
    beta_local, beta_excitations = bpair_ref.shape
    pairs = blocks // BATCHES
    slots = hot_ref.shape[0] // pairs
    for move in moves[:3]:
        move.wait()
    bpair = bpair_ref[...].astype(F32).T.astype(jnp.int32)
    bfactor = (1 - 2 * bparity_ref[...]).astype(F32)
    btarget = btarget_ref[...] - lax.axis_index("beta") * beta_local
    btarget = jnp.where(btarget < 0, btarget + beta_blocks, btarget)
    for v in range(beta_local):
        left = jnp.where(column_of(beta_blocks) == btarget[v : v + 1], bfactor[v : v + 1], 0.0)
        right = one(row_of(orbitals) == bpair[:, v : v + 1])
        t_ref[v * beta_blocks : (v + 1) * beta_blocks, :] = dot(left.astype(BF), right).astype(BF)
    for move in moves[3:]:
        move.wait()
    high, low = split(dot(t_ref[...], integrals_ref[...]))
    w_ref[0] = high
    w_ref[1] = low
    pair = pair_ref[...].astype(F32).T.astype(jnp.int32)
    factor = (1 - 2 * parity_ref[...]).astype(F32)
    slot = slot_ref[...]
    place = over(slot, CAP) * (BATCHES * CAP) + modulo(slot, CAP)
    for t in range(pairs):
        total = None
        for h in range(BATCHES):
            g = h * pairs + t
            row = place[g : g + 1] + h * CAP
            left = jnp.where(column_of(slots) == row, factor[g : g + 1], 0.0).astype(BF)
            part = dot(left, one(row_of(orbitals) == pair[:, g : g + 1]))
            total = part if total is None else total + part
        hot_ref[t * slots : (t + 1) * slots, :] = total.astype(BF)
    step = max(1, WIDE // slots)
    results = []
    for start in range(0, pairs, step):
        hot = hot_ref[start * slots : (start + step) * slots, :]
        high, low = split(dot_nt(w_ref[0], hot) + dot_nt(w_ref[1], hot))
        for i in range(step):
            rows = slice((start + i) * beta_blocks, (start + i + 1) * beta_blocks)
            lanes = slice(i * slots, (i + 1) * slots)
            for v in range(beta_local):
                source = slice(v * beta_blocks, (v + 1) * beta_blocks)
                first = v * 2 * slots
                out_ref[rows, first : first + slots] = high[source, lanes]
                out_ref[rows, first + slots : first + 2 * slots] = low[source, lanes]
        done = pl.ds(start * beta_blocks, step * beta_blocks)
        result = pltpu.make_async_copy(out_ref.at[done], target_ref.at[done], out_sems.at[start])
        result.start()
        results.append(result)
    for result in results:
        result.wait()


def sigma_kernel(strings, width, table_ref, received_ref, *refs):
    outs, (right_ref, sum_ref, place_ref) = refs[:-3], refs[-3:]
    slots, wide = received_ref.shape
    group = strings * width
    both = BATCHES * group
    pairs = outs[0].shape[0] // strings // BATCHES
    blocks = table_ref.shape[0] // pairs
    batch = modulo(over(column_of(slots), CAP), BATCHES)
    low = one((batch == 0) & (row_of(both) < group))
    high = one((batch == 1) & (row_of(both) >= group))
    for tile in range(wide // both):
        x = received_ref[:, tile * both : (tile + 1) * both]
        turned = jnp.concatenate([x[:, group:], x[:, :group]], axis=1)
        for v, (a, b) in ((2 * tile, (x, turned)), (2 * tile + 1, (turned, x))):
            value = a * low + b * high
            right_ref[2 * v * slots : (2 * v + 1) * slots, :] = value
            right_ref[(2 * v + 1) * slots : (2 * v + 2) * slots, :] = value
    product = dot(table_ref[...], right_ref[...])
    both_parts = jnp.concatenate(split(product), axis=1)
    per_tile = LANES // width
    columns = BATCHES * strings * LANES
    n = row_of(columns)
    expand = one(
        modulo(column_of(2 * both), both) == over(n, LANES) * width + modulo(n, width)
    )
    spread = dot(both_parts, expand)
    keep = modulo(column_of(pairs * blocks), per_tile) == modulo(over(n, width), per_tile)
    spread = jnp.where(keep, spread, 0.0)
    tiles = blocks // per_tile
    summed = jnp.sum(spread.reshape(pairs * tiles, per_tile, columns), axis=1)
    for hs in range(BATCHES * strings):
        sum_ref[hs] = summed[:, hs * LANES : (hs + 1) * LANES]
    per_out = tiles // len(outs)
    for q in range(tiles):
        for h in range(BATCHES):
            for s in range(strings):
                place_ref[q, pl.ds(h * pairs * strings + s, pairs, stride=strings), :] = sum_ref[
                    h * strings + s, pl.ds(q, pairs, stride=tiles), :
                ]
        at = q % per_out * LANES
        outs[q // per_out][:, at : at + LANES] = place_ref[q]


def on_device(
    coeffs,
    integrals,
    send_block,
    alpha_slot,
    alpha_pair,
    alpha_parity,
    beta_pair,
    beta_target,
    beta_parity,
):
    local_rows, local_columns = coeffs.shape
    local_blocks = alpha_slot.shape[0]
    strings = local_rows // local_blocks
    pairs = local_blocks // BATCHES
    beta_local = beta_pair.shape[0]
    width = local_columns // beta_local
    cores = lax.axis_size("beta")
    senders = lax.axis_size("alpha")
    beta_blocks = cores * beta_local
    orbitals = integrals.shape[0]
    slots = send_block.shape[1]
    wide = strings * local_columns

    outgoing = pl.pallas_call(
        lambda *refs: outgoing_kernel(strings, width, *refs),
        out_shape=jax.ShapeDtypeStruct((slots, wide), BF),
        compiler_params=pltpu.CompilerParams(vmem_limit_bytes=60 * 2**20),
        name="outgoing",
    )(coeffs, send_block)
    received = lax.all_to_all(
        outgoing.reshape(senders, slots // senders, wide), "alpha", split_axis=0, concat_axis=0, tiled=True
    ).reshape(slots, wide)
    tables = (
        beta_pair,
        beta_target,
        beta_parity,
        alpha_slot,
        alpha_pair,
        alpha_parity,
        integrals,
    )
    flops = 2 * beta_local * beta_blocks * orbitals * (orbitals + 2 * pairs * slots)
    shape = (pairs * beta_blocks, 2 * beta_local * slots)
    table = pl.pallas_call(
        lambda *refs: tables_kernel(beta_blocks, *refs),
        in_specs=[pl.BlockSpec(memory_space=pltpu.HBM)] * len(tables),
        out_specs=pl.BlockSpec(memory_space=pltpu.HBM),
        out_shape=jax.ShapeDtypeStruct(shape, BF),
        scratch_shapes=[pltpu.VMEM(x.shape, x.dtype) for x in tables]
        + [
            pltpu.VMEM(shape, BF),
            pltpu.VMEM((beta_local * beta_blocks, orbitals), BF),
            pltpu.VMEM((2, beta_local * beta_blocks, orbitals), BF),
            pltpu.VMEM((pairs * slots, orbitals), BF),
            pltpu.SemaphoreType.DMA((len(tables),)),
            pltpu.SemaphoreType.DMA((pairs,)),
        ],
        compiler_params=pltpu.CompilerParams(vmem_limit_bytes=60 * 2**20),
        cost_estimate=pl.CostEstimate(flops=flops, bytes_accessed=8 * 2**20, transcendentals=0),
        name="tables",
    )(*tables)
    part = jax.ShapeDtypeStruct((local_rows, local_columns), F32)
    both = BATCHES * strings * width
    tiles = beta_blocks * width // LANES
    parts = pl.pallas_call(
        lambda *refs: sigma_kernel(strings, width, *refs),
        out_shape=[part] * cores,
        scratch_shapes=[
            pltpu.VMEM((2 * beta_local * slots, both), BF),
            pltpu.VMEM((BATCHES * strings, pairs * tiles, LANES), F32),
            pltpu.VMEM((tiles, local_rows, LANES), F32),
        ],
        compiler_params=pltpu.CompilerParams(vmem_limit_bytes=40 * 2**20),
        name="sigma",
    )(table, received)
    result = parts[0]
    for step in range(1, cores):
        route = [(core, (core + step) % cores) for core in range(cores)]
        result = result + lax.ppermute(parts[step], "beta", route)
    return result


def solution(mesh):
    in_specs = (
        P("alpha", "beta"),
        P(),
        P("alpha", None),
        P("alpha", None),
        P("alpha", None),
        P("alpha", None),
        P("beta", None),
        P("beta", None),
        P("beta", None),
    )
    out_specs = P("alpha", "beta")
    return jax.shard_map(
        on_device, mesh=mesh, in_specs=in_specs, out_specs=out_specs, check_vma=False
    )
```

```python
import jax
import jax.numpy as jnp
from jax import lax
from jax.experimental import pallas as pl
from jax.experimental.pallas import tpu as pltpu
from jax.sharding import PartitionSpec as P

BATCHES = 2
CAP = 4
BF = jnp.bfloat16
F32 = jnp.float32
LANES = 128
WIDE = 256


def row_of(length):
    return lax.broadcasted_iota(jnp.int32, (1, length), 1)


def column_of(length):
    return lax.broadcasted_iota(jnp.int32, (length, 1), 0)


def over(x, n):
    if n & (n - 1) == 0:
        return lax.shift_right_logical(x, jnp.int32(n.bit_length() - 1))
    return lax.div(x, jnp.int32(n))


def modulo(x, n):
    if n & (n - 1) == 0:
        return x & (n - 1)
    return lax.rem(x, jnp.int32(n))


def one(condition):
    return jnp.where(condition, 1.0, 0.0).astype(BF)


def dot(a, b):
    return jnp.dot(a, b, preferred_element_type=F32)


def dot_nt(a, b):
    return lax.dot_general(a, b, (((1,), (1,)), ((), ())), preferred_element_type=F32)


def split(x):
    high = x.astype(BF)
    return high, (x - high.astype(F32)).astype(BF)


def forward_kernel(strings, width, inner, *refs):
    outer = (len(refs) - inner) // 2
    coeff_refs, list_refs, out_refs = refs[:outer], refs[outer : 2 * outer], refs[2 * outer :]
    rows, columns = coeff_refs[0].shape
    slots = list_refs[0].shape[1]
    wide = strings * columns
    group = strings * width
    per = BATCHES * CAP
    n = row_of(wide)
    spread = one(column_of(columns) == over(n, group) * width + modulo(n, width))
    gathered = jnp.concatenate([ref[...] for ref in coeff_refs], axis=0)
    keep = modulo(column_of(outer * rows), strings) == modulo(over(n, width), strings)
    spaced = jnp.where(keep, dot(gathered, spread), 0.0).astype(BF)
    r = column_of(inner * per)
    receiver = over(r, per) ^ lax.axis_index("alpha")
    wanted = over(modulo(r, per), CAP) * (slots // BATCHES) + receiver * CAP + modulo(r, CAP)
    wanted = wanted == row_of(slots)
    picks = []
    for k in range(outer):
        listed = jnp.where(wanted, list_refs[k][...].astype(F32), 0.0)
        chosen = jnp.sum(listed, axis=1, keepdims=True).astype(jnp.int32)
        chosen = jnp.where(chosen < rows // strings, chosen + k * (rows // strings), -1)
        picks.append(jnp.where(over(row_of(outer * rows), strings) == chosen, 1.0, 0.0))
    for j in range(inner):
        pick = jnp.concatenate([part[j * per : (j + 1) * per] for part in picks], axis=0)
        out_refs[j][...] = dot(pick.astype(BF), spaced).astype(BF)


def tables_kernel(
    blocks, beta_blocks, outer, inner, index_ref, integrals_ref, _, out_ref, t_ref, w_ref, hot_ref
):
    orbitals = integrals_ref.shape[0]
    slot_ref, pair_ref, parity_ref = (
        index_ref.at[i * blocks : (i + 1) * blocks] for i in range(3)
    )
    beta_local = index_ref.shape[0] // 3 - blocks
    bpair_ref, btarget_ref, bparity_ref = (
        index_ref.at[3 * blocks + i * beta_local : 3 * blocks + (i + 1) * beta_local]
        for i in range(3)
    )
    excitations = beta_excitations = index_ref.shape[1]
    pairs = blocks // BATCHES
    slots = hot_ref.shape[0] // pairs
    bpair = bpair_ref[...].astype(F32).T.astype(jnp.int32)
    bfactor = (1 - 2 * bparity_ref[...]).astype(F32)
    btarget = btarget_ref[...] - lax.axis_index("beta") * beta_local
    btarget = jnp.where(btarget < 0, btarget + beta_blocks, btarget)
    for v in range(beta_local):
        left = jnp.where(column_of(beta_blocks) == btarget[v : v + 1], bfactor[v : v + 1], 0.0)
        right = one(row_of(orbitals) == bpair[:, v : v + 1])
        t_ref[v * beta_blocks : (v + 1) * beta_blocks, :] = dot(left.astype(BF), right).astype(BF)
    high, low = split(dot(t_ref[...], integrals_ref[...]))
    w_ref[0] = high
    w_ref[1] = low
    pair = pair_ref[...].astype(F32).T.astype(jnp.int32)
    factor = (1 - 2 * parity_ref[...]).astype(F32)
    slot = slot_ref[...]
    partner = over(slot, CAP) ^ lax.axis_index("alpha")
    place = modulo(partner, inner) * outer + over(partner, inner)
    place = place * (BATCHES * CAP) + modulo(slot, CAP)
    for t in range(pairs):
        total = None
        for h in range(BATCHES):
            g = h * pairs + t
            row = place[g : g + 1] + h * CAP
            left = jnp.where(column_of(slots) == row, factor[g : g + 1], 0.0).astype(BF)
            part = dot(left, one(row_of(orbitals) == pair[:, g : g + 1]))
            total = part if total is None else total + part
        hot_ref[t * slots : (t + 1) * slots, :] = total.astype(BF)
    step = max(1, WIDE // slots)
    for start in range(0, pairs, step):
        hot = hot_ref[start * slots : (start + step) * slots, :]
        high, low = split(dot_nt(w_ref[0], hot) + dot_nt(w_ref[1], hot))
        for i in range(step):
            rows = slice((start + i) * beta_blocks, (start + i + 1) * beta_blocks)
            lanes = slice(i * slots, (i + 1) * slots)
            for v in range(beta_local):
                source = slice(v * beta_blocks, (v + 1) * beta_blocks)
                first = v * 2 * slots
                out_ref[rows, first : first + slots] = high[source, lanes]
                out_ref[rows, first + slots : first + 2 * slots] = low[source, lanes]


def sigma_kernel(strings, width, inner, table_ref, *refs):
    received_refs, outs, (right_ref, sum_ref, place_ref) = refs[:inner], refs[inner:-3], refs[-3:]
    received = jnp.concatenate([ref[...] for ref in received_refs], axis=0)
    slots, wide = received.shape
    group = strings * width
    both = BATCHES * group
    pairs = outs[0].shape[0] // strings // BATCHES
    blocks = table_ref.shape[0] // pairs
    batch = modulo(over(column_of(slots), CAP), BATCHES)
    low = one((batch == 0) & (row_of(both) < group))
    high = one((batch == 1) & (row_of(both) >= group))
    for tile in range(wide // both):
        x = received[:, tile * both : (tile + 1) * both]
        turned = jnp.concatenate([x[:, group:], x[:, :group]], axis=1)
        for v, (a, b) in ((2 * tile, (x, turned)), (2 * tile + 1, (turned, x))):
            value = a * low + b * high
            right_ref[2 * v * slots : (2 * v + 1) * slots, :] = value
            right_ref[(2 * v + 1) * slots : (2 * v + 2) * slots, :] = value
    product = dot(table_ref[...], right_ref[...])
    both_parts = jnp.concatenate(split(product), axis=1)
    per_tile = LANES // width
    columns = BATCHES * strings * LANES
    n = row_of(columns)
    expand = one(
        modulo(column_of(2 * both), both) == over(n, LANES) * width + modulo(n, width)
    )
    spread = dot(both_parts, expand)
    keep = modulo(column_of(pairs * blocks), per_tile) == modulo(over(n, width), per_tile)
    spread = jnp.where(keep, spread, 0.0)
    tiles = blocks // per_tile
    summed = jnp.sum(spread.reshape(pairs * tiles, per_tile, columns), axis=1)
    for hs in range(BATCHES * strings):
        sum_ref[hs] = summed[:, hs * LANES : (hs + 1) * LANES]
    per_out = tiles // len(outs)
    for q in range(tiles):
        for h in range(BATCHES):
            for s in range(strings):
                place_ref[q, pl.ds(h * pairs * strings + s, pairs, stride=strings), :] = sum_ref[
                    h * strings + s, pl.ds(q, pairs, stride=tiles), :
                ]
        at = q % per_out * LANES
        outs[q // per_out][:, at : at + LANES] = place_ref[q]


def on_device(
    coeffs,
    integrals,
    send_block,
    alpha_slot,
    alpha_pair,
    alpha_parity,
    beta_pair,
    beta_target,
    beta_parity,
):
    local_rows, local_columns = coeffs.shape
    local_blocks = alpha_slot.shape[0]
    strings = local_rows // local_blocks
    pairs = local_blocks // BATCHES
    beta_local = beta_pair.shape[0]
    width = local_columns // beta_local
    cores = lax.axis_size("beta")
    senders = lax.axis_size("alpha")
    beta_blocks = cores * beta_local
    orbitals = integrals.shape[0]
    slots = send_block.shape[1]
    wide = strings * local_columns

    outer = 1 << (senders.bit_length() - 1) // 2
    inner = senders // outer
    per = slots // senders

    def exchange(x, k):
        return lax.ppermute(x, "alpha", [(d, d ^ k) for d in range(senders)]) if k else x

    def near(x):
        return jnp.where(lax.axis_index("alpha") >= 0, x, jnp.zeros_like(x))

    gathered = [exchange(coeffs, k * inner) if k else near(coeffs) for k in range(outer)]
    lists = [exchange(send_block, k * inner) if k else near(send_block) for k in range(outer)]
    outgoing = pl.pallas_call(
        lambda *refs: forward_kernel(strings, width, inner, *refs),
        out_shape=[jax.ShapeDtypeStruct((outer * per, wide), BF)] * inner,
        compiler_params=pltpu.CompilerParams(vmem_limit_bytes=40 * 2**20),
        name="forward",
    )(*gathered, *lists)
    received = [exchange(x, j) for j, x in enumerate(outgoing)]
    index = jnp.concatenate(
        [alpha_slot, alpha_pair, alpha_parity, beta_pair, beta_target, beta_parity], axis=0
    )
    flops = 2 * beta_local * beta_blocks * orbitals * (orbitals + 2 * pairs * slots)
    table = pl.pallas_call(
        lambda *refs: tables_kernel(local_blocks, beta_blocks, outer, inner, *refs),
        in_specs=[pl.BlockSpec(memory_space=pltpu.VMEM)] * 2
        + [pl.BlockSpec(memory_space=pl.ANY)],
        out_shape=jax.ShapeDtypeStruct((pairs * beta_blocks, 2 * beta_local * slots), BF),
        scratch_shapes=[
            pltpu.VMEM((beta_local * beta_blocks, orbitals), BF),
            pltpu.VMEM((2, beta_local * beta_blocks, orbitals), BF),
            pltpu.VMEM((pairs * slots, orbitals), BF),
        ],
        compiler_params=pltpu.CompilerParams(vmem_limit_bytes=40 * 2**20),
        cost_estimate=pl.CostEstimate(flops=flops, bytes_accessed=8 * 2**20, transcendentals=0),
        name="tables",
    )(index, near(integrals), outgoing[0])
    part = jax.ShapeDtypeStruct((local_rows, local_columns), F32)
    both = BATCHES * strings * width
    tiles = beta_blocks * width // LANES
    parts = pl.pallas_call(
        lambda *refs: sigma_kernel(strings, width, inner, *refs),
        out_shape=[part] * cores,
        scratch_shapes=[
            pltpu.VMEM((2 * beta_local * slots, both), BF),
            pltpu.VMEM((BATCHES * strings, pairs * tiles, LANES), F32),
            pltpu.VMEM((tiles, local_rows, LANES), F32),
        ],
        compiler_params=pltpu.CompilerParams(vmem_limit_bytes=40 * 2**20),
        name="sigma",
    )(table, *received)
    result = parts[0]
    for step in range(1, cores):
        route = [(core, (core + step) % cores) for core in range(cores)]
        result = result + lax.ppermute(parts[step], "beta", route)
    return result


def solution(mesh):
    in_specs = (
        P("alpha", "beta"),
        P(),
        P("alpha", None),
        P("alpha", None),
        P("alpha", None),
        P("alpha", None),
        P("beta", None),
        P("beta", None),
        P("beta", None),
    )
    out_specs = P("alpha", "beta")
    return jax.shard_map(
        on_device, mesh=mesh, in_specs=in_specs, out_specs=out_specs, check_vma=False
    )
```

```python
import jax
import jax.numpy as jnp
from jax import lax
from jax.experimental import pallas as pl
from jax.experimental.pallas import tpu as pltpu
from jax.sharding import PartitionSpec as P

BATCHES = 2
CAP = 4
BF = jnp.bfloat16
F32 = jnp.float32
LANES = 128
WIDE = 256


def row_of(length):
    return lax.broadcasted_iota(jnp.int32, (1, length), 1)


def column_of(length):
    return lax.broadcasted_iota(jnp.int32, (length, 1), 0)


def over(x, n):
    if n & (n - 1) == 0:
        return lax.shift_right_logical(x, jnp.int32(n.bit_length() - 1))
    return lax.div(x, jnp.int32(n))


def modulo(x, n):
    if n & (n - 1) == 0:
        return x & (n - 1)
    return lax.rem(x, jnp.int32(n))


def one(condition):
    return jnp.where(condition, 1.0, 0.0).astype(BF)


def dot(a, b):
    return jnp.dot(a, b, preferred_element_type=F32)


def dot_nt(a, b):
    return lax.dot_general(a, b, (((1,), (1,)), ((), ())), preferred_element_type=F32)


def split(x):
    high = x.astype(BF)
    return high, (x - high.astype(F32)).astype(BF)


def collect_kernel(*refs):
    count = (len(refs) - 5) // 2
    coeffs_ref, send_ref = refs[:2]
    others, chunks_ref, copies = refs[2 : 2 + count], refs[2 + count], refs[3 + count : -2]
    list_ref, sems = refs[-2:]
    chunks, total, columns = chunks_ref.shape
    rows, slots = coeffs_ref.shape[0], send_ref.shape[1]
    pairs = [(send_ref, list_ref)]
    pairs += [(coeffs_ref, chunks_ref.at[k, pl.ds(0, rows)]) for k in range(chunks)]
    pairs += list(zip(others, copies))
    moves = [
        pltpu.make_async_copy(source, target, sems.at[i]) for i, (source, target) in enumerate(pairs)
    ]
    for move in moves:
        move.start()
    moves[0].wait()
    values = list_ref[...].astype(F32)
    value = jnp.zeros((total - rows, columns), F32)
    for i, first in enumerate(range(0, slots, columns)):
        row = values[:, first : first + columns]
        if row.shape[1] < columns:
            row = jnp.concatenate([row, jnp.zeros((1, columns - row.shape[1]), F32)], axis=1)
        value = value + jnp.where(column_of(total - rows) == i, row, 0.0)
    for k in range(chunks):
        chunks_ref[k, rows:total, :] = value.astype(BF)
    for move in moves[1:]:
        move.wait()


def forward_kernel(strings, width, inner, rows, slots, gathered_ref, out_ref):
    outer, _, columns = gathered_ref.shape
    wide = strings * columns
    group = strings * width
    per = BATCHES * CAP
    blocks = rows // strings
    n = row_of(wide)
    spread = one(column_of(columns) == over(n, group) * width + modulo(n, width))
    gathered = jnp.concatenate([gathered_ref[k, :rows, :] for k in range(outer)], axis=0)
    keep = modulo(column_of(outer * rows), strings) == modulo(over(n, width), strings)
    spaced = jnp.where(keep, dot(gathered, spread), 0.0).astype(BF)
    r = column_of(inner * per)
    receiver = over(lax.axis_index("alpha"), inner) * inner + over(r, per)
    wanted = over(modulo(r, per), CAP) * (slots // BATCHES) + receiver * CAP + modulo(r, CAP)
    wanted = wanted == row_of(slots)
    picks = []
    for k in range(outer):
        tail = gathered_ref[k, rows:, :].astype(F32)
        listed = [tail[i : i + 1] for i in range((slots + columns - 1) // columns)]
        listed = (listed[0] if len(listed) == 1 else jnp.concatenate(listed, axis=1))[:, :slots]
        chosen = jnp.sum(jnp.where(wanted, listed, 0.0), axis=1, keepdims=True).astype(jnp.int32)
        chosen = jnp.where(chosen < blocks, chosen + k * blocks, -1)
        picks.append(jnp.where(over(row_of(outer * rows), strings) == chosen, 1.0, 0.0))
    for j in range(inner):
        pick = jnp.concatenate([part[j * per : (j + 1) * per] for part in picks], axis=0)
        out_ref[j] = dot(pick.astype(BF), spaced).astype(BF)


def tables_kernel(
    beta_blocks,
    outer,
    inner,
    slot_ref,
    pair_ref,
    parity_ref,
    bpair_ref,
    btarget_ref,
    bparity_ref,
    integrals_ref,
    _,
    out_ref,
    t_ref,
    w_ref,
    hot_ref,
):
    orbitals = integrals_ref.shape[0]
    blocks, excitations = slot_ref.shape
    beta_local, beta_excitations = bpair_ref.shape
    pairs = blocks // BATCHES
    slots = hot_ref.shape[0] // pairs
    bpair = bpair_ref[...].astype(F32).T.astype(jnp.int32)
    bfactor = (1 - 2 * bparity_ref[...]).astype(F32)
    btarget = btarget_ref[...] - lax.axis_index("beta") * beta_local
    btarget = jnp.where(btarget < 0, btarget + beta_blocks, btarget)
    for v in range(beta_local):
        left = jnp.where(column_of(beta_blocks) == btarget[v : v + 1], bfactor[v : v + 1], 0.0)
        right = one(row_of(orbitals) == bpair[:, v : v + 1])
        t_ref[v * beta_blocks : (v + 1) * beta_blocks, :] = dot(left.astype(BF), right).astype(BF)
    high, low = split(dot(t_ref[...], integrals_ref[...]))
    w_ref[0] = high
    w_ref[1] = low
    pair = pair_ref[...].astype(F32).T.astype(jnp.int32)
    factor = (1 - 2 * parity_ref[...]).astype(F32)
    slot = slot_ref[...]
    sender = over(slot, CAP)
    place = modulo(sender, inner) * outer + over(sender, inner)
    place = place * (BATCHES * CAP) + modulo(slot, CAP)
    for t in range(pairs):
        total = None
        for h in range(BATCHES):
            g = h * pairs + t
            row = place[g : g + 1] + h * CAP
            left = jnp.where(column_of(slots) == row, factor[g : g + 1], 0.0).astype(BF)
            part = dot(left, one(row_of(orbitals) == pair[:, g : g + 1]))
            total = part if total is None else total + part
        hot_ref[t * slots : (t + 1) * slots, :] = total.astype(BF)
    step = max(1, WIDE // slots)
    for start in range(0, pairs, step):
        hot = hot_ref[start * slots : (start + step) * slots, :]
        high, low = split(dot_nt(w_ref[0], hot) + dot_nt(w_ref[1], hot))
        for i in range(step):
            rows = slice((start + i) * beta_blocks, (start + i + 1) * beta_blocks)
            lanes = slice(i * slots, (i + 1) * slots)
            for v in range(beta_local):
                source = slice(v * beta_blocks, (v + 1) * beta_blocks)
                first = v * 2 * slots
                out_ref[rows, first : first + slots] = high[source, lanes]
                out_ref[rows, first + slots : first + 2 * slots] = low[source, lanes]


def sigma_kernel(strings, width, table_ref, received_ref, *refs):
    outs, (right_ref, sum_ref, place_ref) = refs[:-3], refs[-3:]
    slots, wide = received_ref.shape
    group = strings * width
    both = BATCHES * group
    pairs = outs[0].shape[0] // strings // BATCHES
    blocks = table_ref.shape[0] // pairs
    batch = modulo(over(column_of(slots), CAP), BATCHES)
    low = one((batch == 0) & (row_of(both) < group))
    high = one((batch == 1) & (row_of(both) >= group))
    for tile in range(wide // both):
        x = received_ref[:, tile * both : (tile + 1) * both]
        turned = jnp.concatenate([x[:, group:], x[:, :group]], axis=1)
        for v, (a, b) in ((2 * tile, (x, turned)), (2 * tile + 1, (turned, x))):
            value = a * low + b * high
            right_ref[2 * v * slots : (2 * v + 1) * slots, :] = value
            right_ref[(2 * v + 1) * slots : (2 * v + 2) * slots, :] = value
    product = dot(table_ref[...], right_ref[...])
    both_parts = jnp.concatenate(split(product), axis=1)
    per_tile = LANES // width
    columns = BATCHES * strings * LANES
    n = row_of(columns)
    expand = one(
        modulo(column_of(2 * both), both) == over(n, LANES) * width + modulo(n, width)
    )
    spread = dot(both_parts, expand)
    keep = modulo(column_of(pairs * blocks), per_tile) == modulo(over(n, width), per_tile)
    spread = jnp.where(keep, spread, 0.0)
    tiles = blocks // per_tile
    summed = jnp.sum(spread.reshape(pairs * tiles, per_tile, columns), axis=1)
    for hs in range(BATCHES * strings):
        sum_ref[hs] = summed[:, hs * LANES : (hs + 1) * LANES]
    per_out = tiles // len(outs)
    for q in range(tiles):
        for h in range(BATCHES):
            for s in range(strings):
                place_ref[q, pl.ds(h * pairs * strings + s, pairs, stride=strings), :] = sum_ref[
                    h * strings + s, pl.ds(q, pairs, stride=tiles), :
                ]
        at = q % per_out * LANES
        outs[q // per_out][:, at : at + LANES] = place_ref[q]


def on_device(
    coeffs,
    integrals,
    send_block,
    alpha_slot,
    alpha_pair,
    alpha_parity,
    beta_pair,
    beta_target,
    beta_parity,
):
    local_rows, local_columns = coeffs.shape
    local_blocks = alpha_slot.shape[0]
    strings = local_rows // local_blocks
    pairs = local_blocks // BATCHES
    beta_local = beta_pair.shape[0]
    width = local_columns // beta_local
    cores = lax.axis_size("beta")
    senders = lax.axis_size("alpha")
    beta_blocks = cores * beta_local
    orbitals = integrals.shape[0]
    slots = send_block.shape[1]
    wide = strings * local_columns

    outer = 1 << (senders.bit_length() - 1) // 2
    inner = senders // outer
    per = slots // senders

    extra = -(-slots // local_columns // 16) * 16
    others = (
        alpha_slot,
        alpha_pair,
        alpha_parity,
        beta_pair,
        beta_target,
        beta_parity,
        integrals,
    )
    chunks = (outer, local_rows + extra, local_columns)
    chunks, *tables = pl.pallas_call(
        collect_kernel,
        in_specs=[pl.BlockSpec(memory_space=pltpu.HBM)] * (2 + len(others)),
        out_shape=[jax.ShapeDtypeStruct(chunks, BF)]
        + [jax.ShapeDtypeStruct(x.shape, x.dtype) for x in others],
        scratch_shapes=[
            pltpu.VMEM(send_block.shape, jnp.int32),
            pltpu.SemaphoreType.DMA((1 + outer + len(others),)),
        ],
        compiler_params=pltpu.CompilerParams(vmem_limit_bytes=40 * 2**20),
        name="collect",
    )(*(pltpu.with_memory_space_constraint(x, pltpu.HBM) for x in (coeffs, send_block, *others)))
    along = [[k * inner + i for k in range(outer)] for i in range(inner)]
    across = [[k * inner + i for i in range(inner)] for k in range(outer)]
    gathered = lax.all_to_all(chunks, "alpha", 0, 0, axis_index_groups=along, tiled=True)
    outgoing = pl.pallas_call(
        lambda *refs: forward_kernel(strings, width, inner, local_rows, slots, *refs),
        out_shape=jax.ShapeDtypeStruct((inner, outer * per, wide), BF),
        compiler_params=pltpu.CompilerParams(vmem_limit_bytes=40 * 2**20),
        name="forward",
    )(gathered)
    received = lax.all_to_all(outgoing, "alpha", 0, 0, axis_index_groups=across, tiled=True)
    received = received.reshape(slots, wide)
    flops = 2 * beta_local * beta_blocks * orbitals * (orbitals + 2 * pairs * slots)
    table = pl.pallas_call(
        lambda *refs: tables_kernel(beta_blocks, outer, inner, *refs),
        in_specs=[pl.BlockSpec(memory_space=pltpu.VMEM)] * len(tables)
        + [pl.BlockSpec(memory_space=pl.ANY)],
        out_shape=jax.ShapeDtypeStruct((pairs * beta_blocks, 2 * beta_local * slots), BF),
        scratch_shapes=[
            pltpu.VMEM((beta_local * beta_blocks, orbitals), BF),
            pltpu.VMEM((2, beta_local * beta_blocks, orbitals), BF),
            pltpu.VMEM((pairs * slots, orbitals), BF),
        ],
        compiler_params=pltpu.CompilerParams(vmem_limit_bytes=40 * 2**20),
        cost_estimate=pl.CostEstimate(flops=flops, bytes_accessed=8 * 2**20, transcendentals=0),
        name="tables",
    )(*tables, outgoing)
    part = jax.ShapeDtypeStruct((local_rows, local_columns), F32)
    both = BATCHES * strings * width
    tiles = beta_blocks * width // LANES
    parts = pl.pallas_call(
        lambda *refs: sigma_kernel(strings, width, *refs),
        out_shape=[part] * cores,
        scratch_shapes=[
            pltpu.VMEM((2 * beta_local * slots, both), BF),
            pltpu.VMEM((BATCHES * strings, pairs * tiles, LANES), F32),
            pltpu.VMEM((tiles, local_rows, LANES), F32),
        ],
        compiler_params=pltpu.CompilerParams(vmem_limit_bytes=40 * 2**20),
        name="sigma",
    )(table, received)
    result = parts[0]
    for step in range(1, cores):
        route = [(core, (core + step) % cores) for core in range(cores)]
        result = result + lax.ppermute(parts[step], "beta", route)
    return result


def solution(mesh):
    in_specs = (
        P("alpha", "beta"),
        P(),
        P("alpha", None),
        P("alpha", None),
        P("alpha", None),
        P("alpha", None),
        P("beta", None),
        P("beta", None),
        P("beta", None),
    )
    out_specs = P("alpha", "beta")
    return jax.shard_map(
        on_device, mesh=mesh, in_specs=in_specs, out_specs=out_specs, check_vma=False
    )
```

```python
import jax
import jax.numpy as jnp
from jax import lax
from jax.experimental import pallas as pl
from jax.experimental.pallas import tpu as pltpu
from jax.sharding import PartitionSpec as P

BATCHES = 2
CAP = 4
BF = jnp.bfloat16
F32 = jnp.float32
LANES = 128
WIDE = 256


def row_of(length):
    return lax.broadcasted_iota(jnp.int32, (1, length), 1)


def column_of(length):
    return lax.broadcasted_iota(jnp.int32, (length, 1), 0)


def over(x, n):
    if n & (n - 1) == 0:
        return lax.shift_right_logical(x, jnp.int32(n.bit_length() - 1))
    return lax.div(x, jnp.int32(n))


def modulo(x, n):
    if n & (n - 1) == 0:
        return x & (n - 1)
    return lax.rem(x, jnp.int32(n))


def one(condition):
    return jnp.where(condition, 1.0, 0.0).astype(BF)


def dot(a, b):
    return jnp.dot(a, b, preferred_element_type=F32)


def dot_nt(a, b):
    return lax.dot_general(a, b, (((1,), (1,)), ((), ())), preferred_element_type=F32)


def split(x):
    high = x.astype(BF)
    return high, (x - high.astype(F32)).astype(BF)


def outgoing_kernel(strings, width, *refs):
    count = (len(refs) - 6) // 2
    sources, out_ref, copies = refs[: 2 + count], refs[2 + count], refs[3 + count : -3]
    coeffs_ref, send_ref, sems = refs[-3:]
    moves = [
        pltpu.make_async_copy(source, target, sems.at[i])
        for i, (source, target) in enumerate(zip(sources, (coeffs_ref, send_ref, *copies)))
    ]
    for move in moves:
        move.start()
    rows, columns = coeffs_ref.shape
    slots = send_ref.shape[1]
    wide = strings * columns
    group = strings * width
    per = BATCHES * CAP
    n = row_of(wide)
    spread = one(column_of(columns) == over(n, group) * width + modulo(n, width))
    keep = modulo(column_of(rows), strings) == modulo(over(n, width), strings)
    r = column_of(slots)
    wanted = over(modulo(r, per), CAP) * (slots // BATCHES) + over(r, per) * CAP + modulo(r, CAP)
    moves[0].wait()
    moves[1].wait()
    spaced = jnp.where(keep, dot(coeffs_ref[...], spread), 0.0).astype(BF)
    chosen = jnp.sum(
        jnp.where(wanted == row_of(slots), send_ref[...].astype(F32), 0.0), axis=1, keepdims=True
    ).astype(jnp.int32)
    pick = one(over(row_of(rows), strings) == chosen)
    out_ref[...] = dot(pick, spaced).astype(BF)
    for move in moves[2:]:
        move.wait()


def tables_kernel(
    beta_blocks,
    slot_ref,
    pair_ref,
    parity_ref,
    bpair_ref,
    btarget_ref,
    bparity_ref,
    integrals_ref,
    out_ref,
    t_ref,
    w_ref,
    hot_ref,
):
    orbitals = integrals_ref.shape[0]
    blocks, excitations = slot_ref.shape
    beta_local, beta_excitations = bpair_ref.shape
    pairs = blocks // BATCHES
    slots = hot_ref.shape[0] // pairs
    bpair = bpair_ref[...].astype(F32).T.astype(jnp.int32)
    bfactor = (1 - 2 * bparity_ref[...]).astype(F32)
    btarget = btarget_ref[...] - lax.axis_index("beta") * beta_local
    btarget = jnp.where(btarget < 0, btarget + beta_blocks, btarget)
    for v in range(beta_local):
        left = jnp.where(column_of(beta_blocks) == btarget[v : v + 1], bfactor[v : v + 1], 0.0)
        right = one(row_of(orbitals) == bpair[:, v : v + 1])
        t_ref[v * beta_blocks : (v + 1) * beta_blocks, :] = dot(left.astype(BF), right).astype(BF)
    high, low = split(dot(t_ref[...], integrals_ref[...]))
    w_ref[0] = high
    w_ref[1] = low
    pair = pair_ref[...].astype(F32).T.astype(jnp.int32)
    factor = (1 - 2 * parity_ref[...]).astype(F32)
    slot = slot_ref[...]
    place = over(slot, CAP) * (BATCHES * CAP) + modulo(slot, CAP)
    for t in range(pairs):
        total = None
        for h in range(BATCHES):
            g = h * pairs + t
            row = place[g : g + 1] + h * CAP
            left = jnp.where(column_of(slots) == row, factor[g : g + 1], 0.0).astype(BF)
            part = dot(left, one(row_of(orbitals) == pair[:, g : g + 1]))
            total = part if total is None else total + part
        hot_ref[t * slots : (t + 1) * slots, :] = total.astype(BF)
    step = max(1, WIDE // slots)
    for start in range(0, pairs, step):
        hot = hot_ref[start * slots : (start + step) * slots, :]
        high, low = split(dot_nt(w_ref[0], hot) + dot_nt(w_ref[1], hot))
        for i in range(step):
            rows = slice((start + i) * beta_blocks, (start + i + 1) * beta_blocks)
            lanes = slice(i * slots, (i + 1) * slots)
            for v in range(beta_local):
                source = slice(v * beta_blocks, (v + 1) * beta_blocks)
                first = v * 2 * slots
                out_ref[rows, first : first + slots] = high[source, lanes]
                out_ref[rows, first + slots : first + 2 * slots] = low[source, lanes]


def sigma_kernel(strings, width, table_ref, received_ref, *refs):
    outs, (right_ref, sum_ref, place_ref) = refs[:-3], refs[-3:]
    slots, wide = received_ref.shape
    group = strings * width
    both = BATCHES * group
    pairs = outs[0].shape[0] // strings // BATCHES
    blocks = table_ref.shape[0] // pairs
    batch = modulo(over(column_of(slots), CAP), BATCHES)
    low = one((batch == 0) & (row_of(both) < group))
    high = one((batch == 1) & (row_of(both) >= group))
    for tile in range(wide // both):
        x = received_ref[:, tile * both : (tile + 1) * both]
        turned = jnp.concatenate([x[:, group:], x[:, :group]], axis=1)
        for v, (a, b) in ((2 * tile, (x, turned)), (2 * tile + 1, (turned, x))):
            value = a * low + b * high
            right_ref[2 * v * slots : (2 * v + 1) * slots, :] = value
            right_ref[(2 * v + 1) * slots : (2 * v + 2) * slots, :] = value
    product = dot(table_ref[...], right_ref[...])
    both_parts = jnp.concatenate(split(product), axis=1)
    per_tile = LANES // width
    columns = BATCHES * strings * LANES
    n = row_of(columns)
    expand = one(
        modulo(column_of(2 * both), both) == over(n, LANES) * width + modulo(n, width)
    )
    spread = dot(both_parts, expand)
    keep = modulo(column_of(pairs * blocks), per_tile) == modulo(over(n, width), per_tile)
    spread = jnp.where(keep, spread, 0.0)
    tiles = blocks // per_tile
    summed = jnp.sum(spread.reshape(pairs * tiles, per_tile, columns), axis=1)
    for hs in range(BATCHES * strings):
        sum_ref[hs] = summed[:, hs * LANES : (hs + 1) * LANES]
    per_out = tiles // len(outs)
    for q in range(tiles):
        for h in range(BATCHES):
            for s in range(strings):
                place_ref[q, pl.ds(h * pairs * strings + s, pairs, stride=strings), :] = sum_ref[
                    h * strings + s, pl.ds(q, pairs, stride=tiles), :
                ]
        at = q % per_out * LANES
        outs[q // per_out][:, at : at + LANES] = place_ref[q]


def on_device(
    coeffs,
    integrals,
    send_block,
    alpha_slot,
    alpha_pair,
    alpha_parity,
    beta_pair,
    beta_target,
    beta_parity,
):
    local_rows, local_columns = coeffs.shape
    local_blocks = alpha_slot.shape[0]
    strings = local_rows // local_blocks
    pairs = local_blocks // BATCHES
    beta_local = beta_pair.shape[0]
    width = local_columns // beta_local
    cores = lax.axis_size("beta")
    senders = lax.axis_size("alpha")
    beta_blocks = cores * beta_local
    orbitals = integrals.shape[0]
    slots = send_block.shape[1]
    wide = strings * local_columns

    others = (
        alpha_slot,
        alpha_pair,
        alpha_parity,
        beta_pair,
        beta_target,
        beta_parity,
        integrals,
    )
    outgoing, *tables = pl.pallas_call(
        lambda *refs: outgoing_kernel(strings, width, *refs),
        in_specs=[pl.BlockSpec(memory_space=pltpu.HBM)] * (2 + len(others)),
        out_shape=[jax.ShapeDtypeStruct((slots, wide), BF)]
        + [jax.ShapeDtypeStruct(x.shape, x.dtype) for x in others],
        scratch_shapes=[
            pltpu.VMEM(coeffs.shape, BF),
            pltpu.VMEM(send_block.shape, jnp.int32),
            pltpu.SemaphoreType.DMA((2 + len(others),)),
        ],
        compiler_params=pltpu.CompilerParams(vmem_limit_bytes=40 * 2**20),
        name="outgoing",
    )(*(pltpu.with_memory_space_constraint(x, pltpu.HBM) for x in (coeffs, send_block, *others)))
    received = lax.all_to_all(
        outgoing.reshape(senders, slots // senders, wide), "alpha", split_axis=0, concat_axis=0, tiled=True
    ).reshape(slots, wide)
    flops = 2 * beta_local * beta_blocks * orbitals * (orbitals + 2 * pairs * slots)
    table = pl.pallas_call(
        lambda *refs: tables_kernel(beta_blocks, *refs),
        out_shape=jax.ShapeDtypeStruct((pairs * beta_blocks, 2 * beta_local * slots), BF),
        scratch_shapes=[
            pltpu.VMEM((beta_local * beta_blocks, orbitals), BF),
            pltpu.VMEM((2, beta_local * beta_blocks, orbitals), BF),
            pltpu.VMEM((pairs * slots, orbitals), BF),
        ],
        compiler_params=pltpu.CompilerParams(vmem_limit_bytes=40 * 2**20),
        cost_estimate=pl.CostEstimate(flops=flops, bytes_accessed=8 * 2**20, transcendentals=0),
        name="tables",
    )(*tables)
    part = jax.ShapeDtypeStruct((local_rows, local_columns), F32)
    both = BATCHES * strings * width
    tiles = beta_blocks * width // LANES
    parts = pl.pallas_call(
        lambda *refs: sigma_kernel(strings, width, *refs),
        out_shape=[part] * cores,
        scratch_shapes=[
            pltpu.VMEM((2 * beta_local * slots, both), BF),
            pltpu.VMEM((BATCHES * strings, pairs * tiles, LANES), F32),
            pltpu.VMEM((tiles, local_rows, LANES), F32),
        ],
        compiler_params=pltpu.CompilerParams(vmem_limit_bytes=40 * 2**20),
        name="sigma",
    )(table, received)
    result = parts[0]
    for step in range(1, cores):
        route = [(core, (core + step) % cores) for core in range(cores)]
        result = result + lax.ppermute(parts[step], "beta", route)
    return result


def solution(mesh):
    in_specs = (
        P("alpha", "beta"),
        P(),
        P("alpha", None),
        P("alpha", None),
        P("alpha", None),
        P("alpha", None),
        P("beta", None),
        P("beta", None),
        P("beta", None),
    )
    out_specs = P("alpha", "beta")
    return jax.shard_map(
        on_device, mesh=mesh, in_specs=in_specs, out_specs=out_specs, check_vma=False
    )
```

```python
import jax
import jax.numpy as jnp
from jax import lax
from jax.experimental import pallas as pl
from jax.experimental.pallas import tpu as pltpu
from jax.sharding import PartitionSpec as P

BATCHES = 2
CAP = 4
BF = jnp.bfloat16
F32 = jnp.float32
LANES = 128
WIDE = 256


def row_of(length):
    return lax.broadcasted_iota(jnp.int32, (1, length), 1)


def column_of(length):
    return lax.broadcasted_iota(jnp.int32, (length, 1), 0)


def over(x, n):
    if n & (n - 1) == 0:
        return lax.shift_right_logical(x, jnp.int32(n.bit_length() - 1))
    return lax.div(x, jnp.int32(n))


def modulo(x, n):
    if n & (n - 1) == 0:
        return x & (n - 1)
    return lax.rem(x, jnp.int32(n))


def one(condition):
    return jnp.where(condition, 1.0, 0.0).astype(BF)


def dot(a, b):
    return jnp.dot(a, b, preferred_element_type=F32)


def dot_nt(a, b):
    return lax.dot_general(a, b, (((1,), (1,)), ((), ())), preferred_element_type=F32)


def split(x):
    high = x.astype(BF)
    return high, (x - high.astype(F32)).astype(BF)


def outgoing_kernel(strings, width, outer, inner, *refs):
    count = (len(refs) - 6) // 2
    sources, out_ref, copies = refs[: 2 + count], refs[2 + count], refs[3 + count : -3]
    coeffs_ref, send_ref, sems = refs[-3:]
    moves = [
        pltpu.make_async_copy(source, target, sems.at[i])
        for i, (source, target) in enumerate(zip(sources, (coeffs_ref, send_ref, *copies)))
    ]
    for move in moves:
        move.start()
    rows, columns = coeffs_ref.shape
    slots = send_ref.shape[1]
    wide = strings * columns
    group = strings * width
    per = BATCHES * CAP
    n = row_of(wide)
    spread = one(column_of(columns) == over(n, group) * width + modulo(n, width))
    keep = modulo(column_of(rows), strings) == modulo(over(n, width), strings)
    r = column_of(slots)
    receiver = modulo(over(r, per), outer) * inner + over(over(r, per), outer)
    wanted = over(modulo(r, per), CAP) * (slots // BATCHES) + receiver * CAP + modulo(r, CAP)
    moves[0].wait()
    moves[1].wait()
    spaced = jnp.where(keep, dot(coeffs_ref[...], spread), 0.0).astype(BF)
    chosen = jnp.sum(
        jnp.where(wanted == row_of(slots), send_ref[...].astype(F32), 0.0), axis=1, keepdims=True
    ).astype(jnp.int32)
    pick = one(over(row_of(rows), strings) == chosen)
    out_ref[...] = dot(pick, spaced).astype(BF)
    for move in moves[2:]:
        move.wait()


def tables_kernel(
    beta_blocks,
    outer,
    inner,
    slot_ref,
    pair_ref,
    parity_ref,
    bpair_ref,
    btarget_ref,
    bparity_ref,
    integrals_ref,
    out_ref,
    t_ref,
    w_ref,
    hot_ref,
):
    orbitals = integrals_ref.shape[0]
    blocks, excitations = slot_ref.shape
    beta_local, beta_excitations = bpair_ref.shape
    pairs = blocks // BATCHES
    slots = hot_ref.shape[0] // pairs
    bpair = bpair_ref[...].astype(F32).T.astype(jnp.int32)
    bfactor = (1 - 2 * bparity_ref[...]).astype(F32)
    btarget = btarget_ref[...] - lax.axis_index("beta") * beta_local
    btarget = jnp.where(btarget < 0, btarget + beta_blocks, btarget)
    for v in range(beta_local):
        left = jnp.where(column_of(beta_blocks) == btarget[v : v + 1], bfactor[v : v + 1], 0.0)
        right = one(row_of(orbitals) == bpair[:, v : v + 1])
        t_ref[v * beta_blocks : (v + 1) * beta_blocks, :] = dot(left.astype(BF), right).astype(BF)
    high, low = split(dot(t_ref[...], integrals_ref[...]))
    w_ref[0] = high
    w_ref[1] = low
    pair = pair_ref[...].astype(F32).T.astype(jnp.int32)
    factor = (1 - 2 * parity_ref[...]).astype(F32)
    slot = slot_ref[...]
    sender = over(slot, CAP)
    place = modulo(sender, inner) * outer + over(sender, inner)
    place = place * (BATCHES * CAP) + modulo(slot, CAP)
    for t in range(pairs):
        total = None
        for h in range(BATCHES):
            g = h * pairs + t
            row = place[g : g + 1] + h * CAP
            left = jnp.where(column_of(slots) == row, factor[g : g + 1], 0.0).astype(BF)
            part = dot(left, one(row_of(orbitals) == pair[:, g : g + 1]))
            total = part if total is None else total + part
        hot_ref[t * slots : (t + 1) * slots, :] = total.astype(BF)
    step = max(1, WIDE // slots)
    for start in range(0, pairs, step):
        hot = hot_ref[start * slots : (start + step) * slots, :]
        high, low = split(dot_nt(w_ref[0], hot) + dot_nt(w_ref[1], hot))
        for i in range(step):
            rows = slice((start + i) * beta_blocks, (start + i + 1) * beta_blocks)
            lanes = slice(i * slots, (i + 1) * slots)
            for v in range(beta_local):
                source = slice(v * beta_blocks, (v + 1) * beta_blocks)
                first = v * 2 * slots
                out_ref[rows, first : first + slots] = high[source, lanes]
                out_ref[rows, first + slots : first + 2 * slots] = low[source, lanes]


def sigma_kernel(strings, width, table_ref, received_ref, *refs):
    outs, (right_ref, sum_ref, place_ref) = refs[:-3], refs[-3:]
    slots, wide = received_ref.shape
    group = strings * width
    both = BATCHES * group
    pairs = outs[0].shape[0] // strings // BATCHES
    blocks = table_ref.shape[0] // pairs
    batch = modulo(over(column_of(slots), CAP), BATCHES)
    low = one((batch == 0) & (row_of(both) < group))
    high = one((batch == 1) & (row_of(both) >= group))
    for tile in range(wide // both):
        x = received_ref[:, tile * both : (tile + 1) * both]
        turned = jnp.concatenate([x[:, group:], x[:, :group]], axis=1)
        for v, (a, b) in ((2 * tile, (x, turned)), (2 * tile + 1, (turned, x))):
            value = a * low + b * high
            right_ref[2 * v * slots : (2 * v + 1) * slots, :] = value
            right_ref[(2 * v + 1) * slots : (2 * v + 2) * slots, :] = value
    product = dot(table_ref[...], right_ref[...])
    both_parts = jnp.concatenate(split(product), axis=1)
    per_tile = LANES // width
    columns = BATCHES * strings * LANES
    n = row_of(columns)
    expand = one(
        modulo(column_of(2 * both), both) == over(n, LANES) * width + modulo(n, width)
    )
    spread = dot(both_parts, expand)
    keep = modulo(column_of(pairs * blocks), per_tile) == modulo(over(n, width), per_tile)
    spread = jnp.where(keep, spread, 0.0)
    tiles = blocks // per_tile
    summed = jnp.sum(spread.reshape(pairs * tiles, per_tile, columns), axis=1)
    for hs in range(BATCHES * strings):
        sum_ref[hs] = summed[:, hs * LANES : (hs + 1) * LANES]
    per_out = tiles // len(outs)
    for q in range(tiles):
        for h in range(BATCHES):
            for s in range(strings):
                place_ref[q, pl.ds(h * pairs * strings + s, pairs, stride=strings), :] = sum_ref[
                    h * strings + s, pl.ds(q, pairs, stride=tiles), :
                ]
        at = q % per_out * LANES
        outs[q // per_out][:, at : at + LANES] = place_ref[q]


def on_device(
    coeffs,
    integrals,
    send_block,
    alpha_slot,
    alpha_pair,
    alpha_parity,
    beta_pair,
    beta_target,
    beta_parity,
):
    local_rows, local_columns = coeffs.shape
    local_blocks = alpha_slot.shape[0]
    strings = local_rows // local_blocks
    pairs = local_blocks // BATCHES
    beta_local = beta_pair.shape[0]
    width = local_columns // beta_local
    cores = lax.axis_size("beta")
    senders = lax.axis_size("alpha")
    beta_blocks = cores * beta_local
    orbitals = integrals.shape[0]
    slots = send_block.shape[1]
    wide = strings * local_columns

    outer = 1 << (senders.bit_length() - 1) // 2
    inner = senders // outer
    order = [k * inner + i for i in range(inner) for k in range(outer)]
    others = (
        alpha_slot,
        alpha_pair,
        alpha_parity,
        beta_pair,
        beta_target,
        beta_parity,
        integrals,
    )
    outgoing, *tables = pl.pallas_call(
        lambda *refs: outgoing_kernel(strings, width, outer, inner, *refs),
        in_specs=[pl.BlockSpec(memory_space=pltpu.HBM)] * (2 + len(others)),
        out_shape=[jax.ShapeDtypeStruct((slots, wide), BF)]
        + [jax.ShapeDtypeStruct(x.shape, x.dtype) for x in others],
        scratch_shapes=[
            pltpu.VMEM(coeffs.shape, BF),
            pltpu.VMEM(send_block.shape, jnp.int32),
            pltpu.SemaphoreType.DMA((2 + len(others),)),
        ],
        compiler_params=pltpu.CompilerParams(vmem_limit_bytes=40 * 2**20),
        name="outgoing",
    )(*(pltpu.with_memory_space_constraint(x, pltpu.HBM) for x in (coeffs, send_block, *others)))
    received = lax.all_to_all(
        outgoing.reshape(senders, slots // senders, wide),
        "alpha",
        split_axis=0,
        concat_axis=0,
        axis_index_groups=[order],
        tiled=True,
    ).reshape(slots, wide)
    flops = 2 * beta_local * beta_blocks * orbitals * (orbitals + 2 * pairs * slots)
    table = pl.pallas_call(
        lambda *refs: tables_kernel(beta_blocks, outer, inner, *refs),
        out_shape=jax.ShapeDtypeStruct((pairs * beta_blocks, 2 * beta_local * slots), BF),
        scratch_shapes=[
            pltpu.VMEM((beta_local * beta_blocks, orbitals), BF),
            pltpu.VMEM((2, beta_local * beta_blocks, orbitals), BF),
            pltpu.VMEM((pairs * slots, orbitals), BF),
        ],
        compiler_params=pltpu.CompilerParams(vmem_limit_bytes=40 * 2**20),
        cost_estimate=pl.CostEstimate(flops=flops, bytes_accessed=8 * 2**20, transcendentals=0),
        name="tables",
    )(*tables)
    part = jax.ShapeDtypeStruct((local_rows, local_columns), F32)
    both = BATCHES * strings * width
    tiles = beta_blocks * width // LANES
    parts = pl.pallas_call(
        lambda *refs: sigma_kernel(strings, width, *refs),
        out_shape=[part] * cores,
        scratch_shapes=[
            pltpu.VMEM((2 * beta_local * slots, both), BF),
            pltpu.VMEM((BATCHES * strings, pairs * tiles, LANES), F32),
            pltpu.VMEM((tiles, local_rows, LANES), F32),
        ],
        compiler_params=pltpu.CompilerParams(vmem_limit_bytes=40 * 2**20),
        name="sigma",
    )(table, received)
    result = parts[0]
    for step in range(1, cores):
        route = [(core, (core + step) % cores) for core in range(cores)]
        result = result + lax.ppermute(parts[step], "beta", route)
    return result


def solution(mesh):
    in_specs = (
        P("alpha", "beta"),
        P(),
        P("alpha", None),
        P("alpha", None),
        P("alpha", None),
        P("alpha", None),
        P("beta", None),
        P("beta", None),
        P("beta", None),
    )
    out_specs = P("alpha", "beta")
    return jax.shard_map(
        on_device, mesh=mesh, in_specs=in_specs, out_specs=out_specs, check_vma=False
    )
```

```python
import jax
import jax.numpy as jnp
from jax import lax
from jax.experimental import pallas as pl
from jax.experimental.pallas import tpu as pltpu
from jax.sharding import PartitionSpec as P

BATCHES = 2
CAP = 4
BF = jnp.bfloat16
F32 = jnp.float32
LANES = 128
WIDE = 256


def row_of(length):
    return lax.broadcasted_iota(jnp.int32, (1, length), 1)


def column_of(length):
    return lax.broadcasted_iota(jnp.int32, (length, 1), 0)


def over(x, n):
    if n & (n - 1) == 0:
        return lax.shift_right_logical(x, jnp.int32(n.bit_length() - 1))
    return lax.div(x, jnp.int32(n))


def modulo(x, n):
    if n & (n - 1) == 0:
        return x & (n - 1)
    return lax.rem(x, jnp.int32(n))


def one(condition):
    return jnp.where(condition, 1.0, 0.0).astype(BF)


def dot(a, b):
    return jnp.dot(a, b, preferred_element_type=F32)


def dot_nt(a, b):
    return lax.dot_general(a, b, (((1,), (1,)), ((), ())), preferred_element_type=F32)


def split(x):
    high = x.astype(BF)
    return high, (x - high.astype(F32)).astype(BF)


def pack_kernel(coeffs_ref, send_ref, out_ref, list_ref, sems):
    rows, slots = coeffs_ref.shape[0], send_ref.shape[1]
    total, columns = out_ref.shape
    moves = [
        pltpu.make_async_copy(send_ref, list_ref, sems.at[0]),
        pltpu.make_async_copy(coeffs_ref, out_ref.at[pl.ds(0, rows)], sems.at[1]),
    ]
    for move in moves:
        move.start()
    moves[0].wait()
    values = list_ref[...].astype(F32)
    value = jnp.zeros((total - rows, columns), F32)
    for i, first in enumerate(range(0, slots, columns)):
        row = values[:, first : first + columns]
        if row.shape[1] < columns:
            row = jnp.concatenate([row, jnp.zeros((1, columns - row.shape[1]), F32)], axis=1)
        value = value + jnp.where(column_of(total - rows) == i, row, 0.0)
    out_ref[rows:total, :] = value.astype(BF)
    moves[1].wait()


def fetch_kernel(*refs):
    count = (len(refs) - 2) // 2
    moves = [
        pltpu.make_async_copy(refs[i], refs[count + 1 + i], refs[-1].at[i]) for i in range(count)
    ]
    for move in moves:
        move.start()
    for move in moves:
        move.wait()


def forward_kernel(strings, width, rows, slots, outer, *refs):
    gathered_refs, out_refs = refs[:outer], refs[outer:]
    inner = len(out_refs)
    columns = gathered_refs[0].shape[1]
    wide = strings * columns
    group = strings * width
    per = BATCHES * CAP
    blocks = rows // strings
    n = row_of(wide)
    spread = one(column_of(columns) == over(n, group) * width + modulo(n, width))
    gathered = jnp.concatenate([ref[:rows, :] for ref in gathered_refs], axis=0)
    keep = modulo(column_of(outer * rows), strings) == modulo(over(n, width), strings)
    spaced = jnp.where(keep, dot(gathered, spread), 0.0).astype(BF)
    r = column_of(inner * per)
    receiver = over(r, per) ^ lax.axis_index("alpha")
    wanted = over(modulo(r, per), CAP) * (slots // BATCHES) + receiver * CAP + modulo(r, CAP)
    wanted = wanted == row_of(slots)
    picks = []
    for k in range(outer):
        tail = gathered_refs[k][rows:, :].astype(F32)
        listed = [tail[i : i + 1] for i in range((slots + columns - 1) // columns)]
        listed = (listed[0] if len(listed) == 1 else jnp.concatenate(listed, axis=1))[:, :slots]
        chosen = jnp.sum(jnp.where(wanted, listed, 0.0), axis=1, keepdims=True).astype(jnp.int32)
        chosen = jnp.where(chosen < blocks, chosen + k * blocks, -1)
        picks.append(jnp.where(over(row_of(outer * rows), strings) == chosen, 1.0, 0.0))
    for j in range(inner):
        pick = jnp.concatenate([part[j * per : (j + 1) * per] for part in picks], axis=0)
        out_refs[j][...] = dot(pick.astype(BF), spaced).astype(BF)


def tables_kernel(
    beta_blocks,
    outer,
    inner,
    slot_ref,
    pair_ref,
    parity_ref,
    bpair_ref,
    btarget_ref,
    bparity_ref,
    integrals_ref,
    _,
    out_ref,
    t_ref,
    w_ref,
    hot_ref,
):
    orbitals = integrals_ref.shape[0]
    blocks, excitations = slot_ref.shape
    beta_local, beta_excitations = bpair_ref.shape
    pairs = blocks // BATCHES
    slots = hot_ref.shape[0] // pairs
    bpair = bpair_ref[...].astype(F32).T.astype(jnp.int32)
    bfactor = (1 - 2 * bparity_ref[...]).astype(F32)
    btarget = btarget_ref[...] - lax.axis_index("beta") * beta_local
    btarget = jnp.where(btarget < 0, btarget + beta_blocks, btarget)
    for v in range(beta_local):
        left = jnp.where(column_of(beta_blocks) == btarget[v : v + 1], bfactor[v : v + 1], 0.0)
        right = one(row_of(orbitals) == bpair[:, v : v + 1])
        t_ref[v * beta_blocks : (v + 1) * beta_blocks, :] = dot(left.astype(BF), right).astype(BF)
    high, low = split(dot(t_ref[...], integrals_ref[...]))
    w_ref[0] = high
    w_ref[1] = low
    pair = pair_ref[...].astype(F32).T.astype(jnp.int32)
    factor = (1 - 2 * parity_ref[...]).astype(F32)
    slot = slot_ref[...]
    partner = over(slot, CAP) ^ lax.axis_index("alpha")
    place = modulo(partner, inner) * outer + over(partner, inner)
    place = place * (BATCHES * CAP) + modulo(slot, CAP)
    for t in range(pairs):
        total = None
        for h in range(BATCHES):
            g = h * pairs + t
            row = place[g : g + 1] + h * CAP
            left = jnp.where(column_of(slots) == row, factor[g : g + 1], 0.0).astype(BF)
            part = dot(left, one(row_of(orbitals) == pair[:, g : g + 1]))
            total = part if total is None else total + part
        hot_ref[t * slots : (t + 1) * slots, :] = total.astype(BF)
    step = max(1, WIDE // slots)
    for start in range(0, pairs, step):
        hot = hot_ref[start * slots : (start + step) * slots, :]
        high, low = split(dot_nt(w_ref[0], hot) + dot_nt(w_ref[1], hot))
        for i in range(step):
            rows = slice((start + i) * beta_blocks, (start + i + 1) * beta_blocks)
            lanes = slice(i * slots, (i + 1) * slots)
            for v in range(beta_local):
                source = slice(v * beta_blocks, (v + 1) * beta_blocks)
                first = v * 2 * slots
                out_ref[rows, first : first + slots] = high[source, lanes]
                out_ref[rows, first + slots : first + 2 * slots] = low[source, lanes]


def sigma_kernel(strings, width, inner, table_ref, *refs):
    received_refs, outs, (right_ref, sum_ref, place_ref) = refs[:inner], refs[inner:-3], refs[-3:]
    received = jnp.concatenate([ref[...] for ref in received_refs], axis=0)
    slots, wide = received.shape
    group = strings * width
    both = BATCHES * group
    pairs = outs[0].shape[0] // strings // BATCHES
    blocks = table_ref.shape[0] // pairs
    batch = modulo(over(column_of(slots), CAP), BATCHES)
    low = one((batch == 0) & (row_of(both) < group))
    high = one((batch == 1) & (row_of(both) >= group))
    for tile in range(wide // both):
        x = received[:, tile * both : (tile + 1) * both]
        turned = jnp.concatenate([x[:, group:], x[:, :group]], axis=1)
        for v, (a, b) in ((2 * tile, (x, turned)), (2 * tile + 1, (turned, x))):
            value = a * low + b * high
            right_ref[2 * v * slots : (2 * v + 1) * slots, :] = value
            right_ref[(2 * v + 1) * slots : (2 * v + 2) * slots, :] = value
    product = dot(table_ref[...], right_ref[...])
    both_parts = jnp.concatenate(split(product), axis=1)
    per_tile = LANES // width
    columns = BATCHES * strings * LANES
    n = row_of(columns)
    expand = one(
        modulo(column_of(2 * both), both) == over(n, LANES) * width + modulo(n, width)
    )
    spread = dot(both_parts, expand)
    keep = modulo(column_of(pairs * blocks), per_tile) == modulo(over(n, width), per_tile)
    spread = jnp.where(keep, spread, 0.0)
    tiles = blocks // per_tile
    summed = jnp.sum(spread.reshape(pairs * tiles, per_tile, columns), axis=1)
    for hs in range(BATCHES * strings):
        sum_ref[hs] = summed[:, hs * LANES : (hs + 1) * LANES]
    per_out = tiles // len(outs)
    for q in range(tiles):
        for h in range(BATCHES):
            for s in range(strings):
                place_ref[q, pl.ds(h * pairs * strings + s, pairs, stride=strings), :] = sum_ref[
                    h * strings + s, pl.ds(q, pairs, stride=tiles), :
                ]
        at = q % per_out * LANES
        outs[q // per_out][:, at : at + LANES] = place_ref[q]


def on_device(
    coeffs,
    integrals,
    send_block,
    alpha_slot,
    alpha_pair,
    alpha_parity,
    beta_pair,
    beta_target,
    beta_parity,
):
    local_rows, local_columns = coeffs.shape
    local_blocks = alpha_slot.shape[0]
    strings = local_rows // local_blocks
    pairs = local_blocks // BATCHES
    beta_local = beta_pair.shape[0]
    width = local_columns // beta_local
    cores = lax.axis_size("beta")
    senders = lax.axis_size("alpha")
    beta_blocks = cores * beta_local
    orbitals = integrals.shape[0]
    slots = send_block.shape[1]
    wide = strings * local_columns

    outer = 1 << (senders.bit_length() - 1) // 2
    inner = senders // outer
    per = slots // senders

    extra = -(-slots // local_columns // 16) * 16
    others = (
        alpha_slot,
        alpha_pair,
        alpha_parity,
        beta_pair,
        beta_target,
        beta_parity,
        integrals,
    )
    def exchange(x, k):
        return lax.ppermute(x, "alpha", [(d, d ^ k) for d in range(senders)]) if k else x

    def pinned(*arrays):
        return [pltpu.with_memory_space_constraint(x, pltpu.HBM) for x in arrays]

    packed = pl.pallas_call(
        pack_kernel,
        in_specs=[pl.BlockSpec(memory_space=pltpu.HBM)] * 2,
        out_shape=jax.ShapeDtypeStruct((local_rows + extra, local_columns), BF),
        scratch_shapes=[
            pltpu.VMEM(send_block.shape, jnp.int32),
            pltpu.SemaphoreType.DMA((2,)),
        ],
        compiler_params=pltpu.CompilerParams(vmem_limit_bytes=40 * 2**20),
        name="pack",
    )(*pinned(coeffs, send_block))
    gathered = [exchange(packed, k * inner) for k in range(outer)]
    tables = pl.pallas_call(
        fetch_kernel,
        in_specs=[pl.BlockSpec(memory_space=pltpu.HBM)] * len(others)
        + [pl.BlockSpec(memory_space=pl.ANY)],
        out_shape=[jax.ShapeDtypeStruct(x.shape, x.dtype) for x in others],
        scratch_shapes=[pltpu.SemaphoreType.DMA((len(others),))],
        compiler_params=pltpu.CompilerParams(vmem_limit_bytes=40 * 2**20),
        name="fetch",
    )(*pinned(*others), packed)
    outgoing = pl.pallas_call(
        lambda *refs: forward_kernel(strings, width, local_rows, slots, outer, *refs),
        out_shape=[jax.ShapeDtypeStruct((outer * per, wide), BF)] * inner,
        compiler_params=pltpu.CompilerParams(vmem_limit_bytes=40 * 2**20),
        name="forward",
    )(*gathered)
    received = [exchange(x, j) for j, x in enumerate(outgoing)]
    flops = 2 * beta_local * beta_blocks * orbitals * (orbitals + 2 * pairs * slots)
    table = pl.pallas_call(
        lambda *refs: tables_kernel(beta_blocks, outer, inner, *refs),
        in_specs=[pl.BlockSpec(memory_space=pltpu.VMEM)] * len(tables)
        + [pl.BlockSpec(memory_space=pl.ANY)],
        out_shape=jax.ShapeDtypeStruct((pairs * beta_blocks, 2 * beta_local * slots), BF),
        scratch_shapes=[
            pltpu.VMEM((beta_local * beta_blocks, orbitals), BF),
            pltpu.VMEM((2, beta_local * beta_blocks, orbitals), BF),
            pltpu.VMEM((pairs * slots, orbitals), BF),
        ],
        compiler_params=pltpu.CompilerParams(vmem_limit_bytes=40 * 2**20),
        cost_estimate=pl.CostEstimate(flops=flops, bytes_accessed=8 * 2**20, transcendentals=0),
        name="tables",
    )(*tables, outgoing[0])
    part = jax.ShapeDtypeStruct((local_rows, local_columns), F32)
    both = BATCHES * strings * width
    tiles = beta_blocks * width // LANES
    parts = pl.pallas_call(
        lambda *refs: sigma_kernel(strings, width, inner, *refs),
        out_shape=[part] * cores,
        scratch_shapes=[
            pltpu.VMEM((2 * beta_local * slots, both), BF),
            pltpu.VMEM((BATCHES * strings, pairs * tiles, LANES), F32),
            pltpu.VMEM((tiles, local_rows, LANES), F32),
        ],
        compiler_params=pltpu.CompilerParams(vmem_limit_bytes=40 * 2**20),
        name="sigma",
    )(table, *received)
    result = parts[0]
    for step in range(1, cores):
        route = [(core, (core + step) % cores) for core in range(cores)]
        result = result + lax.ppermute(parts[step], "beta", route)
    return result


def solution(mesh):
    in_specs = (
        P("alpha", "beta"),
        P(),
        P("alpha", None),
        P("alpha", None),
        P("alpha", None),
        P("alpha", None),
        P("beta", None),
        P("beta", None),
        P("beta", None),
    )
    out_specs = P("alpha", "beta")
    return jax.shard_map(
        on_device, mesh=mesh, in_specs=in_specs, out_specs=out_specs, check_vma=False
    )
```

```python
import jax
import jax.numpy as jnp
from jax import lax
from jax.experimental import pallas as pl
from jax.experimental.pallas import tpu as pltpu
from jax.sharding import PartitionSpec as P

BATCHES = 2
CAP = 4
BF = jnp.bfloat16
F32 = jnp.float32
LANES = 128
WIDE = 256


def row_of(length):
    return lax.broadcasted_iota(jnp.int32, (1, length), 1)


def column_of(length):
    return lax.broadcasted_iota(jnp.int32, (length, 1), 0)


def over(x, n):
    if n & (n - 1) == 0:
        return lax.shift_right_logical(x, jnp.int32(n.bit_length() - 1))
    return lax.div(x, jnp.int32(n))


def modulo(x, n):
    if n & (n - 1) == 0:
        return x & (n - 1)
    return lax.rem(x, jnp.int32(n))


def one(condition):
    return jnp.where(condition, 1.0, 0.0).astype(BF)


def dot(a, b):
    return jnp.dot(a, b, preferred_element_type=F32)


def dot_nt(a, b):
    return lax.dot_general(a, b, (((1,), (1,)), ((), ())), preferred_element_type=F32)


def split(x):
    high = x.astype(BF)
    return high, (x - high.astype(F32)).astype(BF)


def pack_kernel(coeffs_ref, send_ref, out_ref, list_ref, sems):
    rows, slots = coeffs_ref.shape[0], send_ref.shape[1]
    total, columns = out_ref.shape
    moves = [
        pltpu.make_async_copy(send_ref, list_ref, sems.at[0]),
        pltpu.make_async_copy(coeffs_ref, out_ref.at[pl.ds(0, rows)], sems.at[1]),
    ]
    for move in moves:
        move.start()
    moves[0].wait()
    values = list_ref[...].astype(F32)
    value = jnp.zeros((total - rows, columns), F32)
    for i, first in enumerate(range(0, slots, columns)):
        row = values[:, first : first + columns]
        if row.shape[1] < columns:
            row = jnp.concatenate([row, jnp.zeros((1, columns - row.shape[1]), F32)], axis=1)
        value = value + jnp.where(column_of(total - rows) == i, row, 0.0)
    out_ref[rows:total, :] = value.astype(BF)
    moves[1].wait()


def fetch_kernel(width, *refs):
    count = (len(refs) - 3) // 2
    expand_ref, sems = refs[-2:]
    moves = [
        pltpu.make_async_copy(refs[i], refs[count + 1 + i], sems.at[i]) for i in range(count)
    ]
    for move in moves:
        move.start()
    rows, columns = expand_ref.shape
    n = row_of(columns)
    expand_ref[...] = one(
        modulo(column_of(rows), rows // 2) == over(n, LANES) * width + modulo(n, width)
    )
    for move in moves:
        move.wait()


def forward_kernel(strings, width, rows, slots, outer, *refs):
    gathered_refs, out_refs = refs[:outer], refs[outer:]
    inner = len(out_refs)
    columns = gathered_refs[0].shape[1]
    wide = strings * columns
    group = strings * width
    per = BATCHES * CAP
    blocks = rows // strings
    n = row_of(wide)
    spread = one(column_of(columns) == over(n, group) * width + modulo(n, width))
    gathered = jnp.concatenate([ref[:rows, :] for ref in gathered_refs], axis=0)
    keep = modulo(column_of(outer * rows), strings) == modulo(over(n, width), strings)
    spaced = jnp.where(keep, dot(gathered, spread), 0.0).astype(BF)
    r = column_of(inner * per)
    receiver = over(r, per) ^ lax.axis_index("alpha")
    wanted = over(modulo(r, per), CAP) * (slots // BATCHES) + receiver * CAP + modulo(r, CAP)
    wanted = wanted == row_of(slots)
    picks = []
    for k in range(outer):
        tail = gathered_refs[k][rows:, :].astype(F32)
        listed = [tail[i : i + 1] for i in range((slots + columns - 1) // columns)]
        listed = (listed[0] if len(listed) == 1 else jnp.concatenate(listed, axis=1))[:, :slots]
        chosen = jnp.sum(jnp.where(wanted, listed, 0.0), axis=1, keepdims=True).astype(jnp.int32)
        chosen = jnp.where(chosen < blocks, chosen + k * blocks, -1)
        picks.append(jnp.where(over(row_of(outer * rows), strings) == chosen, 1.0, 0.0))
    for j in range(inner):
        pick = jnp.concatenate([part[j * per : (j + 1) * per] for part in picks], axis=0)
        out_refs[j][...] = dot(pick.astype(BF), spaced).astype(BF)


def tables_kernel(
    beta_blocks,
    outer,
    inner,
    slot_ref,
    pair_ref,
    parity_ref,
    bpair_ref,
    btarget_ref,
    bparity_ref,
    integrals_ref,
    _,
    out_ref,
    t_ref,
    w_ref,
    hot_ref,
):
    orbitals = integrals_ref.shape[0]
    blocks, excitations = slot_ref.shape
    beta_local, beta_excitations = bpair_ref.shape
    pairs = blocks // BATCHES
    slots = hot_ref.shape[0] // pairs
    bpair = bpair_ref[...].astype(F32).T.astype(jnp.int32)
    bfactor = (1 - 2 * bparity_ref[...]).astype(F32)
    btarget = btarget_ref[...] - lax.axis_index("beta") * beta_local
    btarget = jnp.where(btarget < 0, btarget + beta_blocks, btarget)
    for v in range(beta_local):
        left = jnp.where(column_of(beta_blocks) == btarget[v : v + 1], bfactor[v : v + 1], 0.0)
        right = one(row_of(orbitals) == bpair[:, v : v + 1])
        t_ref[v * beta_blocks : (v + 1) * beta_blocks, :] = dot(left.astype(BF), right).astype(BF)
    high, low = split(dot(t_ref[...], integrals_ref[...]))
    w_ref[0] = high
    w_ref[1] = low
    pair = pair_ref[...].astype(F32).T.astype(jnp.int32)
    factor = (1 - 2 * parity_ref[...]).astype(F32)
    slot = slot_ref[...]
    partner = over(slot, CAP) ^ lax.axis_index("alpha")
    place = modulo(partner, inner) * outer + over(partner, inner)
    place = place * (BATCHES * CAP) + modulo(slot, CAP)
    for t in range(pairs):
        total = None
        for h in range(BATCHES):
            g = h * pairs + t
            row = place[g : g + 1] + h * CAP
            left = jnp.where(column_of(slots) == row, factor[g : g + 1], 0.0).astype(BF)
            part = dot(left, one(row_of(orbitals) == pair[:, g : g + 1]))
            total = part if total is None else total + part
        hot_ref[t * slots : (t + 1) * slots, :] = total.astype(BF)
    step = max(1, WIDE // slots)
    for start in range(0, pairs, step):
        hot = hot_ref[start * slots : (start + step) * slots, :]
        high, low = split(dot_nt(w_ref[0], hot) + dot_nt(w_ref[1], hot))
        for i in range(step):
            lanes = slice(i * slots, (i + 1) * slots)
            for v in range(beta_local):
                first = v * 2 * slots
                for part in range(beta_blocks // beta_local):
                    row = (part * pairs + start + i) * beta_local
                    rows = slice(row, row + beta_local)
                    row = v * beta_blocks + part * beta_local
                    source = slice(row, row + beta_local)
                    out_ref[rows, first : first + slots] = high[source, lanes]
                    out_ref[rows, first + slots : first + 2 * slots] = low[source, lanes]


def right_kernel(strings, width, inner, *refs):
    received_refs, (table_ref, expand_ref, right_ref), rest = refs[:inner], refs[inner : inner + 3], refs[inner + 3 :]
    received = jnp.concatenate([ref[...] for ref in received_refs], axis=0)
    slots, wide = received.shape
    group = strings * width
    both = BATCHES * group
    batch = modulo(over(column_of(slots), CAP), BATCHES)
    low = one((batch == 0) & (row_of(both) < group))
    high = one((batch == 1) & (row_of(both) >= group))
    for tile in range(wide // both):
        x = received[:, tile * both : (tile + 1) * both]
        turned = jnp.concatenate([x[:, group:], x[:, :group]], axis=1)
        for v, (a, b) in ((2 * tile, (x, turned)), (2 * tile + 1, (turned, x))):
            value = a * low + b * high
            right_ref[2 * v * slots : (2 * v + 1) * slots, :] = value
            right_ref[(2 * v + 1) * slots : (2 * v + 2) * slots, :] = value
    sigma_kernel(strings, width, 1, right_ref, table_ref, expand_ref, *rest)


def sigma_kernel(strings, width, part, right_ref, table_ref, expand_ref, out_ref, sum_ref, place_ref):
    local_rows, columns = out_ref.shape
    pairs = local_rows // strings // BATCHES
    blocks = columns // width
    rows = pairs * blocks
    product = dot(table_ref[part * rows : (part + 1) * rows, :], right_ref[...])
    both_parts = jnp.concatenate(split(product), axis=1)
    per_tile = LANES // width
    spread = dot(both_parts, expand_ref[...])
    wide = spread.shape[1]
    keep = modulo(column_of(rows), per_tile) == modulo(over(row_of(wide), width), per_tile)
    spread = jnp.where(keep, spread, 0.0)
    tiles = blocks // per_tile
    summed = jnp.sum(spread.reshape(pairs * tiles, per_tile, wide), axis=1)
    for hs in range(BATCHES * strings):
        sum_ref[hs] = summed[:, hs * LANES : (hs + 1) * LANES]
    for q in range(tiles):
        for h in range(BATCHES):
            for s in range(strings):
                place_ref[q, pl.ds(h * pairs * strings + s, pairs, stride=strings), :] = sum_ref[
                    h * strings + s, pl.ds(q, pairs, stride=tiles), :
                ]
        out_ref[:, q * LANES : (q + 1) * LANES] = place_ref[q]


def on_device(
    coeffs,
    integrals,
    send_block,
    alpha_slot,
    alpha_pair,
    alpha_parity,
    beta_pair,
    beta_target,
    beta_parity,
):
    local_rows, local_columns = coeffs.shape
    local_blocks = alpha_slot.shape[0]
    strings = local_rows // local_blocks
    pairs = local_blocks // BATCHES
    beta_local = beta_pair.shape[0]
    width = local_columns // beta_local
    cores = lax.axis_size("beta")
    senders = lax.axis_size("alpha")
    beta_blocks = cores * beta_local
    orbitals = integrals.shape[0]
    slots = send_block.shape[1]
    wide = strings * local_columns

    outer = 1 << (senders.bit_length() - 1) // 2
    inner = senders // outer
    per = slots // senders

    extra = -(-slots // local_columns // 16) * 16
    others = (
        alpha_slot,
        alpha_pair,
        alpha_parity,
        beta_pair,
        beta_target,
        beta_parity,
        integrals,
    )
    def exchange(x, k):
        return lax.ppermute(x, "alpha", [(d, d ^ k) for d in range(senders)]) if k else x

    def pinned(*arrays):
        return [pltpu.with_memory_space_constraint(x, pltpu.HBM) for x in arrays]

    packed = pl.pallas_call(
        pack_kernel,
        in_specs=[pl.BlockSpec(memory_space=pltpu.HBM)] * 2,
        out_shape=jax.ShapeDtypeStruct((local_rows + extra, local_columns), BF),
        scratch_shapes=[
            pltpu.VMEM(send_block.shape, jnp.int32),
            pltpu.SemaphoreType.DMA((2,)),
        ],
        compiler_params=pltpu.CompilerParams(vmem_limit_bytes=40 * 2**20),
        name="pack",
    )(*pinned(coeffs, send_block))
    gathered = [exchange(packed, k * inner) for k in range(outer)]
    both = BATCHES * strings * width
    *tables, expand = pl.pallas_call(
        lambda *refs: fetch_kernel(width, *refs),
        in_specs=[pl.BlockSpec(memory_space=pltpu.HBM)] * len(others)
        + [pl.BlockSpec(memory_space=pl.ANY)],
        out_shape=[jax.ShapeDtypeStruct(x.shape, x.dtype) for x in others]
        + [jax.ShapeDtypeStruct((2 * both, BATCHES * strings * LANES), BF)],
        scratch_shapes=[pltpu.SemaphoreType.DMA((len(others),))],
        compiler_params=pltpu.CompilerParams(vmem_limit_bytes=40 * 2**20),
        name="fetch",
    )(*pinned(*others), packed)
    outgoing = pl.pallas_call(
        lambda *refs: forward_kernel(strings, width, local_rows, slots, outer, *refs),
        out_shape=[jax.ShapeDtypeStruct((outer * per, wide), BF)] * inner,
        compiler_params=pltpu.CompilerParams(vmem_limit_bytes=40 * 2**20),
        name="forward",
    )(*gathered)
    received = [exchange(x, j) for j, x in enumerate(outgoing)]
    flops = 2 * beta_local * beta_blocks * orbitals * (orbitals + 2 * pairs * slots)
    table = pl.pallas_call(
        lambda *refs: tables_kernel(beta_blocks, outer, inner, *refs),
        in_specs=[pl.BlockSpec(memory_space=pltpu.VMEM)] * len(tables)
        + [pl.BlockSpec(memory_space=pl.ANY)],
        out_shape=jax.ShapeDtypeStruct((pairs * beta_blocks, 2 * beta_local * slots), BF),
        scratch_shapes=[
            pltpu.VMEM((beta_local * beta_blocks, orbitals), BF),
            pltpu.VMEM((2, beta_local * beta_blocks, orbitals), BF),
            pltpu.VMEM((pairs * slots, orbitals), BF),
        ],
        compiler_params=pltpu.CompilerParams(vmem_limit_bytes=40 * 2**20),
        cost_estimate=pl.CostEstimate(flops=flops, bytes_accessed=8 * 2**20, transcendentals=0),
        name="tables",
    )(*tables, outgoing[0])
    part = jax.ShapeDtypeStruct((local_rows, local_columns), F32)
    tiles = local_columns // LANES
    call = dict(
        scratch_shapes=[
            pltpu.VMEM((BATCHES * strings, pairs * tiles, LANES), F32),
            pltpu.VMEM((tiles, local_rows, LANES), F32),
        ],
        compiler_params=pltpu.CompilerParams(vmem_limit_bytes=40 * 2**20),
        cost_estimate=pl.CostEstimate(
            flops=4 * pairs * slots * beta_local * beta_local * both,
            bytes_accessed=3 * 2**20,
            transcendentals=0,
        ),
    )
    right, theirs = pl.pallas_call(
        lambda *refs: right_kernel(strings, width, inner, *refs),
        out_shape=[jax.ShapeDtypeStruct((2 * beta_local * slots, both), BF), part],
        name="theirs",
        **call,
    )(*received, table, expand)

    def route(step):
        return [(core, (core + step) % cores) for core in range(cores)]

    arrived = [lax.ppermute(theirs, "beta", route(1))]
    for step in range(2, cores):
        other = pl.pallas_call(
            lambda *refs, step=step: sigma_kernel(strings, width, step, *refs),
            out_shape=part,
            name="theirs%d" % step,
            **call,
        )(right, table, expand)
        arrived.append(lax.ppermute(other, "beta", route(step)))
    result = pl.pallas_call(
        lambda *refs: sigma_kernel(strings, width, 0, *refs), out_shape=part, name="mine", **call
    )(right, table, expand)
    for value in arrived:
        result = result + value
    return result


def solution(mesh):
    in_specs = (
        P("alpha", "beta"),
        P(),
        P("alpha", None),
        P("alpha", None),
        P("alpha", None),
        P("alpha", None),
        P("beta", None),
        P("beta", None),
        P("beta", None),
    )
    out_specs = P("alpha", "beta")
    return jax.shard_map(
        on_device, mesh=mesh, in_specs=in_specs, out_specs=out_specs, check_vma=False
    )
```

```python
import jax
import jax.numpy as jnp
from jax import lax
from jax.experimental import pallas as pl
from jax.experimental.pallas import tpu as pltpu
from jax.sharding import PartitionSpec as P

BATCHES = 2
CAP = 4
BF = jnp.bfloat16
F32 = jnp.float32
LANES = 128
WIDE = 256


def row_of(length):
    return lax.broadcasted_iota(jnp.int32, (1, length), 1)


def column_of(length):
    return lax.broadcasted_iota(jnp.int32, (length, 1), 0)


def over(x, n):
    if n & (n - 1) == 0:
        return lax.shift_right_logical(x, jnp.int32(n.bit_length() - 1))
    return lax.div(x, jnp.int32(n))


def modulo(x, n):
    if n & (n - 1) == 0:
        return x & (n - 1)
    return lax.rem(x, jnp.int32(n))


def one(condition):
    return jnp.where(condition, 1.0, 0.0).astype(BF)


def dot(a, b):
    return jnp.dot(a, b, preferred_element_type=F32)


def dot_nt(a, b):
    return lax.dot_general(a, b, (((1,), (1,)), ((), ())), preferred_element_type=F32)


def split(x):
    high = x.astype(BF)
    return high, (x - high.astype(F32)).astype(BF)


def pack_kernel(coeffs_ref, send_ref, out_ref, list_ref, sems):
    rows, slots = coeffs_ref.shape[0], send_ref.shape[1]
    total, columns = out_ref.shape
    moves = [
        pltpu.make_async_copy(send_ref, list_ref, sems.at[0]),
        pltpu.make_async_copy(coeffs_ref, out_ref.at[pl.ds(0, rows)], sems.at[1]),
    ]
    for move in moves:
        move.start()
    moves[0].wait()
    values = list_ref[...].astype(F32)
    value = jnp.zeros((total - rows, columns), F32)
    for i, first in enumerate(range(0, slots, columns)):
        row = values[:, first : first + columns]
        if row.shape[1] < columns:
            row = jnp.concatenate([row, jnp.zeros((1, columns - row.shape[1]), F32)], axis=1)
        value = value + jnp.where(column_of(total - rows) == i, row, 0.0)
    out_ref[rows:total, :] = value.astype(BF)
    moves[1].wait()


def fetch_kernel(width, *refs):
    count = (len(refs) - 3) // 2
    expand_ref, sems = refs[-2:]
    moves = [
        pltpu.make_async_copy(refs[i], refs[count + 1 + i], sems.at[i]) for i in range(count)
    ]
    for move in moves:
        move.start()
    rows, columns = expand_ref.shape
    n = row_of(columns)
    expand_ref[...] = one(
        modulo(column_of(rows), rows // 2) == over(n, LANES) * width + modulo(n, width)
    )
    for move in moves:
        move.wait()


def forward_kernel(strings, width, rows, slots, outer, turn, *refs):
    gathered_refs, out_refs = [refs[turn.index(k)] for k in range(outer)], refs[outer:]
    inner = len(out_refs)
    columns = gathered_refs[0].shape[1]
    wide = strings * columns
    group = strings * width
    per = BATCHES * CAP
    blocks = rows // strings
    n = row_of(wide)
    spread = one(column_of(columns) == over(n, group) * width + modulo(n, width))
    gathered = jnp.concatenate([ref[:rows, :] for ref in gathered_refs], axis=0)
    keep = modulo(column_of(outer * rows), strings) == modulo(over(n, width), strings)
    spaced = jnp.where(keep, dot(gathered, spread), 0.0).astype(BF)
    r = column_of(inner * per)
    receiver = over(r, per) ^ lax.axis_index("alpha")
    wanted = over(modulo(r, per), CAP) * (slots // BATCHES) + receiver * CAP + modulo(r, CAP)
    wanted = wanted == row_of(slots)
    picks = []
    for k in range(outer):
        tail = gathered_refs[k][rows:, :].astype(F32)
        listed = [tail[i : i + 1] for i in range((slots + columns - 1) // columns)]
        listed = (listed[0] if len(listed) == 1 else jnp.concatenate(listed, axis=1))[:, :slots]
        chosen = jnp.sum(jnp.where(wanted, listed, 0.0), axis=1, keepdims=True).astype(jnp.int32)
        chosen = jnp.where(chosen < blocks, chosen + k * blocks, -1)
        picks.append(jnp.where(over(row_of(outer * rows), strings) == chosen, 1.0, 0.0))
    for j in range(inner):
        pick = jnp.concatenate([part[j * per : (j + 1) * per] for part in picks], axis=0)
        out_refs[j][...] = dot(pick.astype(BF), spaced).astype(BF)


def tables_kernel(
    beta_blocks,
    outer,
    inner,
    slot_ref,
    pair_ref,
    parity_ref,
    bpair_ref,
    btarget_ref,
    bparity_ref,
    integrals_ref,
    _,
    out_ref,
    t_ref,
    w_ref,
    hot_ref,
):
    orbitals = integrals_ref.shape[0]
    blocks, excitations = slot_ref.shape
    beta_local, beta_excitations = bpair_ref.shape
    pairs = blocks // BATCHES
    slots = hot_ref.shape[0] // pairs
    bpair = bpair_ref[...].astype(F32).T.astype(jnp.int32)
    bfactor = (1 - 2 * bparity_ref[...]).astype(F32)
    btarget = btarget_ref[...] - lax.axis_index("beta") * beta_local
    btarget = jnp.where(btarget < 0, btarget + beta_blocks, btarget)
    for v in range(beta_local):
        left = jnp.where(column_of(beta_blocks) == btarget[v : v + 1], bfactor[v : v + 1], 0.0)
        right = one(row_of(orbitals) == bpair[:, v : v + 1])
        t_ref[v * beta_blocks : (v + 1) * beta_blocks, :] = dot(left.astype(BF), right).astype(BF)
    high, low = split(dot(t_ref[...], integrals_ref[...]))
    w_ref[0] = high
    w_ref[1] = low
    pair = pair_ref[...].astype(F32).T.astype(jnp.int32)
    factor = (1 - 2 * parity_ref[...]).astype(F32)
    slot = slot_ref[...]
    partner = over(slot, CAP) ^ lax.axis_index("alpha")
    place = modulo(partner, inner) * outer + over(partner, inner)
    place = place * (BATCHES * CAP) + modulo(slot, CAP)
    for t in range(pairs):
        total = None
        for h in range(BATCHES):
            g = h * pairs + t
            row = place[g : g + 1] + h * CAP
            left = jnp.where(column_of(slots) == row, factor[g : g + 1], 0.0).astype(BF)
            part = dot(left, one(row_of(orbitals) == pair[:, g : g + 1]))
            total = part if total is None else total + part
        hot_ref[t * slots : (t + 1) * slots, :] = total.astype(BF)
    step = max(1, WIDE // slots)
    for start in range(0, pairs, step):
        hot = hot_ref[start * slots : (start + step) * slots, :]
        high, low = split(dot_nt(w_ref[0], hot) + dot_nt(w_ref[1], hot))
        for i in range(step):
            lanes = slice(i * slots, (i + 1) * slots)
            for v in range(beta_local):
                first = v * 2 * slots
                for part in range(beta_blocks // beta_local):
                    row = (part * pairs + start + i) * beta_local
                    rows = slice(row, row + beta_local)
                    row = v * beta_blocks + part * beta_local
                    source = slice(row, row + beta_local)
                    out_ref[rows, first : first + slots] = high[source, lanes]
                    out_ref[rows, first + slots : first + 2 * slots] = low[source, lanes]


def right_kernel(strings, width, inner, *refs):
    received_refs, (table_ref, expand_ref, right_ref), rest = refs[:inner], refs[inner : inner + 3], refs[inner + 3 :]
    received = jnp.concatenate([ref[...] for ref in received_refs], axis=0)
    slots, wide = received.shape
    group = strings * width
    both = BATCHES * group
    batch = modulo(over(column_of(slots), CAP), BATCHES)
    low = one((batch == 0) & (row_of(both) < group))
    high = one((batch == 1) & (row_of(both) >= group))
    for tile in range(wide // both):
        x = received[:, tile * both : (tile + 1) * both]
        turned = jnp.concatenate([x[:, group:], x[:, :group]], axis=1)
        for v, (a, b) in ((2 * tile, (x, turned)), (2 * tile + 1, (turned, x))):
            value = a * low + b * high
            right_ref[2 * v * slots : (2 * v + 1) * slots, :] = value
            right_ref[(2 * v + 1) * slots : (2 * v + 2) * slots, :] = value
    sigma_kernel(strings, width, 1, right_ref, table_ref, expand_ref, *rest)


def sigma_kernel(strings, width, part, right_ref, table_ref, expand_ref, out_ref, sum_ref, place_ref):
    local_rows, columns = out_ref.shape
    pairs = local_rows // strings // BATCHES
    blocks = columns // width
    rows = pairs * blocks
    product = dot(table_ref[part * rows : (part + 1) * rows, :], right_ref[...])
    both_parts = jnp.concatenate(split(product), axis=1)
    per_tile = LANES // width
    spread = dot(both_parts, expand_ref[...])
    wide = spread.shape[1]
    keep = modulo(column_of(rows), per_tile) == modulo(over(row_of(wide), width), per_tile)
    spread = jnp.where(keep, spread, 0.0)
    tiles = blocks // per_tile
    summed = jnp.sum(spread.reshape(pairs * tiles, per_tile, wide), axis=1)
    for hs in range(BATCHES * strings):
        sum_ref[hs] = summed[:, hs * LANES : (hs + 1) * LANES]
    for q in range(tiles):
        for h in range(BATCHES):
            for s in range(strings):
                place_ref[q, pl.ds(h * pairs * strings + s, pairs, stride=strings), :] = sum_ref[
                    h * strings + s, pl.ds(q, pairs, stride=tiles), :
                ]
        out_ref[:, q * LANES : (q + 1) * LANES] = place_ref[q]


def on_device(
    coeffs,
    integrals,
    send_block,
    alpha_slot,
    alpha_pair,
    alpha_parity,
    beta_pair,
    beta_target,
    beta_parity,
):
    local_rows, local_columns = coeffs.shape
    local_blocks = alpha_slot.shape[0]
    strings = local_rows // local_blocks
    pairs = local_blocks // BATCHES
    beta_local = beta_pair.shape[0]
    width = local_columns // beta_local
    cores = lax.axis_size("beta")
    senders = lax.axis_size("alpha")
    beta_blocks = cores * beta_local
    orbitals = integrals.shape[0]
    slots = send_block.shape[1]
    wide = strings * local_columns

    outer = 1 << (senders.bit_length() - 1) // 2
    inner = senders // outer
    per = slots // senders

    extra = -(-slots // local_columns // 16) * 16
    others = (
        alpha_slot,
        alpha_pair,
        alpha_parity,
        beta_pair,
        beta_target,
        beta_parity,
        integrals,
    )
    def exchange(x, k):
        return lax.ppermute(x, "alpha", [(d, d ^ k) for d in range(senders)]) if k else x

    def pinned(*arrays):
        return [pltpu.with_memory_space_constraint(x, pltpu.HBM) for x in arrays]

    packed = pl.pallas_call(
        pack_kernel,
        in_specs=[pl.BlockSpec(memory_space=pltpu.HBM)] * 2,
        out_shape=jax.ShapeDtypeStruct((local_rows + extra, local_columns), BF),
        scratch_shapes=[
            pltpu.VMEM(send_block.shape, jnp.int32),
            pltpu.SemaphoreType.DMA((2,)),
        ],
        compiler_params=pltpu.CompilerParams(vmem_limit_bytes=40 * 2**20),
        name="pack",
    )(*pinned(coeffs, send_block))
    bits = outer.bit_length() - 1
    starts = sorted(range(outer), key=lambda k: int(format(k, "0%db" % bits)[::-1], 2))
    turn = starts[:1] + starts[:0:-1]
    gathered = [exchange(packed, k * inner) for k in turn]
    both = BATCHES * strings * width
    *tables, expand = pl.pallas_call(
        lambda *refs: fetch_kernel(width, *refs),
        in_specs=[pl.BlockSpec(memory_space=pltpu.HBM)] * len(others)
        + [pl.BlockSpec(memory_space=pl.ANY)],
        out_shape=[jax.ShapeDtypeStruct(x.shape, x.dtype) for x in others]
        + [jax.ShapeDtypeStruct((2 * both, BATCHES * strings * LANES), BF)],
        scratch_shapes=[pltpu.SemaphoreType.DMA((len(others),))],
        compiler_params=pltpu.CompilerParams(vmem_limit_bytes=40 * 2**20),
        name="fetch",
    )(*pinned(*others), packed)
    outgoing = pl.pallas_call(
        lambda *refs: forward_kernel(strings, width, local_rows, slots, outer, turn, *refs),
        out_shape=[jax.ShapeDtypeStruct((outer * per, wide), BF)] * inner,
        compiler_params=pltpu.CompilerParams(vmem_limit_bytes=40 * 2**20),
        name="forward",
    )(*gathered)
    received = [exchange(x, j) for j, x in enumerate(outgoing)]
    flops = 2 * beta_local * beta_blocks * orbitals * (orbitals + 2 * pairs * slots)
    table = pl.pallas_call(
        lambda *refs: tables_kernel(beta_blocks, outer, inner, *refs),
        in_specs=[pl.BlockSpec(memory_space=pltpu.VMEM)] * len(tables)
        + [pl.BlockSpec(memory_space=pl.ANY)],
        out_shape=jax.ShapeDtypeStruct((pairs * beta_blocks, 2 * beta_local * slots), BF),
        scratch_shapes=[
            pltpu.VMEM((beta_local * beta_blocks, orbitals), BF),
            pltpu.VMEM((2, beta_local * beta_blocks, orbitals), BF),
            pltpu.VMEM((pairs * slots, orbitals), BF),
        ],
        compiler_params=pltpu.CompilerParams(vmem_limit_bytes=40 * 2**20),
        cost_estimate=pl.CostEstimate(flops=flops, bytes_accessed=8 * 2**20, transcendentals=0),
        name="tables",
    )(*tables, outgoing[0])
    part = jax.ShapeDtypeStruct((local_rows, local_columns), F32)
    tiles = local_columns // LANES
    call = dict(
        scratch_shapes=[
            pltpu.VMEM((BATCHES * strings, pairs * tiles, LANES), F32),
            pltpu.VMEM((tiles, local_rows, LANES), F32),
        ],
        compiler_params=pltpu.CompilerParams(vmem_limit_bytes=40 * 2**20),
        cost_estimate=pl.CostEstimate(
            flops=4 * pairs * slots * beta_local * beta_local * both,
            bytes_accessed=3 * 2**20,
            transcendentals=0,
        ),
    )
    right, theirs = pl.pallas_call(
        lambda *refs: right_kernel(strings, width, inner, *refs),
        out_shape=[jax.ShapeDtypeStruct((2 * beta_local * slots, both), BF), part],
        name="theirs",
        **call,
    )(*received, table, expand)

    def route(step):
        return [(core, (core + step) % cores) for core in range(cores)]

    arrived = [lax.ppermute(theirs, "beta", route(1))]
    for step in range(2, cores):
        other = pl.pallas_call(
            lambda *refs, step=step: sigma_kernel(strings, width, step, *refs),
            out_shape=part,
            name="theirs%d" % step,
            **call,
        )(right, table, expand)
        arrived.append(lax.ppermute(other, "beta", route(step)))
    result = pl.pallas_call(
        lambda *refs: sigma_kernel(strings, width, 0, *refs), out_shape=part, name="mine", **call
    )(right, table, expand)
    for value in arrived:
        result = result + value
    return result


def solution(mesh):
    in_specs = (
        P("alpha", "beta"),
        P(),
        P("alpha", None),
        P("alpha", None),
        P("alpha", None),
        P("alpha", None),
        P("beta", None),
        P("beta", None),
        P("beta", None),
    )
    out_specs = P("alpha", "beta")
    return jax.shard_map(
        on_device, mesh=mesh, in_specs=in_specs, out_specs=out_specs, check_vma=False
    )
```

```python
import jax
import jax.numpy as jnp
from jax import lax
from jax.experimental import pallas as pl
from jax.experimental.pallas import tpu as pltpu
from jax.sharding import PartitionSpec as P

BATCHES = 2
CAP = 4
BF = jnp.bfloat16
F32 = jnp.float32
LANES = 128
WIDE = 256


def row_of(length):
    return lax.broadcasted_iota(jnp.int32, (1, length), 1)


def column_of(length):
    return lax.broadcasted_iota(jnp.int32, (length, 1), 0)


def over(x, n):
    if n & (n - 1) == 0:
        return lax.shift_right_logical(x, jnp.int32(n.bit_length() - 1))
    return lax.div(x, jnp.int32(n))


def modulo(x, n):
    if n & (n - 1) == 0:
        return x & (n - 1)
    return lax.rem(x, jnp.int32(n))


def one(condition):
    return jnp.where(condition, 1.0, 0.0).astype(BF)


def dot(a, b):
    return jnp.dot(a, b, preferred_element_type=F32)


def dot_nt(a, b):
    return lax.dot_general(a, b, (((1,), (1,)), ((), ())), preferred_element_type=F32)


def split(x):
    high = x.astype(BF)
    return high, (x - high.astype(F32)).astype(BF)


def pack_kernel(coeffs_ref, send_ref, out_ref, list_ref, sems):
    rows, slots = coeffs_ref.shape[0], send_ref.shape[1]
    total, columns = out_ref.shape
    moves = [
        pltpu.make_async_copy(send_ref, list_ref, sems.at[0]),
        pltpu.make_async_copy(coeffs_ref, out_ref.at[pl.ds(0, rows)], sems.at[1]),
    ]
    for move in moves:
        move.start()
    moves[0].wait()
    values = list_ref[...].astype(F32)
    value = jnp.zeros((total - rows, columns), F32)
    for i, first in enumerate(range(0, slots, columns)):
        row = values[:, first : first + columns]
        if row.shape[1] < columns:
            row = jnp.concatenate([row, jnp.zeros((1, columns - row.shape[1]), F32)], axis=1)
        value = value + jnp.where(column_of(total - rows) == i, row, 0.0)
    out_ref[rows:total, :] = value.astype(BF)
    moves[1].wait()


def fetch_kernel(width, *refs):
    count = (len(refs) - 3) // 2
    expand_ref, sems = refs[-2:]
    moves = [
        pltpu.make_async_copy(refs[i], refs[count + 1 + i], sems.at[i]) for i in range(count)
    ]
    for move in moves:
        move.start()
    rows, columns = expand_ref.shape
    n = row_of(columns)
    expand_ref[...] = one(
        modulo(column_of(rows), rows // 2) == over(n, LANES) * width + modulo(n, width)
    )
    for move in moves:
        move.wait()


def forward_kernel(strings, width, rows, slots, outer, *refs):
    gathered_refs, out_refs = refs[:outer], refs[outer:]
    inner = len(out_refs)
    columns = gathered_refs[0].shape[1]
    wide = strings * columns
    group = strings * width
    per = BATCHES * CAP
    blocks = rows // strings
    n = row_of(wide)
    spread = one(column_of(columns) == over(n, group) * width + modulo(n, width))
    gathered = jnp.concatenate([ref[:rows, :] for ref in gathered_refs], axis=0)
    keep = modulo(column_of(outer * rows), strings) == modulo(over(n, width), strings)
    spaced = jnp.where(keep, dot(gathered, spread), 0.0).astype(BF)
    r = column_of(inner * per)
    receiver = over(r, per) ^ lax.axis_index("alpha")
    wanted = over(modulo(r, per), CAP) * (slots // BATCHES) + receiver * CAP + modulo(r, CAP)
    wanted = wanted == row_of(slots)
    picks = []
    for k in range(outer):
        tail = gathered_refs[k][rows:, :].astype(F32)
        listed = [tail[i : i + 1] for i in range((slots + columns - 1) // columns)]
        listed = (listed[0] if len(listed) == 1 else jnp.concatenate(listed, axis=1))[:, :slots]
        chosen = jnp.sum(jnp.where(wanted, listed, 0.0), axis=1, keepdims=True).astype(jnp.int32)
        chosen = jnp.where(chosen < blocks, chosen + k * blocks, -1)
        picks.append(jnp.where(over(row_of(outer * rows), strings) == chosen, 1.0, 0.0))
    for j in range(inner):
        pick = jnp.concatenate([part[j * per : (j + 1) * per] for part in picks], axis=0)
        out_refs[j][...] = dot(pick.astype(BF), spaced).astype(BF)


def tables_kernel(
    beta_blocks,
    outer,
    inner,
    slot_ref,
    pair_ref,
    parity_ref,
    bpair_ref,
    btarget_ref,
    bparity_ref,
    integrals_ref,
    _,
    out_ref,
    t_ref,
    w_ref,
    hot_ref,
):
    orbitals = integrals_ref.shape[0]
    blocks, excitations = slot_ref.shape
    beta_local, beta_excitations = bpair_ref.shape
    pairs = blocks // BATCHES
    slots = hot_ref.shape[0] // pairs
    bpair = bpair_ref[...].astype(F32).T.astype(jnp.int32)
    bfactor = (1 - 2 * bparity_ref[...]).astype(F32)
    btarget = btarget_ref[...] - lax.axis_index("beta") * beta_local
    btarget = jnp.where(btarget < 0, btarget + beta_blocks, btarget)
    for v in range(beta_local):
        left = jnp.where(column_of(beta_blocks) == btarget[v : v + 1], bfactor[v : v + 1], 0.0)
        right = one(row_of(orbitals) == bpair[:, v : v + 1])
        t_ref[v * beta_blocks : (v + 1) * beta_blocks, :] = dot(left.astype(BF), right).astype(BF)
    high, low = split(dot(t_ref[...], integrals_ref[...]))
    w_ref[0] = high
    w_ref[1] = low
    pair = pair_ref[...].astype(F32).T.astype(jnp.int32)
    factor = (1 - 2 * parity_ref[...]).astype(F32)
    slot = slot_ref[...]
    partner = over(slot, CAP) ^ lax.axis_index("alpha")
    place = modulo(partner, inner) * outer + over(partner, inner)
    place = place * (BATCHES * CAP) + modulo(slot, CAP)
    for t in range(pairs):
        total = None
        for h in range(BATCHES):
            g = h * pairs + t
            row = place[g : g + 1] + h * CAP
            left = jnp.where(column_of(slots) == row, factor[g : g + 1], 0.0).astype(BF)
            part = dot(left, one(row_of(orbitals) == pair[:, g : g + 1]))
            total = part if total is None else total + part
        hot_ref[t * slots : (t + 1) * slots, :] = total.astype(BF)
    step = max(1, WIDE // slots)
    for start in range(0, pairs, step):
        hot = hot_ref[start * slots : (start + step) * slots, :]
        high, low = split(dot_nt(w_ref[0], hot) + dot_nt(w_ref[1], hot))
        for i in range(step):
            lanes = slice(i * slots, (i + 1) * slots)
            for v in range(beta_local):
                first = v * 2 * slots
                for part in range(beta_blocks // beta_local):
                    row = (part * pairs + start + i) * beta_local
                    rows = slice(row, row + beta_local)
                    row = v * beta_blocks + part * beta_local
                    source = slice(row, row + beta_local)
                    out_ref[rows, first : first + slots] = high[source, lanes]
                    out_ref[rows, first + slots : first + 2 * slots] = low[source, lanes]


def right_kernel(strings, width, inner, turn, *refs):
    received_refs, (table_ref, expand_ref, right_ref), rest = refs[:inner], refs[inner : inner + 3], refs[inner + 3 :]
    received = jnp.concatenate([received_refs[turn.index(j)][...] for j in range(inner)], axis=0)
    slots, wide = received.shape
    group = strings * width
    both = BATCHES * group
    batch = modulo(over(column_of(slots), CAP), BATCHES)
    low = one((batch == 0) & (row_of(both) < group))
    high = one((batch == 1) & (row_of(both) >= group))
    for tile in range(wide // both):
        x = received[:, tile * both : (tile + 1) * both]
        turned = jnp.concatenate([x[:, group:], x[:, :group]], axis=1)
        for v, (a, b) in ((2 * tile, (x, turned)), (2 * tile + 1, (turned, x))):
            value = a * low + b * high
            right_ref[2 * v * slots : (2 * v + 1) * slots, :] = value
            right_ref[(2 * v + 1) * slots : (2 * v + 2) * slots, :] = value
    sigma_kernel(strings, width, 1, right_ref, table_ref, expand_ref, *rest)


def sigma_kernel(strings, width, part, right_ref, table_ref, expand_ref, out_ref, sum_ref, place_ref):
    local_rows, columns = out_ref.shape
    pairs = local_rows // strings // BATCHES
    blocks = columns // width
    rows = pairs * blocks
    product = dot(table_ref[part * rows : (part + 1) * rows, :], right_ref[...])
    both_parts = jnp.concatenate(split(product), axis=1)
    per_tile = LANES // width
    spread = dot(both_parts, expand_ref[...])
    wide = spread.shape[1]
    keep = modulo(column_of(rows), per_tile) == modulo(over(row_of(wide), width), per_tile)
    spread = jnp.where(keep, spread, 0.0)
    tiles = blocks // per_tile
    summed = jnp.sum(spread.reshape(pairs * tiles, per_tile, wide), axis=1)
    for hs in range(BATCHES * strings):
        sum_ref[hs] = summed[:, hs * LANES : (hs + 1) * LANES]
    for q in range(tiles):
        for h in range(BATCHES):
            for s in range(strings):
                place_ref[q, pl.ds(h * pairs * strings + s, pairs, stride=strings), :] = sum_ref[
                    h * strings + s, pl.ds(q, pairs, stride=tiles), :
                ]
        out_ref[:, q * LANES : (q + 1) * LANES] = place_ref[q]


def on_device(
    coeffs,
    integrals,
    send_block,
    alpha_slot,
    alpha_pair,
    alpha_parity,
    beta_pair,
    beta_target,
    beta_parity,
):
    local_rows, local_columns = coeffs.shape
    local_blocks = alpha_slot.shape[0]
    strings = local_rows // local_blocks
    pairs = local_blocks // BATCHES
    beta_local = beta_pair.shape[0]
    width = local_columns // beta_local
    cores = lax.axis_size("beta")
    senders = lax.axis_size("alpha")
    beta_blocks = cores * beta_local
    orbitals = integrals.shape[0]
    slots = send_block.shape[1]
    wide = strings * local_columns

    outer = 1 << (senders.bit_length() - 1) // 2
    inner = senders // outer
    per = slots // senders

    extra = -(-slots // local_columns // 16) * 16
    others = (
        alpha_slot,
        alpha_pair,
        alpha_parity,
        beta_pair,
        beta_target,
        beta_parity,
        integrals,
    )
    def exchange(x, k):
        return lax.ppermute(x, "alpha", [(d, d ^ k) for d in range(senders)]) if k else x

    def pinned(*arrays):
        return [pltpu.with_memory_space_constraint(x, pltpu.HBM) for x in arrays]

    packed = pl.pallas_call(
        pack_kernel,
        in_specs=[pl.BlockSpec(memory_space=pltpu.HBM)] * 2,
        out_shape=jax.ShapeDtypeStruct((local_rows + extra, local_columns), BF),
        scratch_shapes=[
            pltpu.VMEM(send_block.shape, jnp.int32),
            pltpu.SemaphoreType.DMA((2,)),
        ],
        compiler_params=pltpu.CompilerParams(vmem_limit_bytes=40 * 2**20),
        name="pack",
    )(*pinned(coeffs, send_block))
    gathered = [exchange(packed, k * inner) for k in range(outer)]
    both = BATCHES * strings * width
    *tables, expand = pl.pallas_call(
        lambda *refs: fetch_kernel(width, *refs),
        in_specs=[pl.BlockSpec(memory_space=pltpu.HBM)] * len(others)
        + [pl.BlockSpec(memory_space=pl.ANY)],
        out_shape=[jax.ShapeDtypeStruct(x.shape, x.dtype) for x in others]
        + [jax.ShapeDtypeStruct((2 * both, BATCHES * strings * LANES), BF)],
        scratch_shapes=[pltpu.SemaphoreType.DMA((len(others),))],
        compiler_params=pltpu.CompilerParams(vmem_limit_bytes=40 * 2**20),
        name="fetch",
    )(*pinned(*others), packed)
    outgoing = pl.pallas_call(
        lambda *refs: forward_kernel(strings, width, local_rows, slots, outer, *refs),
        out_shape=[jax.ShapeDtypeStruct((outer * per, wide), BF)] * inner,
        compiler_params=pltpu.CompilerParams(vmem_limit_bytes=40 * 2**20),
        name="forward",
    )(*gathered)
    received = [exchange(x, j) for j, x in enumerate(outgoing)]
    turn = sorted(range(inner), key=lambda j: -format(j or outer * inner * 2 - 1, "b").count("1"))
    flops = 2 * beta_local * beta_blocks * orbitals * (orbitals + 2 * pairs * slots)
    table = pl.pallas_call(
        lambda *refs: tables_kernel(beta_blocks, outer, inner, *refs),
        in_specs=[pl.BlockSpec(memory_space=pltpu.VMEM)] * len(tables)
        + [pl.BlockSpec(memory_space=pl.ANY)],
        out_shape=jax.ShapeDtypeStruct((pairs * beta_blocks, 2 * beta_local * slots), BF),
        scratch_shapes=[
            pltpu.VMEM((beta_local * beta_blocks, orbitals), BF),
            pltpu.VMEM((2, beta_local * beta_blocks, orbitals), BF),
            pltpu.VMEM((pairs * slots, orbitals), BF),
        ],
        compiler_params=pltpu.CompilerParams(vmem_limit_bytes=40 * 2**20),
        cost_estimate=pl.CostEstimate(flops=flops, bytes_accessed=8 * 2**20, transcendentals=0),
        name="tables",
    )(*tables, outgoing[0])
    part = jax.ShapeDtypeStruct((local_rows, local_columns), F32)
    tiles = local_columns // LANES
    call = dict(
        scratch_shapes=[
            pltpu.VMEM((BATCHES * strings, pairs * tiles, LANES), F32),
            pltpu.VMEM((tiles, local_rows, LANES), F32),
        ],
        compiler_params=pltpu.CompilerParams(vmem_limit_bytes=40 * 2**20),
        cost_estimate=pl.CostEstimate(
            flops=4 * pairs * slots * beta_local * beta_local * both,
            bytes_accessed=3 * 2**20,
            transcendentals=0,
        ),
    )
    right, theirs = pl.pallas_call(
        lambda *refs: right_kernel(strings, width, inner, turn, *refs),
        out_shape=[jax.ShapeDtypeStruct((2 * beta_local * slots, both), BF), part],
        name="theirs",
        **call,
    )(*(received[j] for j in turn), table, expand)

    def route(step):
        return [(core, (core + step) % cores) for core in range(cores)]

    arrived = [lax.ppermute(theirs, "beta", route(1))]
    for step in range(2, cores):
        other = pl.pallas_call(
            lambda *refs, step=step: sigma_kernel(strings, width, step, *refs),
            out_shape=part,
            name="theirs%d" % step,
            **call,
        )(right, table, expand)
        arrived.append(lax.ppermute(other, "beta", route(step)))
    result = pl.pallas_call(
        lambda *refs: sigma_kernel(strings, width, 0, *refs), out_shape=part, name="mine", **call
    )(right, table, expand)
    for value in arrived:
        result = result + value
    return result


def solution(mesh):
    in_specs = (
        P("alpha", "beta"),
        P(),
        P("alpha", None),
        P("alpha", None),
        P("alpha", None),
        P("alpha", None),
        P("beta", None),
        P("beta", None),
        P("beta", None),
    )
    out_specs = P("alpha", "beta")
    return jax.shard_map(
        on_device, mesh=mesh, in_specs=in_specs, out_specs=out_specs, check_vma=False
    )
```

```python
import jax
import jax.numpy as jnp
from jax import lax
from jax.experimental import pallas as pl
from jax.experimental.pallas import tpu as pltpu
from jax.sharding import PartitionSpec as P

BATCHES = 2
CAP = 4
BF = jnp.bfloat16
F32 = jnp.float32
LANES = 128
WIDE = 256


def row_of(length):
    return lax.broadcasted_iota(jnp.int32, (1, length), 1)


def column_of(length):
    return lax.broadcasted_iota(jnp.int32, (length, 1), 0)


def over(x, n):
    if n & (n - 1) == 0:
        return lax.shift_right_logical(x, jnp.int32(n.bit_length() - 1))
    return lax.div(x, jnp.int32(n))


def modulo(x, n):
    if n & (n - 1) == 0:
        return x & (n - 1)
    return lax.rem(x, jnp.int32(n))


def one(condition):
    return jnp.where(condition, 1.0, 0.0).astype(BF)


def dot(a, b):
    return jnp.dot(a, b, preferred_element_type=F32)


def dot_nt(a, b):
    return lax.dot_general(a, b, (((1,), (1,)), ((), ())), preferred_element_type=F32)


def split(x):
    high = x.astype(BF)
    return high, (x - high.astype(F32)).astype(BF)


def pack_kernel(coeffs_ref, send_ref, out_ref, list_ref, sems):
    rows, slots = coeffs_ref.shape[0], send_ref.shape[1]
    total, columns = out_ref.shape
    moves = [
        pltpu.make_async_copy(send_ref, list_ref, sems.at[0]),
        pltpu.make_async_copy(coeffs_ref, out_ref.at[pl.ds(0, rows)], sems.at[1]),
    ]
    for move in moves:
        move.start()
    moves[0].wait()
    values = list_ref[...].astype(F32)
    value = jnp.zeros((total - rows, columns), F32)
    for i, first in enumerate(range(0, slots, columns)):
        row = values[:, first : first + columns]
        if row.shape[1] < columns:
            row = jnp.concatenate([row, jnp.zeros((1, columns - row.shape[1]), F32)], axis=1)
        value = value + jnp.where(column_of(total - rows) == i, row, 0.0)
    out_ref[rows:total, :] = value.astype(BF)
    moves[1].wait()


def fetch_kernel(width, *refs):
    count = (len(refs) - 4) // 2
    expand_ref, spread_ref, sems = refs[-3:]
    moves = [
        pltpu.make_async_copy(refs[i], refs[count + 1 + i], sems.at[i]) for i in range(count)
    ]
    for move in moves:
        move.start()
    rows, columns = expand_ref.shape
    n = row_of(columns)
    expand_ref[...] = one(
        modulo(column_of(rows), rows // 2) == over(n, LANES) * width + modulo(n, width)
    )
    rows, columns = spread_ref.shape
    n = row_of(columns)
    group = columns // rows * width
    spread_ref[...] = one(column_of(rows) == over(n, group) * width + modulo(n, width))
    for move in moves:
        move.wait()


def forward_kernel(strings, width, rows, slots, outer, *refs):
    gathered_refs, spread_ref, out_refs = refs[:outer], refs[outer], refs[outer + 1 :]
    inner = len(out_refs)
    columns = gathered_refs[0].shape[1]
    wide = strings * columns
    group = strings * width
    per = BATCHES * CAP
    blocks = rows // strings
    n = row_of(wide)
    gathered = jnp.concatenate([ref[:rows, :] for ref in gathered_refs], axis=0)
    keep = modulo(column_of(outer * rows), strings) == modulo(over(n, width), strings)
    spaced = jnp.where(keep, dot(gathered, spread_ref[...]), 0.0).astype(BF)
    r = column_of(inner * per)
    receiver = over(r, per) ^ lax.axis_index("alpha")
    wanted = over(modulo(r, per), CAP) * (slots // BATCHES) + receiver * CAP + modulo(r, CAP)
    wanted = wanted == row_of(slots)
    picks = []
    for k in range(outer):
        tail = gathered_refs[k][rows:, :].astype(F32)
        listed = [tail[i : i + 1] for i in range((slots + columns - 1) // columns)]
        listed = (listed[0] if len(listed) == 1 else jnp.concatenate(listed, axis=1))[:, :slots]
        chosen = jnp.sum(jnp.where(wanted, listed, 0.0), axis=1, keepdims=True).astype(jnp.int32)
        chosen = jnp.where(chosen < blocks, chosen + k * blocks, -1)
        picks.append(jnp.where(over(row_of(outer * rows), strings) == chosen, 1.0, 0.0))
    for j in range(inner):
        pick = jnp.concatenate([part[j * per : (j + 1) * per] for part in picks], axis=0)
        out_refs[j][...] = dot(pick.astype(BF), spaced).astype(BF)


def tables_kernel(
    beta_blocks,
    outer,
    inner,
    slot_ref,
    pair_ref,
    parity_ref,
    bpair_ref,
    btarget_ref,
    bparity_ref,
    integrals_ref,
    _,
    out_ref,
    t_ref,
    w_ref,
    hot_ref,
):
    orbitals = integrals_ref.shape[0]
    blocks, excitations = slot_ref.shape
    beta_local, beta_excitations = bpair_ref.shape
    pairs = blocks // BATCHES
    slots = hot_ref.shape[0] // pairs
    bpair = bpair_ref[...].astype(F32).T.astype(jnp.int32)
    bfactor = (1 - 2 * bparity_ref[...]).astype(F32)
    btarget = btarget_ref[...] - lax.axis_index("beta") * beta_local
    btarget = jnp.where(btarget < 0, btarget + beta_blocks, btarget)
    for v in range(beta_local):
        left = jnp.where(column_of(beta_blocks) == btarget[v : v + 1], bfactor[v : v + 1], 0.0)
        right = one(row_of(orbitals) == bpair[:, v : v + 1])
        t_ref[v * beta_blocks : (v + 1) * beta_blocks, :] = dot(left.astype(BF), right).astype(BF)
    high, low = split(dot(t_ref[...], integrals_ref[...]))
    w_ref[0] = high
    w_ref[1] = low
    pair = pair_ref[...].astype(F32).T.astype(jnp.int32)
    factor = (1 - 2 * parity_ref[...]).astype(F32)
    slot = slot_ref[...]
    partner = over(slot, CAP) ^ lax.axis_index("alpha")
    place = modulo(partner, inner) * outer + over(partner, inner)
    place = place * (BATCHES * CAP) + modulo(slot, CAP)
    for t in range(pairs):
        total = None
        for h in range(BATCHES):
            g = h * pairs + t
            row = place[g : g + 1] + h * CAP
            left = jnp.where(column_of(slots) == row, factor[g : g + 1], 0.0).astype(BF)
            part = dot(left, one(row_of(orbitals) == pair[:, g : g + 1]))
            total = part if total is None else total + part
        hot_ref[t * slots : (t + 1) * slots, :] = total.astype(BF)
    step = max(1, WIDE // slots)
    for start in range(0, pairs, step):
        hot = hot_ref[start * slots : (start + step) * slots, :]
        high, low = split(dot_nt(w_ref[0], hot) + dot_nt(w_ref[1], hot))
        for i in range(step):
            lanes = slice(i * slots, (i + 1) * slots)
            for v in range(beta_local):
                first = v * 2 * slots
                for part in range(beta_blocks // beta_local):
                    row = (part * pairs + start + i) * beta_local
                    rows = slice(row, row + beta_local)
                    row = v * beta_blocks + part * beta_local
                    source = slice(row, row + beta_local)
                    out_ref[rows, first : first + slots] = high[source, lanes]
                    out_ref[rows, first + slots : first + 2 * slots] = low[source, lanes]


def right_kernel(strings, width, inner, turn, *refs):
    received_refs, (table_ref, expand_ref, right_ref), rest = refs[:inner], refs[inner : inner + 3], refs[inner + 3 :]
    received = jnp.concatenate([received_refs[turn.index(j)][...] for j in range(inner)], axis=0)
    slots, wide = received.shape
    group = strings * width
    both = BATCHES * group
    batch = modulo(over(column_of(slots), CAP), BATCHES)
    low = one((batch == 0) & (row_of(both) < group))
    high = one((batch == 1) & (row_of(both) >= group))
    for tile in range(wide // both):
        x = received[:, tile * both : (tile + 1) * both]
        turned = jnp.concatenate([x[:, group:], x[:, :group]], axis=1)
        for v, (a, b) in ((2 * tile, (x, turned)), (2 * tile + 1, (turned, x))):
            value = a * low + b * high
            right_ref[2 * v * slots : (2 * v + 1) * slots, :] = value
            right_ref[(2 * v + 1) * slots : (2 * v + 2) * slots, :] = value
    sigma_kernel(strings, width, 1, right_ref, table_ref, expand_ref, *rest)


def sigma_kernel(strings, width, part, right_ref, table_ref, expand_ref, out_ref, sum_ref, place_ref):
    local_rows, columns = out_ref.shape
    pairs = local_rows // strings // BATCHES
    blocks = columns // width
    rows = pairs * blocks
    product = dot(table_ref[part * rows : (part + 1) * rows, :], right_ref[...])
    both_parts = jnp.concatenate(split(product), axis=1)
    per_tile = LANES // width
    spread = dot(both_parts, expand_ref[...])
    wide = spread.shape[1]
    keep = modulo(column_of(rows), per_tile) == modulo(over(row_of(wide), width), per_tile)
    spread = jnp.where(keep, spread, 0.0)
    tiles = blocks // per_tile
    summed = jnp.sum(spread.reshape(pairs * tiles, per_tile, wide), axis=1)
    for hs in range(BATCHES * strings):
        sum_ref[hs] = summed[:, hs * LANES : (hs + 1) * LANES]
    for q in range(tiles):
        for h in range(BATCHES):
            for s in range(strings):
                place_ref[q, pl.ds(h * pairs * strings + s, pairs, stride=strings), :] = sum_ref[
                    h * strings + s, pl.ds(q, pairs, stride=tiles), :
                ]
        out_ref[:, q * LANES : (q + 1) * LANES] = place_ref[q]


def on_device(
    coeffs,
    integrals,
    send_block,
    alpha_slot,
    alpha_pair,
    alpha_parity,
    beta_pair,
    beta_target,
    beta_parity,
):
    local_rows, local_columns = coeffs.shape
    local_blocks = alpha_slot.shape[0]
    strings = local_rows // local_blocks
    pairs = local_blocks // BATCHES
    beta_local = beta_pair.shape[0]
    width = local_columns // beta_local
    cores = lax.axis_size("beta")
    senders = lax.axis_size("alpha")
    beta_blocks = cores * beta_local
    orbitals = integrals.shape[0]
    slots = send_block.shape[1]
    wide = strings * local_columns

    outer = 1 << (senders.bit_length() - 1) // 2
    inner = senders // outer
    per = slots // senders

    extra = -(-slots // local_columns // 16) * 16
    others = (
        alpha_slot,
        alpha_pair,
        alpha_parity,
        beta_pair,
        beta_target,
        beta_parity,
        integrals,
    )
    def exchange(x, k):
        return lax.ppermute(x, "alpha", [(d, d ^ k) for d in range(senders)]) if k else x

    def pinned(*arrays):
        return [pltpu.with_memory_space_constraint(x, pltpu.HBM) for x in arrays]

    packed = pl.pallas_call(
        pack_kernel,
        in_specs=[pl.BlockSpec(memory_space=pltpu.HBM)] * 2,
        out_shape=jax.ShapeDtypeStruct((local_rows + extra, local_columns), BF),
        scratch_shapes=[
            pltpu.VMEM(send_block.shape, jnp.int32),
            pltpu.SemaphoreType.DMA((2,)),
        ],
        compiler_params=pltpu.CompilerParams(vmem_limit_bytes=40 * 2**20),
        name="pack",
    )(*pinned(coeffs, send_block))
    gathered = [exchange(packed, k * inner) for k in range(outer)]
    both = BATCHES * strings * width
    *tables, expand, spread = pl.pallas_call(
        lambda *refs: fetch_kernel(width, *refs),
        in_specs=[pl.BlockSpec(memory_space=pltpu.HBM)] * len(others)
        + [pl.BlockSpec(memory_space=pl.ANY)],
        out_shape=[jax.ShapeDtypeStruct(x.shape, x.dtype) for x in others]
        + [
            jax.ShapeDtypeStruct((2 * both, BATCHES * strings * LANES), BF),
            jax.ShapeDtypeStruct((local_columns, wide), BF),
        ],
        scratch_shapes=[pltpu.SemaphoreType.DMA((len(others),))],
        compiler_params=pltpu.CompilerParams(vmem_limit_bytes=40 * 2**20),
        name="fetch",
    )(*pinned(*others), packed)
    outgoing = pl.pallas_call(
        lambda *refs: forward_kernel(strings, width, local_rows, slots, outer, *refs),
        out_shape=[jax.ShapeDtypeStruct((outer * per, wide), BF)] * inner,
        compiler_params=pltpu.CompilerParams(vmem_limit_bytes=40 * 2**20),
        name="forward",
    )(*gathered, spread)
    received = [exchange(x, j) for j, x in enumerate(outgoing)]
    turn = sorted(range(inner), key=lambda j: -format(j or outer * inner * 2 - 1, "b").count("1"))
    turn = turn[:1] + turn[-2:-1] + turn[1:-2] + turn[-1:]
    flops = 2 * beta_local * beta_blocks * orbitals * (orbitals + 2 * pairs * slots)
    table = pl.pallas_call(
        lambda *refs: tables_kernel(beta_blocks, outer, inner, *refs),
        in_specs=[pl.BlockSpec(memory_space=pltpu.VMEM)] * len(tables)
        + [pl.BlockSpec(memory_space=pl.ANY)],
        out_shape=jax.ShapeDtypeStruct((pairs * beta_blocks, 2 * beta_local * slots), BF),
        scratch_shapes=[
            pltpu.VMEM((beta_local * beta_blocks, orbitals), BF),
            pltpu.VMEM((2, beta_local * beta_blocks, orbitals), BF),
            pltpu.VMEM((pairs * slots, orbitals), BF),
        ],
        compiler_params=pltpu.CompilerParams(vmem_limit_bytes=40 * 2**20),
        cost_estimate=pl.CostEstimate(flops=flops, bytes_accessed=8 * 2**20, transcendentals=0),
        name="tables",
    )(*tables, outgoing[0])
    part = jax.ShapeDtypeStruct((local_rows, local_columns), F32)
    tiles = local_columns // LANES
    call = dict(
        scratch_shapes=[
            pltpu.VMEM((BATCHES * strings, pairs * tiles, LANES), F32),
            pltpu.VMEM((tiles, local_rows, LANES), F32),
        ],
        compiler_params=pltpu.CompilerParams(vmem_limit_bytes=40 * 2**20),
        cost_estimate=pl.CostEstimate(
            flops=4 * pairs * slots * beta_local * beta_local * both,
            bytes_accessed=3 * 2**20,
            transcendentals=0,
        ),
    )
    right, theirs = pl.pallas_call(
        lambda *refs: right_kernel(strings, width, inner, turn, *refs),
        out_shape=[jax.ShapeDtypeStruct((2 * beta_local * slots, both), BF), part],
        name="theirs",
        **call,
    )(*(received[j] for j in turn), table, expand)

    def route(step):
        return [(core, (core + step) % cores) for core in range(cores)]

    arrived = [lax.ppermute(theirs, "beta", route(1))]
    for step in range(2, cores):
        other = pl.pallas_call(
            lambda *refs, step=step: sigma_kernel(strings, width, step, *refs),
            out_shape=part,
            name="theirs%d" % step,
            **call,
        )(right, table, expand)
        arrived.append(lax.ppermute(other, "beta", route(step)))
    result = pl.pallas_call(
        lambda *refs: sigma_kernel(strings, width, 0, *refs), out_shape=part, name="mine", **call
    )(right, table, expand)
    for value in arrived:
        result = result + value
    return result


def solution(mesh):
    in_specs = (
        P("alpha", "beta"),
        P(),
        P("alpha", None),
        P("alpha", None),
        P("alpha", None),
        P("alpha", None),
        P("beta", None),
        P("beta", None),
        P("beta", None),
    )
    out_specs = P("alpha", "beta")
    return jax.shard_map(
        on_device, mesh=mesh, in_specs=in_specs, out_specs=out_specs, check_vma=False
    )
```

```python
import jax
import jax.numpy as jnp
from jax import lax
from jax.experimental import pallas as pl
from jax.experimental.pallas import tpu as pltpu
from jax.sharding import PartitionSpec as P

BATCHES = 2
CAP = 4
BF = jnp.bfloat16
F32 = jnp.float32
LANES = 128
WIDE = 256


def row_of(length):
    return lax.broadcasted_iota(jnp.int32, (1, length), 1)


def column_of(length):
    return lax.broadcasted_iota(jnp.int32, (length, 1), 0)


def over(x, n):
    if n & (n - 1) == 0:
        return lax.shift_right_logical(x, jnp.int32(n.bit_length() - 1))
    return lax.div(x, jnp.int32(n))


def modulo(x, n):
    if n & (n - 1) == 0:
        return x & (n - 1)
    return lax.rem(x, jnp.int32(n))


def one(condition):
    return jnp.where(condition, 1.0, 0.0).astype(BF)


def dot(a, b):
    return jnp.dot(a, b, preferred_element_type=F32)


def dot_nt(a, b):
    return lax.dot_general(a, b, (((1,), (1,)), ((), ())), preferred_element_type=F32)


def split(x):
    high = x.astype(BF)
    return high, (x - high.astype(F32)).astype(BF)


def pack_kernel(coeffs_ref, send_ref, out_ref, list_ref, sems):
    rows, slots = coeffs_ref.shape[0], send_ref.shape[1]
    total, columns = out_ref.shape
    moves = [
        pltpu.make_async_copy(send_ref, list_ref, sems.at[0]),
        pltpu.make_async_copy(coeffs_ref, out_ref.at[pl.ds(0, rows)], sems.at[1]),
    ]
    for move in moves:
        move.start()
    moves[0].wait()
    values = list_ref[...].astype(F32)
    value = jnp.zeros((total - rows, columns), F32)
    for i, first in enumerate(range(0, slots, columns)):
        row = values[:, first : first + columns]
        if row.shape[1] < columns:
            row = jnp.concatenate([row, jnp.zeros((1, columns - row.shape[1]), F32)], axis=1)
        value = value + jnp.where(column_of(total - rows) == i, row, 0.0)
    out_ref[rows:total, :] = value.astype(BF)
    moves[1].wait()


def fetch_kernel(width, *refs):
    count = (len(refs) - 4) // 2
    expand_ref, spread_ref, sems = refs[-3:]
    moves = [
        pltpu.make_async_copy(refs[i], refs[count + 1 + i], sems.at[i]) for i in range(count)
    ]
    for move in moves:
        move.start()
    rows, columns = expand_ref.shape
    n = row_of(columns)
    expand_ref[...] = one(
        modulo(column_of(rows), rows // 2) == over(n, LANES) * width + modulo(n, width)
    )
    rows, columns = spread_ref.shape
    n = row_of(columns)
    group = columns // rows * width
    spread_ref[...] = one(column_of(rows) == over(n, group) * width + modulo(n, width))
    for move in moves:
        move.wait()


def forward_kernel(strings, width, rows, slots, outer, *refs):
    gathered_refs, spread_ref, out_refs = refs[:outer], refs[outer], refs[outer + 1 :]
    inner = len(out_refs)
    columns = gathered_refs[0].shape[1]
    wide = strings * columns
    group = strings * width
    per = BATCHES * CAP
    blocks = rows // strings
    n = row_of(wide)
    gathered = jnp.concatenate([ref[:rows, :] for ref in gathered_refs], axis=0)
    keep = modulo(column_of(outer * rows), strings) == modulo(over(n, width), strings)
    spaced = jnp.where(keep, dot(gathered, spread_ref[...]), 0.0).astype(BF)
    r = column_of(inner * per)
    receiver = over(r, per) ^ lax.axis_index("alpha")
    wanted = over(modulo(r, per), CAP) * (slots // BATCHES) + receiver * CAP + modulo(r, CAP)
    wanted = wanted == row_of(slots)
    picks = []
    for k in range(outer):
        tail = gathered_refs[k][rows:, :].astype(F32)
        listed = [tail[i : i + 1] for i in range((slots + columns - 1) // columns)]
        listed = (listed[0] if len(listed) == 1 else jnp.concatenate(listed, axis=1))[:, :slots]
        chosen = jnp.sum(jnp.where(wanted, listed, 0.0), axis=1, keepdims=True).astype(jnp.int32)
        chosen = jnp.where(chosen < blocks, chosen + k * blocks, -1)
        picks.append(jnp.where(over(row_of(outer * rows), strings) == chosen, 1.0, 0.0))
    for j in range(inner):
        pick = jnp.concatenate([part[j * per : (j + 1) * per] for part in picks], axis=0)
        out_refs[j][...] = dot(pick.astype(BF), spaced).astype(BF)


def tables_kernel(
    beta_blocks,
    outer,
    inner,
    slot_ref,
    pair_ref,
    parity_ref,
    bpair_ref,
    btarget_ref,
    bparity_ref,
    integrals_ref,
    _,
    out_ref,
    t_ref,
    w_ref,
    hot_ref,
):
    orbitals = integrals_ref.shape[0]
    blocks, excitations = slot_ref.shape
    beta_local, beta_excitations = bpair_ref.shape
    pairs = blocks // BATCHES
    slots = hot_ref.shape[0] // pairs
    bpair = bpair_ref[...].astype(F32).T.astype(jnp.int32)
    bfactor = (1 - 2 * bparity_ref[...]).astype(F32)
    btarget = btarget_ref[...] - lax.axis_index("beta") * beta_local
    btarget = jnp.where(btarget < 0, btarget + beta_blocks, btarget)
    for v in range(beta_local):
        left = jnp.where(column_of(beta_blocks) == btarget[v : v + 1], bfactor[v : v + 1], 0.0)
        right = one(row_of(orbitals) == bpair[:, v : v + 1])
        t_ref[v * beta_blocks : (v + 1) * beta_blocks, :] = dot(left.astype(BF), right).astype(BF)
    high, low = split(dot(t_ref[...], integrals_ref[...]))
    wide = beta_local * beta_blocks
    w_ref[:wide] = high
    w_ref[wide:] = low
    pair = pair_ref[...].astype(F32).T.astype(jnp.int32)
    factor = (1 - 2 * parity_ref[...]).astype(F32)
    slot = slot_ref[...]
    partner = over(slot, CAP) ^ lax.axis_index("alpha")
    place = modulo(partner, inner) * outer + over(partner, inner)
    place = place * (BATCHES * CAP) + modulo(slot, CAP)
    for t in range(pairs):
        total = None
        for h in range(BATCHES):
            g = h * pairs + t
            row = place[g : g + 1] + h * CAP
            left = jnp.where(column_of(slots) == row, factor[g : g + 1], 0.0).astype(BF)
            part = dot(left, one(row_of(orbitals) == pair[:, g : g + 1]))
            total = part if total is None else total + part
        hot_ref[t * slots : (t + 1) * slots, :] = total.astype(BF)
    step = max(1, WIDE // slots)
    for start in range(0, pairs, step):
        hot = hot_ref[start * slots : (start + step) * slots, :]
        product = dot_nt(w_ref[...], hot)
        high, low = split(product[:wide] + product[wide:])
        for i in range(step):
            lanes = slice(i * slots, (i + 1) * slots)
            for v in range(beta_local):
                columns = slice(v * slots, (v + 1) * slots)
                for part in range(beta_blocks // beta_local):
                    row = v * beta_blocks + part * beta_local
                    source = slice(row, row + beta_local)
                    row = (2 * part * pairs + start + i) * beta_local
                    out_ref[row : row + beta_local, columns] = high[source, lanes]
                    row += pairs * beta_local
                    out_ref[row : row + beta_local, columns] = low[source, lanes]


def right_kernel(strings, width, inner, turn, *refs):
    received_refs, (table_ref, expand_ref, right_ref), rest = refs[:inner], refs[inner : inner + 3], refs[inner + 3 :]
    received = jnp.concatenate([received_refs[turn.index(j)][...] for j in range(inner)], axis=0)
    slots, wide = received.shape
    group = strings * width
    both = BATCHES * group
    batch = modulo(over(column_of(slots), CAP), BATCHES)
    low = one((batch == 0) & (row_of(both) < group))
    high = one((batch == 1) & (row_of(both) >= group))
    for tile in range(wide // both):
        x = received[:, tile * both : (tile + 1) * both]
        turned = jnp.concatenate([x[:, group:], x[:, :group]], axis=1)
        for v, (a, b) in ((2 * tile, (x, turned)), (2 * tile + 1, (turned, x))):
            right_ref[v * slots : (v + 1) * slots, :] = a * low + b * high
    sigma_kernel(strings, width, 1, right_ref, table_ref, expand_ref, *rest)


def sigma_kernel(strings, width, part, right_ref, table_ref, expand_ref, out_ref, sum_ref, place_ref):
    local_rows, columns = out_ref.shape
    pairs = local_rows // strings // BATCHES
    blocks = columns // width
    rows = pairs * blocks
    product = dot(table_ref[part * 2 * rows : (part + 1) * 2 * rows, :], right_ref[...])
    product = product[:rows] + product[rows:]
    both_parts = jnp.concatenate(split(product), axis=1)
    per_tile = LANES // width
    spread = dot(both_parts, expand_ref[...])
    wide = spread.shape[1]
    keep = modulo(column_of(rows), per_tile) == modulo(over(row_of(wide), width), per_tile)
    spread = jnp.where(keep, spread, 0.0)
    tiles = blocks // per_tile
    summed = jnp.sum(spread.reshape(pairs * tiles, per_tile, wide), axis=1)
    for hs in range(BATCHES * strings):
        sum_ref[hs] = summed[:, hs * LANES : (hs + 1) * LANES]
    for q in range(tiles):
        for h in range(BATCHES):
            for s in range(strings):
                place_ref[q, pl.ds(h * pairs * strings + s, pairs, stride=strings), :] = sum_ref[
                    h * strings + s, pl.ds(q, pairs, stride=tiles), :
                ]
        out_ref[:, q * LANES : (q + 1) * LANES] = place_ref[q]


def on_device(
    coeffs,
    integrals,
    send_block,
    alpha_slot,
    alpha_pair,
    alpha_parity,
    beta_pair,
    beta_target,
    beta_parity,
):
    local_rows, local_columns = coeffs.shape
    local_blocks = alpha_slot.shape[0]
    strings = local_rows // local_blocks
    pairs = local_blocks // BATCHES
    beta_local = beta_pair.shape[0]
    width = local_columns // beta_local
    cores = lax.axis_size("beta")
    senders = lax.axis_size("alpha")
    beta_blocks = cores * beta_local
    orbitals = integrals.shape[0]
    slots = send_block.shape[1]
    wide = strings * local_columns

    outer = 1 << (senders.bit_length() - 1) // 2
    inner = senders // outer
    per = slots // senders

    extra = -(-slots // local_columns // 16) * 16
    others = (
        alpha_slot,
        alpha_pair,
        alpha_parity,
        beta_pair,
        beta_target,
        beta_parity,
        integrals,
    )
    def exchange(x, k):
        return lax.ppermute(x, "alpha", [(d, d ^ k) for d in range(senders)]) if k else x

    def pinned(*arrays):
        return [pltpu.with_memory_space_constraint(x, pltpu.HBM) for x in arrays]

    packed = pl.pallas_call(
        pack_kernel,
        in_specs=[pl.BlockSpec(memory_space=pltpu.HBM)] * 2,
        out_shape=jax.ShapeDtypeStruct((local_rows + extra, local_columns), BF),
        scratch_shapes=[
            pltpu.VMEM(send_block.shape, jnp.int32),
            pltpu.SemaphoreType.DMA((2,)),
        ],
        compiler_params=pltpu.CompilerParams(vmem_limit_bytes=40 * 2**20),
        name="pack",
    )(*pinned(coeffs, send_block))
    gathered = [exchange(packed, k * inner) for k in range(outer)]
    both = BATCHES * strings * width
    *tables, expand, spread = pl.pallas_call(
        lambda *refs: fetch_kernel(width, *refs),
        in_specs=[pl.BlockSpec(memory_space=pltpu.HBM)] * len(others)
        + [pl.BlockSpec(memory_space=pl.ANY)],
        out_shape=[jax.ShapeDtypeStruct(x.shape, x.dtype) for x in others]
        + [
            jax.ShapeDtypeStruct((2 * both, BATCHES * strings * LANES), BF),
            jax.ShapeDtypeStruct((local_columns, wide), BF),
        ],
        scratch_shapes=[pltpu.SemaphoreType.DMA((len(others),))],
        compiler_params=pltpu.CompilerParams(vmem_limit_bytes=40 * 2**20),
        name="fetch",
    )(*pinned(*others), packed)
    outgoing = pl.pallas_call(
        lambda *refs: forward_kernel(strings, width, local_rows, slots, outer, *refs),
        out_shape=[jax.ShapeDtypeStruct((outer * per, wide), BF)] * inner,
        compiler_params=pltpu.CompilerParams(vmem_limit_bytes=40 * 2**20),
        name="forward",
    )(*gathered, spread)
    received = [exchange(x, j) for j, x in enumerate(outgoing)]
    turn = sorted(range(inner), key=lambda j: -format(j or outer * inner * 2 - 1, "b").count("1"))
    turn = turn[:1] + turn[-2:-1] + turn[1:-2] + turn[-1:]
    flops = 2 * beta_local * beta_blocks * orbitals * (orbitals + 2 * pairs * slots)
    table = pl.pallas_call(
        lambda *refs: tables_kernel(beta_blocks, outer, inner, *refs),
        in_specs=[pl.BlockSpec(memory_space=pltpu.VMEM)] * len(tables)
        + [pl.BlockSpec(memory_space=pl.ANY)],
        out_shape=jax.ShapeDtypeStruct((2 * pairs * beta_blocks, beta_local * slots), BF),
        scratch_shapes=[
            pltpu.VMEM((beta_local * beta_blocks, orbitals), BF),
            pltpu.VMEM((2 * beta_local * beta_blocks, orbitals), BF),
            pltpu.VMEM((pairs * slots, orbitals), BF),
        ],
        compiler_params=pltpu.CompilerParams(vmem_limit_bytes=40 * 2**20),
        cost_estimate=pl.CostEstimate(flops=flops, bytes_accessed=8 * 2**20, transcendentals=0),
        name="tables",
    )(*tables, outgoing[0])
    part = jax.ShapeDtypeStruct((local_rows, local_columns), F32)
    tiles = local_columns // LANES
    call = dict(
        scratch_shapes=[
            pltpu.VMEM((BATCHES * strings, pairs * tiles, LANES), F32),
            pltpu.VMEM((tiles, local_rows, LANES), F32),
        ],
        compiler_params=pltpu.CompilerParams(vmem_limit_bytes=40 * 2**20),
        cost_estimate=pl.CostEstimate(
            flops=4 * pairs * slots * beta_local * beta_local * both,
            bytes_accessed=3 * 2**20,
            transcendentals=0,
        ),
    )
    right, theirs = pl.pallas_call(
        lambda *refs: right_kernel(strings, width, inner, turn, *refs),
        out_shape=[jax.ShapeDtypeStruct((beta_local * slots, both), BF), part],
        name="theirs",
        **call,
    )(*(received[j] for j in turn), table, expand)

    def route(step):
        return [(core, (core + step) % cores) for core in range(cores)]

    arrived = [lax.ppermute(theirs, "beta", route(1))]
    for step in range(2, cores):
        other = pl.pallas_call(
            lambda *refs, step=step: sigma_kernel(strings, width, step, *refs),
            out_shape=part,
            name="theirs%d" % step,
            **call,
        )(right, table, expand)
        arrived.append(lax.ppermute(other, "beta", route(step)))
    result = pl.pallas_call(
        lambda *refs: sigma_kernel(strings, width, 0, *refs), out_shape=part, name="mine", **call
    )(right, table, expand)
    for value in arrived:
        result = result + value
    return result


def solution(mesh):
    in_specs = (
        P("alpha", "beta"),
        P(),
        P("alpha", None),
        P("alpha", None),
        P("alpha", None),
        P("alpha", None),
        P("beta", None),
        P("beta", None),
        P("beta", None),
    )
    out_specs = P("alpha", "beta")
    return jax.shard_map(
        on_device, mesh=mesh, in_specs=in_specs, out_specs=out_specs, check_vma=False
    )
```

```python
import jax
import jax.numpy as jnp
from jax import lax
from jax.experimental import pallas as pl
from jax.experimental.pallas import tpu as pltpu
from jax.sharding import PartitionSpec as P

BATCHES = 2
CAP = 4
BF = jnp.bfloat16
F32 = jnp.float32
LANES = 128
WIDE = 256


def row_of(length):
    return lax.broadcasted_iota(jnp.int32, (1, length), 1)


def column_of(length):
    return lax.broadcasted_iota(jnp.int32, (length, 1), 0)


def over(x, n):
    if n & (n - 1) == 0:
        return lax.shift_right_logical(x, jnp.int32(n.bit_length() - 1))
    return lax.div(x, jnp.int32(n))


def modulo(x, n):
    if n & (n - 1) == 0:
        return x & (n - 1)
    return lax.rem(x, jnp.int32(n))


def turned(x, inner):
    bits = inner.bit_length() - 1
    back = sum(((x >> i) & 1) << (bits - 1 - i) for i in range(bits))
    return jnp.where(lax.axis_index("beta") == 1, back, x)


def one(condition):
    return jnp.where(condition, 1.0, 0.0).astype(BF)


def dot(a, b):
    return jnp.dot(a, b, preferred_element_type=F32)


def dot_nt(a, b):
    return lax.dot_general(a, b, (((1,), (1,)), ((), ())), preferred_element_type=F32)


def split(x):
    high = x.astype(BF)
    return high, (x - high.astype(F32)).astype(BF)


def pack_kernel(coeffs_ref, send_ref, out_ref, list_ref, sems):
    rows, slots = coeffs_ref.shape[0], send_ref.shape[1]
    total, columns = out_ref.shape
    moves = [
        pltpu.make_async_copy(send_ref, list_ref, sems.at[0]),
        pltpu.make_async_copy(coeffs_ref, out_ref.at[pl.ds(0, rows)], sems.at[1]),
    ]
    for move in moves:
        move.start()
    moves[0].wait()
    values = list_ref[...].astype(F32)
    value = jnp.zeros((total - rows, columns), F32)
    for i, first in enumerate(range(0, slots, columns)):
        row = values[:, first : first + columns]
        if row.shape[1] < columns:
            row = jnp.concatenate([row, jnp.zeros((1, columns - row.shape[1]), F32)], axis=1)
        value = value + jnp.where(column_of(total - rows) == i, row, 0.0)
    out_ref[rows:total, :] = value.astype(BF)
    moves[1].wait()


def fetch_kernel(width, *refs):
    count = (len(refs) - 4) // 2
    expand_ref, spread_ref, sems = refs[-3:]
    moves = [
        pltpu.make_async_copy(refs[i], refs[count + 1 + i], sems.at[i]) for i in range(count)
    ]
    for move in moves:
        move.start()
    rows, columns = expand_ref.shape
    n = row_of(columns)
    expand_ref[...] = one(
        modulo(column_of(rows), rows // 2) == over(n, LANES) * width + modulo(n, width)
    )
    rows, columns = spread_ref.shape
    n = row_of(columns)
    group = columns // rows * width
    spread_ref[...] = one(column_of(rows) == over(n, group) * width + modulo(n, width))
    for move in moves:
        move.wait()


def forward_kernel(strings, width, rows, slots, outer, *refs):
    gathered_refs, spread_ref, out_refs = refs[:outer], refs[outer], refs[outer + 1 :]
    inner = len(out_refs)
    columns = gathered_refs[0].shape[1]
    wide = strings * columns
    group = strings * width
    per = BATCHES * CAP
    blocks = rows // strings
    n = row_of(wide)
    gathered = jnp.concatenate([ref[:rows, :] for ref in gathered_refs], axis=0)
    keep = modulo(column_of(outer * rows), strings) == modulo(over(n, width), strings)
    spaced = jnp.where(keep, dot(gathered, spread_ref[...]), 0.0).astype(BF)
    r = column_of(inner * per)
    receiver = turned(over(r, per), inner) ^ lax.axis_index("alpha")
    wanted = over(modulo(r, per), CAP) * (slots // BATCHES) + receiver * CAP + modulo(r, CAP)
    wanted = wanted == row_of(slots)
    picks = []
    for k in range(outer):
        tail = gathered_refs[k][rows:, :].astype(F32)
        listed = [tail[i : i + 1] for i in range((slots + columns - 1) // columns)]
        listed = (listed[0] if len(listed) == 1 else jnp.concatenate(listed, axis=1))[:, :slots]
        chosen = jnp.sum(jnp.where(wanted, listed, 0.0), axis=1, keepdims=True).astype(jnp.int32)
        chosen = jnp.where(chosen < blocks, chosen + k * blocks, -1)
        picks.append(jnp.where(over(row_of(outer * rows), strings) == chosen, 1.0, 0.0))
    for j in range(inner):
        pick = jnp.concatenate([part[j * per : (j + 1) * per] for part in picks], axis=0)
        out_refs[j][...] = dot(pick.astype(BF), spaced).astype(BF)


def tables_kernel(
    beta_blocks,
    outer,
    inner,
    slot_ref,
    pair_ref,
    parity_ref,
    bpair_ref,
    btarget_ref,
    bparity_ref,
    integrals_ref,
    _,
    out_ref,
    t_ref,
    w_ref,
    hot_ref,
):
    orbitals = integrals_ref.shape[0]
    blocks, excitations = slot_ref.shape
    beta_local, beta_excitations = bpair_ref.shape
    pairs = blocks // BATCHES
    slots = hot_ref.shape[0] // pairs
    bpair = bpair_ref[...].astype(F32).T.astype(jnp.int32)
    bfactor = (1 - 2 * bparity_ref[...]).astype(F32)
    btarget = btarget_ref[...] - lax.axis_index("beta") * beta_local
    btarget = jnp.where(btarget < 0, btarget + beta_blocks, btarget)
    for v in range(beta_local):
        left = jnp.where(column_of(beta_blocks) == btarget[v : v + 1], bfactor[v : v + 1], 0.0)
        right = one(row_of(orbitals) == bpair[:, v : v + 1])
        t_ref[v * beta_blocks : (v + 1) * beta_blocks, :] = dot(left.astype(BF), right).astype(BF)
    high, low = split(dot(t_ref[...], integrals_ref[...]))
    w_ref[0] = high
    w_ref[1] = low
    pair = pair_ref[...].astype(F32).T.astype(jnp.int32)
    factor = (1 - 2 * parity_ref[...]).astype(F32)
    slot = slot_ref[...]
    partner = over(slot, CAP) ^ lax.axis_index("alpha")
    place = turned(modulo(partner, inner), inner) * outer + over(partner, inner)
    place = place * (BATCHES * CAP) + modulo(slot, CAP)
    for t in range(pairs):
        total = None
        for h in range(BATCHES):
            g = h * pairs + t
            row = place[g : g + 1] + h * CAP
            left = jnp.where(column_of(slots) == row, factor[g : g + 1], 0.0).astype(BF)
            part = dot(left, one(row_of(orbitals) == pair[:, g : g + 1]))
            total = part if total is None else total + part
        hot_ref[t * slots : (t + 1) * slots, :] = total.astype(BF)
    step = max(1, WIDE // slots)
    for start in range(0, pairs, step):
        hot = hot_ref[start * slots : (start + step) * slots, :]
        high, low = split(dot_nt(w_ref[0], hot) + dot_nt(w_ref[1], hot))
        for i in range(step):
            lanes = slice(i * slots, (i + 1) * slots)
            for v in range(beta_local):
                first = v * 2 * slots
                for part in range(beta_blocks // beta_local):
                    row = (part * pairs + start + i) * beta_local
                    rows = slice(row, row + beta_local)
                    row = v * beta_blocks + part * beta_local
                    source = slice(row, row + beta_local)
                    out_ref[rows, first : first + slots] = high[source, lanes]
                    out_ref[rows, first + slots : first + 2 * slots] = low[source, lanes]


def right_kernel(strings, width, inner, turn, *refs):
    received_refs, (table_ref, expand_ref, right_ref), rest = refs[:inner], refs[inner : inner + 3], refs[inner + 3 :]
    received = jnp.concatenate([received_refs[turn.index(j)][...] for j in range(inner)], axis=0)
    slots, wide = received.shape
    group = strings * width
    both = BATCHES * group
    batch = modulo(over(column_of(slots), CAP), BATCHES)
    low = one((batch == 0) & (row_of(both) < group))
    high = one((batch == 1) & (row_of(both) >= group))
    for tile in range(wide // both):
        x = received[:, tile * both : (tile + 1) * both]
        swapped = jnp.concatenate([x[:, group:], x[:, :group]], axis=1)
        for v, (a, b) in ((2 * tile, (x, swapped)), (2 * tile + 1, (swapped, x))):
            value = a * low + b * high
            right_ref[2 * v * slots : (2 * v + 1) * slots, :] = value
            right_ref[(2 * v + 1) * slots : (2 * v + 2) * slots, :] = value
    sigma_kernel(strings, width, 1, right_ref, table_ref, expand_ref, *rest)


def sigma_kernel(strings, width, part, right_ref, table_ref, expand_ref, out_ref, sum_ref, place_ref):
    local_rows, columns = out_ref.shape
    pairs = local_rows // strings // BATCHES
    blocks = columns // width
    rows = pairs * blocks
    product = dot(table_ref[part * rows : (part + 1) * rows, :], right_ref[...])
    both_parts = jnp.concatenate(split(product), axis=1)
    per_tile = LANES // width
    spread = dot(both_parts, expand_ref[...])
    wide = spread.shape[1]
    keep = modulo(column_of(rows), per_tile) == modulo(over(row_of(wide), width), per_tile)
    spread = jnp.where(keep, spread, 0.0)
    tiles = blocks // per_tile
    summed = jnp.sum(spread.reshape(pairs * tiles, per_tile, wide), axis=1)
    for hs in range(BATCHES * strings):
        sum_ref[hs] = summed[:, hs * LANES : (hs + 1) * LANES]
    for q in range(tiles):
        for h in range(BATCHES):
            for s in range(strings):
                place_ref[q, pl.ds(h * pairs * strings + s, pairs, stride=strings), :] = sum_ref[
                    h * strings + s, pl.ds(q, pairs, stride=tiles), :
                ]
        out_ref[:, q * LANES : (q + 1) * LANES] = place_ref[q]


def on_device(
    coeffs,
    integrals,
    send_block,
    alpha_slot,
    alpha_pair,
    alpha_parity,
    beta_pair,
    beta_target,
    beta_parity,
):
    local_rows, local_columns = coeffs.shape
    local_blocks = alpha_slot.shape[0]
    strings = local_rows // local_blocks
    pairs = local_blocks // BATCHES
    beta_local = beta_pair.shape[0]
    width = local_columns // beta_local
    cores = lax.axis_size("beta")
    senders = lax.axis_size("alpha")
    beta_blocks = cores * beta_local
    orbitals = integrals.shape[0]
    slots = send_block.shape[1]
    wide = strings * local_columns

    outer = 1 << (senders.bit_length() - 1) // 2
    inner = senders // outer
    per = slots // senders

    extra = -(-slots // local_columns // 16) * 16
    others = (
        alpha_slot,
        alpha_pair,
        alpha_parity,
        beta_pair,
        beta_target,
        beta_parity,
        integrals,
    )
    def exchange(x, k):
        return lax.ppermute(x, "alpha", [(d, d ^ k) for d in range(senders)]) if k else x

    def pinned(*arrays):
        return [pltpu.with_memory_space_constraint(x, pltpu.HBM) for x in arrays]

    packed = pl.pallas_call(
        pack_kernel,
        in_specs=[pl.BlockSpec(memory_space=pltpu.HBM)] * 2,
        out_shape=jax.ShapeDtypeStruct((local_rows + extra, local_columns), BF),
        scratch_shapes=[
            pltpu.VMEM(send_block.shape, jnp.int32),
            pltpu.SemaphoreType.DMA((2,)),
        ],
        compiler_params=pltpu.CompilerParams(vmem_limit_bytes=40 * 2**20),
        name="pack",
    )(*pinned(coeffs, send_block))
    gathered = [exchange(packed, k * inner) for k in range(outer)]
    both = BATCHES * strings * width
    *tables, expand, spread = pl.pallas_call(
        lambda *refs: fetch_kernel(width, *refs),
        in_specs=[pl.BlockSpec(memory_space=pltpu.HBM)] * len(others)
        + [pl.BlockSpec(memory_space=pl.ANY)],
        out_shape=[jax.ShapeDtypeStruct(x.shape, x.dtype) for x in others]
        + [
            jax.ShapeDtypeStruct((2 * both, BATCHES * strings * LANES), BF),
            jax.ShapeDtypeStruct((local_columns, wide), BF),
        ],
        scratch_shapes=[pltpu.SemaphoreType.DMA((len(others),))],
        compiler_params=pltpu.CompilerParams(vmem_limit_bytes=40 * 2**20),
        name="fetch",
    )(*pinned(*others), packed)
    outgoing = pl.pallas_call(
        lambda *refs: forward_kernel(strings, width, local_rows, slots, outer, *refs),
        out_shape=[jax.ShapeDtypeStruct((outer * per, wide), BF)] * inner,
        compiler_params=pltpu.CompilerParams(vmem_limit_bytes=40 * 2**20),
        name="forward",
    )(*gathered, spread)
    bits = inner.bit_length() - 1

    def across(x, j):
        if not j:
            return x
        partners = [int(format(j, "0%db" % bits)[::-1], 2) if c == 1 else j for c in range(cores)]
        route = [
            (d * cores + c, (d ^ partners[c]) * cores + c) for d in range(senders) for c in range(cores)
        ]
        return lax.ppermute(x, ("alpha", "beta"), route)

    received = [across(x, j) for j, x in enumerate(outgoing)]
    turn = sorted(range(inner), key=lambda j: -format(j or outer * inner * 2 - 1, "b").count("1"))
    turn = turn[:1] + turn[-2:-1] + turn[1:-2] + turn[-1:]
    flops = 2 * beta_local * beta_blocks * orbitals * (orbitals + 2 * pairs * slots)
    table = pl.pallas_call(
        lambda *refs: tables_kernel(beta_blocks, outer, inner, *refs),
        in_specs=[pl.BlockSpec(memory_space=pltpu.VMEM)] * len(tables)
        + [pl.BlockSpec(memory_space=pl.ANY)],
        out_shape=jax.ShapeDtypeStruct((pairs * beta_blocks, 2 * beta_local * slots), BF),
        scratch_shapes=[
            pltpu.VMEM((beta_local * beta_blocks, orbitals), BF),
            pltpu.VMEM((2, beta_local * beta_blocks, orbitals), BF),
            pltpu.VMEM((pairs * slots, orbitals), BF),
        ],
        compiler_params=pltpu.CompilerParams(vmem_limit_bytes=40 * 2**20),
        cost_estimate=pl.CostEstimate(flops=flops, bytes_accessed=8 * 2**20, transcendentals=0),
        name="tables",
    )(*tables, outgoing[0])
    part = jax.ShapeDtypeStruct((local_rows, local_columns), F32)
    tiles = local_columns // LANES
    call = dict(
        scratch_shapes=[
            pltpu.VMEM((BATCHES * strings, pairs * tiles, LANES), F32),
            pltpu.VMEM((tiles, local_rows, LANES), F32),
        ],
        compiler_params=pltpu.CompilerParams(vmem_limit_bytes=40 * 2**20),
        cost_estimate=pl.CostEstimate(
            flops=4 * pairs * slots * beta_local * beta_local * both,
            bytes_accessed=3 * 2**20,
            transcendentals=0,
        ),
    )
    right, theirs = pl.pallas_call(
        lambda *refs: right_kernel(strings, width, inner, turn, *refs),
        out_shape=[jax.ShapeDtypeStruct((2 * beta_local * slots, both), BF), part],
        name="theirs",
        **call,
    )(*(received[j] for j in turn), table, expand)

    def route(step):
        return [(core, (core + step) % cores) for core in range(cores)]

    arrived = [lax.ppermute(theirs, "beta", route(1))]
    for step in range(2, cores):
        other = pl.pallas_call(
            lambda *refs, step=step: sigma_kernel(strings, width, step, *refs),
            out_shape=part,
            name="theirs%d" % step,
            **call,
        )(right, table, expand)
        arrived.append(lax.ppermute(other, "beta", route(step)))
    result = pl.pallas_call(
        lambda *refs: sigma_kernel(strings, width, 0, *refs), out_shape=part, name="mine", **call
    )(right, table, expand)
    for value in arrived:
        result = result + value
    return result


def solution(mesh):
    in_specs = (
        P("alpha", "beta"),
        P(),
        P("alpha", None),
        P("alpha", None),
        P("alpha", None),
        P("alpha", None),
        P("beta", None),
        P("beta", None),
        P("beta", None),
    )
    out_specs = P("alpha", "beta")
    return jax.shard_map(
        on_device, mesh=mesh, in_specs=in_specs, out_specs=out_specs, check_vma=False
    )
```

```python
import jax
import jax.numpy as jnp
from jax import lax
from jax.experimental import pallas as pl
from jax.experimental.pallas import tpu as pltpu
from jax.sharding import PartitionSpec as P

BATCHES = 2
CAP = 4
BF = jnp.bfloat16
F32 = jnp.float32
LANES = 128
WIDE = 256


def row_of(length):
    return lax.broadcasted_iota(jnp.int32, (1, length), 1)


def column_of(length):
    return lax.broadcasted_iota(jnp.int32, (length, 1), 0)


def over(x, n):
    if n & (n - 1) == 0:
        return lax.shift_right_logical(x, jnp.int32(n.bit_length() - 1))
    return lax.div(x, jnp.int32(n))


def modulo(x, n):
    if n & (n - 1) == 0:
        return x & (n - 1)
    return lax.rem(x, jnp.int32(n))


def turned(x, inner):
    bits = inner.bit_length() - 1
    back = sum(((x >> i) & 1) << (bits - 1 - i) for i in range(bits))
    return jnp.where(lax.axis_index("beta") == 1, back, x)


def one(condition):
    return jnp.where(condition, 1.0, 0.0).astype(BF)


def dot(a, b):
    return jnp.dot(a, b, preferred_element_type=F32)


def dot_nt(a, b):
    return lax.dot_general(a, b, (((1,), (1,)), ((), ())), preferred_element_type=F32)


def split(x):
    high = x.astype(BF)
    return high, (x - high.astype(F32)).astype(BF)


def pack_kernel(coeffs_ref, send_ref, out_ref, list_ref, sems):
    rows, slots = coeffs_ref.shape[0], send_ref.shape[1]
    total, columns = out_ref.shape
    moves = [
        pltpu.make_async_copy(send_ref, list_ref, sems.at[0]),
        pltpu.make_async_copy(coeffs_ref, out_ref.at[pl.ds(0, rows)], sems.at[1]),
    ]
    for move in moves:
        move.start()
    moves[0].wait()
    values = list_ref[...].astype(F32)
    value = jnp.zeros((total - rows, columns), F32)
    for i, first in enumerate(range(0, slots, columns)):
        row = values[:, first : first + columns]
        if row.shape[1] < columns:
            row = jnp.concatenate([row, jnp.zeros((1, columns - row.shape[1]), F32)], axis=1)
        value = value + jnp.where(column_of(total - rows) == i, row, 0.0)
    out_ref[rows:total, :] = value.astype(BF)
    moves[1].wait()


def fetch_kernel(width, *refs):
    count = (len(refs) - 4) // 2
    expand_ref, spread_ref, sems = refs[-3:]
    moves = [
        pltpu.make_async_copy(refs[i], refs[count + 1 + i], sems.at[i]) for i in range(count)
    ]
    for move in moves:
        move.start()
    rows, columns = expand_ref.shape
    n = row_of(columns)
    expand_ref[...] = one(
        modulo(column_of(rows), rows // 2) == over(n, LANES) * width + modulo(n, width)
    )
    rows, columns = spread_ref.shape
    n = row_of(columns)
    group = columns // rows * width
    spread_ref[...] = one(column_of(rows) == over(n, group) * width + modulo(n, width))
    for move in moves:
        move.wait()


def forward_kernel(strings, width, rows, slots, outer, *refs):
    gathered_refs, spread_ref, out_refs = refs[:outer], refs[outer], refs[outer + 1 :]
    inner = len(out_refs)
    columns = gathered_refs[0].shape[1]
    wide = strings * columns
    group = strings * width
    per = BATCHES * CAP
    blocks = rows // strings
    n = row_of(wide)
    gathered = jnp.concatenate([ref[:rows, :] for ref in gathered_refs], axis=0)
    keep = modulo(column_of(outer * rows), strings) == modulo(over(n, width), strings)
    spaced = jnp.where(keep, dot(gathered, spread_ref[...]), 0.0).astype(BF)
    r = column_of(inner * per)
    receiver = turned(over(r, per), inner) ^ lax.axis_index("alpha")
    wanted = over(modulo(r, per), CAP) * (slots // BATCHES) + receiver * CAP + modulo(r, CAP)
    wanted = wanted == row_of(slots)
    picks = []
    for k in range(outer):
        tail = gathered_refs[k][rows:, :].astype(F32)
        listed = [tail[i : i + 1] for i in range((slots + columns - 1) // columns)]
        listed = (listed[0] if len(listed) == 1 else jnp.concatenate(listed, axis=1))[:, :slots]
        chosen = jnp.sum(jnp.where(wanted, listed, 0.0), axis=1, keepdims=True).astype(jnp.int32)
        chosen = jnp.where(chosen < blocks, chosen + k * blocks, -1)
        picks.append(jnp.where(over(row_of(outer * rows), strings) == chosen, 1.0, 0.0))
    for j in range(inner):
        pick = jnp.concatenate([part[j * per : (j + 1) * per] for part in picks], axis=0)
        out_refs[j][...] = dot(pick.astype(BF), spaced).astype(BF)


def tables_kernel(
    beta_blocks,
    outer,
    inner,
    slot_ref,
    pair_ref,
    parity_ref,
    bpair_ref,
    btarget_ref,
    bparity_ref,
    integrals_ref,
    _,
    out_ref,
    t_ref,
    w_ref,
    hot_ref,
):
    orbitals = integrals_ref.shape[0]
    blocks, excitations = slot_ref.shape
    beta_local, beta_excitations = bpair_ref.shape
    pairs = blocks // BATCHES
    slots = hot_ref.shape[0] // pairs
    bpair = bpair_ref[...].astype(F32).T.astype(jnp.int32)
    bfactor = (1 - 2 * bparity_ref[...]).astype(F32)
    btarget = btarget_ref[...] - lax.axis_index("beta") * beta_local
    btarget = jnp.where(btarget < 0, btarget + beta_blocks, btarget)
    for v in range(beta_local):
        left = jnp.where(column_of(beta_blocks) == btarget[v : v + 1], bfactor[v : v + 1], 0.0)
        right = one(row_of(orbitals) == bpair[:, v : v + 1])
        t_ref[v * beta_blocks : (v + 1) * beta_blocks, :] = dot(left.astype(BF), right).astype(BF)
    high, low = split(dot(t_ref[...], integrals_ref[...]))
    w_ref[0] = high
    w_ref[1] = low
    pair = pair_ref[...].astype(F32).T.astype(jnp.int32)
    factor = (1 - 2 * parity_ref[...]).astype(F32)
    slot = slot_ref[...]
    partner = over(slot, CAP) ^ lax.axis_index("alpha")
    place = turned(modulo(partner, inner), inner) * outer + over(partner, inner)
    place = place * (BATCHES * CAP) + modulo(slot, CAP)
    for t in range(pairs):
        total = None
        for h in range(BATCHES):
            g = h * pairs + t
            row = place[g : g + 1] + h * CAP
            left = jnp.where(column_of(slots) == row, factor[g : g + 1], 0.0).astype(BF)
            part = dot(left, one(row_of(orbitals) == pair[:, g : g + 1]))
            total = part if total is None else total + part
        hot_ref[t * slots : (t + 1) * slots, :] = total.astype(BF)
    step = max(1, WIDE // slots)
    for start in range(0, pairs, step):
        hot = hot_ref[start * slots : (start + step) * slots, :]
        high, low = split(dot_nt(w_ref[0], hot) + dot_nt(w_ref[1], hot))
        for i in range(step):
            lanes = slice(i * slots, (i + 1) * slots)
            for v in range(beta_local):
                first = v * 2 * slots
                for part in range(beta_blocks // beta_local):
                    row = (part * pairs + start + i) * beta_local
                    rows = slice(row, row + beta_local)
                    row = v * beta_blocks + part * beta_local
                    source = slice(row, row + beta_local)
                    out_ref[rows, first : first + slots] = high[source, lanes]
                    out_ref[rows, first + slots : first + 2 * slots] = low[source, lanes]


def right_kernel(strings, width, inner, turn, *refs):
    received_refs, (table_ref, expand_ref, right_ref), rest = refs[:inner], refs[inner : inner + 3], refs[inner + 3 :]
    received = jnp.concatenate([received_refs[turn.index(j)][...] for j in range(inner)], axis=0)
    slots, wide = received.shape
    group = strings * width
    both = BATCHES * group
    batch = modulo(over(column_of(slots), CAP), BATCHES)
    low = one((batch == 0) & (row_of(both) < group))
    high = one((batch == 1) & (row_of(both) >= group))
    for tile in range(wide // both):
        x = received[:, tile * both : (tile + 1) * both]
        swapped = jnp.concatenate([x[:, group:], x[:, :group]], axis=1)
        for v, (a, b) in ((2 * tile, (x, swapped)), (2 * tile + 1, (swapped, x))):
            value = a * low + b * high
            right_ref[2 * v * slots : (2 * v + 1) * slots, :] = value
            right_ref[(2 * v + 1) * slots : (2 * v + 2) * slots, :] = value
    sigma_kernel(strings, width, 1, right_ref, table_ref, expand_ref, *rest)


def sigma_kernel(strings, width, part, right_ref, table_ref, expand_ref, out_ref, sum_ref, place_ref):
    local_rows, columns = out_ref.shape
    pairs = local_rows // strings // BATCHES
    blocks = columns // width
    rows = pairs * blocks
    product = dot(table_ref[part * rows : (part + 1) * rows, :], right_ref[...])
    both_parts = jnp.concatenate(split(product), axis=1)
    per_tile = LANES // width
    spread = dot(both_parts, expand_ref[...])
    wide = spread.shape[1]
    keep = modulo(column_of(rows), per_tile) == modulo(over(row_of(wide), width), per_tile)
    spread = jnp.where(keep, spread, 0.0)
    tiles = blocks // per_tile
    summed = jnp.sum(spread.reshape(pairs * tiles, per_tile, wide), axis=1)
    for hs in range(BATCHES * strings):
        sum_ref[hs] = summed[:, hs * LANES : (hs + 1) * LANES]
    for q in range(tiles):
        for h in range(BATCHES):
            for s in range(strings):
                place_ref[q, pl.ds(h * pairs * strings + s, pairs, stride=strings), :] = sum_ref[
                    h * strings + s, pl.ds(q, pairs, stride=tiles), :
                ]
        out_ref[:, q * LANES : (q + 1) * LANES] = place_ref[q]


def on_device(
    coeffs,
    integrals,
    send_block,
    alpha_slot,
    alpha_pair,
    alpha_parity,
    beta_pair,
    beta_target,
    beta_parity,
):
    local_rows, local_columns = coeffs.shape
    local_blocks = alpha_slot.shape[0]
    strings = local_rows // local_blocks
    pairs = local_blocks // BATCHES
    beta_local = beta_pair.shape[0]
    width = local_columns // beta_local
    cores = lax.axis_size("beta")
    senders = lax.axis_size("alpha")
    beta_blocks = cores * beta_local
    orbitals = integrals.shape[0]
    slots = send_block.shape[1]
    wide = strings * local_columns

    outer = 1 << (senders.bit_length() - 1) // 2
    inner = senders // outer
    per = slots // senders

    extra = -(-slots // local_columns // 16) * 16
    others = (
        alpha_slot,
        alpha_pair,
        alpha_parity,
        beta_pair,
        beta_target,
        beta_parity,
        integrals,
    )
    def exchange(x, k):
        return lax.ppermute(x, "alpha", [(d, d ^ k) for d in range(senders)]) if k else x

    def pinned(*arrays):
        return [pltpu.with_memory_space_constraint(x, pltpu.HBM) for x in arrays]

    packed = pl.pallas_call(
        pack_kernel,
        in_specs=[pl.BlockSpec(memory_space=pltpu.HBM)] * 2,
        out_shape=jax.ShapeDtypeStruct((local_rows + extra, local_columns), BF),
        scratch_shapes=[
            pltpu.VMEM(send_block.shape, jnp.int32),
            pltpu.SemaphoreType.DMA((2,)),
        ],
        compiler_params=pltpu.CompilerParams(vmem_limit_bytes=40 * 2**20),
        name="pack",
    )(*pinned(coeffs, send_block))
    gathered = [exchange(packed, k * inner) for k in range(outer)]
    both = BATCHES * strings * width
    *tables, expand, spread = pl.pallas_call(
        lambda *refs: fetch_kernel(width, *refs),
        in_specs=[pl.BlockSpec(memory_space=pltpu.HBM)] * len(others)
        + [pl.BlockSpec(memory_space=pl.ANY)],
        out_shape=[jax.ShapeDtypeStruct(x.shape, x.dtype) for x in others]
        + [
            jax.ShapeDtypeStruct((2 * both, BATCHES * strings * LANES), BF),
            jax.ShapeDtypeStruct((local_columns, wide), BF),
        ],
        scratch_shapes=[pltpu.SemaphoreType.DMA((len(others),))],
        compiler_params=pltpu.CompilerParams(vmem_limit_bytes=40 * 2**20),
        name="fetch",
    )(*pinned(*others), packed)
    outgoing = pl.pallas_call(
        lambda *refs: forward_kernel(strings, width, local_rows, slots, outer, *refs),
        out_shape=[jax.ShapeDtypeStruct((outer * per, wide), BF)] * inner,
        compiler_params=pltpu.CompilerParams(vmem_limit_bytes=40 * 2**20),
        name="forward",
    )(*gathered, spread)
    bits = inner.bit_length() - 1

    def across(x, j):
        if not j:
            return x
        partners = [int(format(j, "0%db" % bits)[::-1], 2) if c == 1 else j for c in range(cores)]
        route = [
            (d * cores + c, (d ^ partners[c]) * cores + c) for d in range(senders) for c in range(cores)
        ]
        return lax.ppermute(x, ("alpha", "beta"), route)

    received = [across(x, j) for j, x in enumerate(outgoing)]
    turn = sorted(range(inner), key=lambda j: -format(j or outer * inner * 2 - 1, "b").count("1"))
    flops = 2 * beta_local * beta_blocks * orbitals * (orbitals + 2 * pairs * slots)
    table = pl.pallas_call(
        lambda *refs: tables_kernel(beta_blocks, outer, inner, *refs),
        in_specs=[pl.BlockSpec(memory_space=pltpu.VMEM)] * len(tables)
        + [pl.BlockSpec(memory_space=pl.ANY)],
        out_shape=jax.ShapeDtypeStruct((pairs * beta_blocks, 2 * beta_local * slots), BF),
        scratch_shapes=[
            pltpu.VMEM((beta_local * beta_blocks, orbitals), BF),
            pltpu.VMEM((2, beta_local * beta_blocks, orbitals), BF),
            pltpu.VMEM((pairs * slots, orbitals), BF),
        ],
        compiler_params=pltpu.CompilerParams(vmem_limit_bytes=40 * 2**20),
        cost_estimate=pl.CostEstimate(flops=flops, bytes_accessed=8 * 2**20, transcendentals=0),
        name="tables",
    )(*tables, outgoing[0])
    part = jax.ShapeDtypeStruct((local_rows, local_columns), F32)
    tiles = local_columns // LANES
    call = dict(
        scratch_shapes=[
            pltpu.VMEM((BATCHES * strings, pairs * tiles, LANES), F32),
            pltpu.VMEM((tiles, local_rows, LANES), F32),
        ],
        compiler_params=pltpu.CompilerParams(vmem_limit_bytes=40 * 2**20),
        cost_estimate=pl.CostEstimate(
            flops=4 * pairs * slots * beta_local * beta_local * both,
            bytes_accessed=3 * 2**20,
            transcendentals=0,
        ),
    )
    right, theirs = pl.pallas_call(
        lambda *refs: right_kernel(strings, width, inner, turn, *refs),
        out_shape=[jax.ShapeDtypeStruct((2 * beta_local * slots, both), BF), part],
        name="theirs",
        **call,
    )(*(received[j] for j in turn), table, expand)

    def route(step):
        return [(core, (core + step) % cores) for core in range(cores)]

    arrived = [lax.ppermute(theirs, "beta", route(1))]
    for step in range(2, cores):
        other = pl.pallas_call(
            lambda *refs, step=step: sigma_kernel(strings, width, step, *refs),
            out_shape=part,
            name="theirs%d" % step,
            **call,
        )(right, table, expand)
        arrived.append(lax.ppermute(other, "beta", route(step)))
    result = pl.pallas_call(
        lambda *refs: sigma_kernel(strings, width, 0, *refs), out_shape=part, name="mine", **call
    )(right, table, expand)
    for value in arrived:
        result = result + value
    return result


def solution(mesh):
    in_specs = (
        P("alpha", "beta"),
        P(),
        P("alpha", None),
        P("alpha", None),
        P("alpha", None),
        P("alpha", None),
        P("beta", None),
        P("beta", None),
        P("beta", None),
    )
    out_specs = P("alpha", "beta")
    return jax.shard_map(
        on_device, mesh=mesh, in_specs=in_specs, out_specs=out_specs, check_vma=False
    )
```
